32 devices in a mesh: survey: 2 (over y), inline: 4 (over z), xline: 2 (over x), depth: 2 (over core).
Axes of the slice: x: 2, y: 2, z: 4, core: 2. Of those that a mesh axis runs over, the one named last changes fastest.
Arguments:
- seismic: bfloat16 [128, 64, 512], P(('survey', 'inline'), 'xline', 'depth'), parts along dimension 0, may hold values from -64 to 64
- trace_live: int32 [128, 64], P(('survey', 'inline'), 'xline'), parts along dimension 0, may hold values from 0 to 1
- filter_taps: bfloat16 [3, 96, 5], replicated, may hold values from -2.6875 to 2.6875
Outputs:
- whitened: bfloat16 [96, 64, 32, 256], P(None, ('survey', 'inline'), 'xline', 'depth'), parts along dimension 1
- factor: float32 [192, 96], P('survey'), parts along dimension 0
The draws below stay inside these ranges and needn't reach their ends.
There are 2 independent parts, one for each index of `survey`. The reference program is written for one: setup_inputs(seed, part) draws one part's arguments, and reference() takes and returns one part's arrays. A program takes and returns all parts, laid end to end along the dimension named above; an argument that names none is the same for every part. Nothing has to cross between parts.
All inputs are finite; a program needn't handle non-finite values.
Results may differ from the reference program's by a relative error of at most 0.0039.
The reference program's roundings to bfloat16 on the way (of `live`, `first`, `second`, `attributes` and `inverse`) count: a program that leaves them out, or rounds other values in their place, can miss the bound.
Values may be sent and summed in bfloat16 or wider, within the bound.
No kernel may reach another device: no remote copies, remote signals or barrier semaphores. Data moves between devices by JAX's collectives and lax.ppermute only.
A program may use at most 64 MiB of HBM per device.

```python
import jax
import jax.numpy as jnp
from jax import lax

ORIENT = 32
LEVELS = 3
TAPS = 5
CHAN = 96
IL_DEV = 16
NIL = 64
NXL = 64
NT = 512


def draw_trace_live(key, part):
    key_start, key_end, key_sparse = jax.random.split(jax.random.fold_in(key, 7), 3)
    starts = jax.random.randint(key_start, (NXL,), 0, IL_DEV // 2 + 1)
    ends = NIL - jax.random.randint(key_end, (NXL,), 0, IL_DEV // 2 + 1)
    sparse = jax.random.randint(key_sparse, (NIL, NXL), 0, 16) != 0
    rows = jnp.arange(NIL, dtype=jnp.int32)[:, None]
    inside = (rows >= starts[None, :]) & (rows < ends[None, :]) & sparse
    return inside.astype(jnp.int32)


def amplitude_field(key, noise, rise_end):
    key_trace = jax.random.fold_in(key, 5)
    position = jnp.arange(NIL, dtype=jnp.float32) / jnp.float32(max(NIL - 1, 1))
    rise = jnp.exp(jnp.log(jnp.float32(rise_end)) * position)
    trace_gain = jnp.exp(jax.random.uniform(key_trace, (NIL, NXL), jnp.float32, 0.0, jnp.log(3.5)))
    return noise * rise[:, None, None] * trace_gain[:, :, None]


def draw_seismic(key, part):
    key = jax.random.fold_in(key, 11)
    key_noise = jax.random.fold_in(key, 3)
    noise = jnp.clip(jax.random.normal(key_noise, (NIL, NXL, NT), jnp.float32), -6.0, 6.0)
    field = amplitude_field(key, noise, 3.0)
    return field.astype(jnp.bfloat16)


def normal_values(stream_key, shape, spread, most, kind=jnp.bfloat16):
    result = spread * jax.random.normal(stream_key, shape, jnp.float32)
    return jnp.clip(result, min=-most, max=most).astype(kind)


def setup_inputs(seed: int = 0, part: int = 0) -> dict:
    key_of = jax.random.split(jax.random.key(seed), 4)
    part_splits = jax.random.split(jax.random.fold_in(key_of[3], part), 4)
    seismic = draw_seismic(jax.random.fold_in(jax.random.fold_in(key_of[3], part), 71), part)
    trace_live = draw_trace_live(jax.random.fold_in(jax.random.fold_in(key_of[3], part), 71), part)
    filter_taps = normal_values(key_of[2], (3, CHAN, TAPS), 0.45, 2.6875)
    return {"seismic": seismic, "trace_live": trace_live, "filter_taps": filter_taps}


def filter_axis(arr, axis, tap_row, dilation):
    reach = TAPS // 2 * 2 ** (LEVELS - 1)
    count = (arr.shape[axis] - 2 * reach) // 2
    total = jnp.zeros((), jnp.float32)
    for k in range(TAPS):
        start = reach + dilation * (k - TAPS // 2)
        piece = lax.slice_in_dim(arr, start, start + 2 * (count - 1) + 1, 2, axis)
        total = total + piece.astype(jnp.float32) * tap_row[k].astype(jnp.float32)
    return total

def reference(seismic, trace_live, filter_taps):
    reach = TAPS // 2 * 2 ** (LEVELS - 1)
    weights = trace_live.astype(jnp.bfloat16)
    live = seismic * weights[:, :, None]
    padded = jnp.pad(live, reach)
    row_mask = trace_live[0::2, 0::2].astype(jnp.float32)
    groups = []
    for level in range(LEVELS):
        dilation = 2 ** level

        def channel(taps_three):
            first = filter_axis(padded, 0, taps_three[0], dilation).astype(jnp.bfloat16)
            second = filter_axis(first, 1, taps_three[1], dilation).astype(jnp.bfloat16)
            third = filter_axis(second, 2, taps_three[2], dilation)
            return (third * row_mask[:, :, None]).astype(jnp.bfloat16)
        level_taps = jnp.transpose(filter_taps[:, level * ORIENT:(level + 1) * ORIENT, :], (1, 0, 2))
        groups.append(lax.map(channel, level_taps))
    attributes = jnp.concatenate(groups, axis=0)
    flat = attributes.reshape(CHAN, -1)
    gram = jnp.dot(flat.astype(jnp.float32), flat.T.astype(jnp.float32), preferred_element_type=jnp.float32)
    count = jnp.sum(row_mask) * jnp.float32(NT // 2)
    lower = jnp.linalg.cholesky(gram / count)
    inverse = jax.scipy.linalg.solve_triangular(lower, jnp.eye(CHAN, dtype=jnp.float32), lower=True)
    inverse_low = inverse.astype(jnp.bfloat16)
    blocks = attributes.reshape(CHAN, NIL // 2, -1)

    def whiten_row(index):
        piece = lax.dynamic_index_in_dim(blocks, index, 1, keepdims=False)
        return jnp.dot(inverse_low.astype(jnp.float32), piece.astype(jnp.float32), preferred_element_type=jnp.float32).astype(jnp.bfloat16)
    rows = lax.map(whiten_row, jnp.arange(NIL // 2, dtype=jnp.int32))
    whitened = jnp.transpose(rows, (1, 0, 2)).reshape(CHAN, NIL // 2, NXL // 2, NT // 2)
    return (whitened, lower.T)
```

```python
import functools

import jax
import jax.numpy as jnp
from jax import lax
from jax.experimental import pallas as pl
from jax.experimental.pallas import tpu as pltpu
from jax.sharding import PartitionSpec as P

ORIENT = 32
TAPS = 5
CHAN = 96
REACH = 8
KEPT = 5
F32 = jnp.float32
BF16 = jnp.bfloat16
VMEM_LIMIT = 56 * 1024 * 1024


def iota(shape, dim):
    return lax.broadcasted_iota(jnp.int32, shape, dim)


def rounded(value):
    return value.astype(BF16).astype(F32)


def ones_where(mask):
    return jnp.where(mask, 1.0, 0.0).astype(BF16)


def dot(a, b):
    return jnp.dot(a, b, preferred_element_type=F32)


def shifted(value, axis, step):
    size = lax.axis_size(axis)
    return lax.ppermute(value, axis, [(i, i + step) for i in range(size) if 0 <= i + step < size])


def swapped(value, axis, bit):
    size = lax.axis_size(axis)
    return lax.ppermute(value, axis, [(i, i ^ bit) for i in range(size)])


def summed(value, axes):
    other = None
    for axis in axes:
        size = lax.axis_size(axis)
        assert size & (size - 1) == 0
        bit = 1
        while bit < size:
            if other is not None:
                value = value + other
            other = swapped(value, axis, bit)
            bit *= 2
    return value, other


def halo_select(level, odd, stored, x_left, depth_first):
    dilation = 2 ** level
    rows, cols = 256, TAPS * 128
    lane = iota((1, cols), 1)
    k = lane // 128
    within = lane % 128
    place = (within + 4) % 8 - 4
    q = ((within + 4) // 8) % 16
    j = 2 * q + dilation * (k - 2)
    slot = jnp.where(j < 0, 40 + j, j)
    if stored == 48:
        slot = jnp.where(j >= 32, j + 8, slot)
    else:
        slot = jnp.where((j < 0) & (x_left == 0), -999999, slot)
        slot = jnp.where((j >= 32) & (x_left == 1), -999999, slot)
    if odd:
        source = 4 * stored + slot
        source = jnp.where((place == -1) & (depth_first == 0), source, -1)
    else:
        source = jnp.where(place >= 0, place, place + 4) * stored + slot
        source = jnp.where((place >= 0) & (depth_first == 0), -1, source)
        source = jnp.where((place < 0) & (depth_first == 1), -1, source)
    return ones_where(iota((rows, cols), 0) == source)


def attributes_kernel(
    two_sided, place_ref, live_smem, live_ref, taps_ref, own_ref, before_ref, after_ref, xh_ref, dh_ref,
    attr_ref, gram_ref, bands, first0, first12, halo2, w2, w3, planes,
):
    x_left = place_ref[0]
    depth_first = place_ref[1]
    stored = 48 if two_sided else 40

    for k in range(TAPS):
        w2[k] = jnp.broadcast_to(taps_ref[1, :, k : k + 1], (CHAN, 128))
        w3[k] = jnp.broadcast_to(taps_ref[2, :, k : k + 1], (CHAN, 128))
    lane32 = iota((ORIENT, 128), 1)
    for level in range(3):
        cs = slice(level * ORIENT, (level + 1) * ORIENT)
        cols = [jnp.broadcast_to(taps_ref[0, cs, k : k + 1], (ORIENT, 128)) for k in range(TAPS)]
        for o in range(8):
            total = jnp.zeros((ORIENT, 128), F32)
            for k in range(TAPS):
                total = jnp.where(lane32 == REACH + 2 * o + 2 ** level * (k - 2), cols[k], total)
            bands[pl.ds(level * 256 + o * ORIENT, ORIENT), :] = total.astype(BF16)

    n = iota((256, 256), 1)
    pick = ones_where(iota((256, 256), 0) == jnp.where(n < 128, 2 * n, 2 * n - 255))
    r = iota((512, 512), 0)
    c = iota((512, 512), 1)
    turn = ones_where((c // 16 == r % 32) & (c % 16 == r // 32))
    own = dot(own_ref[...], pick).astype(BF16).reshape(16, 32, 256)
    before = dot(before_ref[...], pick).astype(BF16).reshape(8, 32, 256)
    after = dot(after_ref[...], pick).astype(BF16).reshape(8, 32, 256)
    for half in range(2):
        js = slice(half * 16, half * 16 + 16)
        block = jnp.concatenate([before[:, js], own[:, js], after[:, js]], axis=0).reshape(512, 256)
        planes[8 + half * 16 : 24 + half * 16] = dot(turn, block).astype(BF16).reshape(16, 32, 256)
    turn_x = ones_where((c % 256 // 8 == r % 32) & (c // 256 * 8 + c % 8 == r // 32))
    if two_sided:
        sides = dot(xh_ref[...], pick).astype(BF16)
    else:
        got = dot(xh_ref[...], pick)
        left = jnp.where(x_left == 1, 1.0, 0.0)
        sides = jnp.concatenate([got * left, got * (1.0 - left)], axis=0).astype(BF16)
    edges = dot(turn_x, sides).astype(BF16).reshape(16, 32, 256)
    planes[0:8] = edges[0:8]
    planes[40:48] = edges[8:16]

    a0 = bands[0:256, 0:32]
    a12 = bands[256:768, 0:32]

    def level0_first(j, _):
        first0[j] = rounded(dot(a0, planes[j + 6]))
        return 0

    lax.fori_loop(0, 35, level0_first, 0)

    def even_first(pair, _):
        both = jnp.concatenate([planes[4 * pair, :, 0:128], planes[4 * pair + 2, :, 0:128]], axis=1)
        out = rounded(dot(a12, both))
        first12[2 * pair] = out[:, 0:128]
        first12[2 * pair + 1] = out[:, 128:256]
        return 0

    lax.fori_loop(0, 12, even_first, 0)

    for index, (level, odd) in enumerate(((0, False), (0, True), (1, False), (2, False))):
        cols = dot(dh_ref[...], halo_select(level, odd, stored, x_left, depth_first)).astype(BF16)
        part = rounded(dot(bands[level * 256 : level * 256 + 256, 0:32], cols))
        cs = slice(level * ORIENT, (level + 1) * ORIENT)
        total = jnp.zeros((256, 128), F32)
        for k in range(TAPS):
            total = total + part[:, k * 128 : k * 128 + 128] * jnp.concatenate([w2[k, cs]] * 8, axis=0)
        halo2[index] = rounded(total)
    lane256 = iota((256, 128), 1)
    w3_0, w3_1, w3_4 = [jnp.concatenate([w3[k, 0:ORIENT]] * 8, axis=0) for k in (0, 1, 4)]
    halo2[0] = jnp.where(lane256 % 8 == 7, halo2[0] * w3_0 + halo2[1] * w3_1, halo2[0] * w3_4)

    lane = iota((16, 128), 1)

    def tap_rows(ref, level, c16):
        start = pl.multiple_of(level * ORIENT + c16 * 16, 16)
        return [ref[k, pl.ds(start, 16), :] for k in range(TAPS)], start

    def rolled(value, shift):
        return pltpu.roll(value, shift % 128, 1) if shift % 128 else value

    def level0_rest(step, _):
        o, c16 = step // 2, step % 2
        rows = pl.ds(pl.multiple_of(o * ORIENT + c16 * 16, 16), 16)
        s2, start = tap_rows(w2, 0, c16)
        s3, _ = tap_rows(w3, 0, c16)
        halo = halo2[0, rows, :]
        for q in range(16):
            even = sum(s2[k] * first0[2 * q + k, rows, 0:128] for k in range(TAPS))
            odd = sum(s2[k] * first0[2 * q + k, rows, 128:256] for k in range(TAPS))
            even, odd = rounded(even), rounded(odd)
            mine = rolled(halo, -8 * q)
            back = jnp.where(lane == 127, mine, s3[0] * even + s3[1] * odd)
            ahead = jnp.where(lane == 0, mine, s3[4] * even)
            total = s3[2] * even + s3[3] * odd + rolled(back, 1) + rolled(ahead, -1)
            total = total * live_smem[2 * o, 2 * q].astype(F32)
            attr_ref[o * 16 + q, pl.ds(start, 16), :] = total.astype(BF16)
        return 0

    lax.fori_loop(0, 16, level0_rest, 0)

    def even_rest(level):
        unit = 2 ** (level - 1)

        def body(step, _):
            o, c16 = step // 2, step % 2
            rows = pl.ds(pl.multiple_of((level - 1) * 256 + o * ORIENT + c16 * 16, 16), 16)
            halo_rows = pl.ds(pl.multiple_of(o * ORIENT + c16 * 16, 16), 16)
            s2, start = tap_rows(w2, level, c16)
            s3, _ = tap_rows(w3, level, c16)
            halo = halo2[level + 1, halo_rows, :]
            for q in range(16):
                value = rounded(sum(s2[k] * first12[q + 4 + unit * (k - 2), rows, :] for k in range(TAPS)))
                mine = rolled(halo, -8 * q)
                total = s3[2] * value
                for k in (0, 1, 3, 4):
                    shift = unit * (k - 2)
                    edge = lane < shift if shift > 0 else lane >= 128 + shift
                    total = total + s3[k] * rolled(jnp.where(edge, mine, value), -shift)
                total = total * live_smem[2 * o, 2 * q].astype(F32)
                attr_ref[o * 16 + q, pl.ds(start, 16), :] = total.astype(BF16)
            return 0

        return body

    lax.fori_loop(0, 16, even_rest(1), 0)
    lax.fori_loop(0, 16, even_rest(2), 0)

    def add_gram(o, total):
        for q in range(0, 16, 2):
            both = jnp.concatenate([attr_ref[o * 16 + q], attr_ref[o * 16 + q + 1]], axis=1)
            total = total + lax.dot_general(
                both, both, (((1,), (1,)), ((), ())), preferred_element_type=F32
            )
        return total

    gram = lax.fori_loop(0, 8, add_gram, jnp.zeros((CHAN, CHAN), F32))
    alive = live_ref[...]
    chosen = (iota(alive.shape, 0) % 2 == 0) & (iota(alive.shape, 1) % 2 == 0)
    count = jnp.sum(jnp.where(chosen, alive.astype(F32), 0.0)) * 128.0
    gram_ref[...] = jnp.full((CHAN, 128), count, F32)
    gram_ref[:, 0:CHAN] = gram


def whiten_kernel(mine_ref, other_ref, attr_ref, out_ref, factor_ref, inverse, kron):
    step = pl.program_id(0)

    @pl.when(step == 0)
    def _():
        total = mine_ref[...] + other_ref[...]
        lane = iota((8, 128), 1)
        sub = iota((8, 128), 0)
        count = jnp.broadcast_to(total[0:1, CHAN : CHAN + 1], (8, 128))
        blocks = []
        for g in range(CHAN // 8):
            blocks.append(jnp.where(lane < CHAN, total[8 * g : 8 * g + 8] / count, 0.0))
        row_lane = iota((1, 128), 1)
        for j in range(CHAN):
            g, s = j // 8, j % 8
            row = blocks[g][s : s + 1, :]
            pivot = row[:, j : j + 1]
            scale = lax.rsqrt(pivot)
            recip = 1.0 / pivot
            factor_ref[j : j + 1, :] = (jnp.where(row_lane >= j, row, 0.0) * scale)[:, 0:CHAN]
            unit = jnp.where(row_lane == j, 1.0, row)
            inverse[j : j + 1, :] = jnp.where(row_lane <= j, unit, 0.0) * scale
            if j == CHAN - 1:
                break
            scaled_row = unit * recip
            for h in range(g, CHAN // 8):
                col = blocks[h][:, j : j + 1]
                if h == g:
                    col = jnp.where(sub[:, 0:1] > s, col, 0.0)
                blocks[h] = jnp.where(lane == j, 0.0, blocks[h]) - col * scaled_row
        low = inverse[:, 0:CHAN].astype(BF16)
        spread = ones_where(iota((CHAN, 768), 0) == iota((CHAN, 768), 1) % CHAN)
        wide = dot(low, spread).astype(BF16)
        tall = ones_where(iota((768, CHAN), 0) // 8 == iota((768, CHAN), 1))
        full = dot(tall, wide)
        keep = iota((768, 768), 0) % 8 == iota((768, 768), 1) // CHAN
        kron[...] = jnp.where(keep, full, 0.0).astype(BF16)

    weights = kron[...]
    halves = []
    for half in range(2):
        pair = [
            attr_ref[pl.ds((2 * step + i) * 16 + 8 * half, 8)].reshape(768, 128) for i in range(2)
        ]
        halves.append(dot(weights, jnp.concatenate(pair, axis=1)))
    for i in range(2):
        both = [half[:, i * 128 : i * 128 + 128].reshape(CHAN, 8, 128) for half in halves]
        out_ref[:, i] = jnp.concatenate(both, axis=1).astype(BF16)


def local(seismic, trace_live, filter_taps):
    il_len, xl_len, t_len = seismic.shape
    assert (il_len, xl_len, t_len) == (16, 32, 256) and lax.axis_size("depth") == 2
    live = seismic * trace_live.astype(BF16)[:, :, None]
    taps = filter_taps.astype(F32)
    x_index = lax.axis_index("xline")
    d_index = lax.axis_index("depth")
    two_sided = lax.axis_size("xline") > 2

    before = shifted(live[il_len - REACH :], "inline", 1)
    after = shifted(live[:REACH], "inline", -1)

    def stack(js):
        return jnp.concatenate([before[:, js], live[:, js], after[:, js]], axis=0)

    low, high = slice(0, REACH), slice(xl_len - REACH, xl_len)
    if two_sided:
        xh = [shifted(stack(high), "xline", 1), shifted(stack(low), "xline", -1)]
    else:
        xh = [swapped(jnp.where(x_index == 0, stack(high), stack(low)), "xline", 1)]
    whole = jnp.concatenate([jnp.concatenate([before, live, after], axis=0)] + xh, axis=1)
    last = jnp.concatenate(
        [whole[:, :, t] for t in (t_len - 8, t_len - 6, t_len - 4, t_len - 2, t_len - 1)], axis=1
    )
    initial = jnp.concatenate([whole[:, :, t] for t in (0, 2, 4, 6, 7)], axis=1)
    dh = jnp.where(d_index == 0, last, initial)
    dh = jnp.pad(dh, ((0, 0), (0, 256 - dh.shape[1])))
    dh = swapped(dh, "depth", 1)

    place = jnp.stack([(x_index == 1).astype(jnp.int32), (d_index == 0).astype(jnp.int32)])
    vmem = pl.BlockSpec(memory_space=pltpu.VMEM)
    smem = pl.BlockSpec(memory_space=pltpu.SMEM)
    xrows = jnp.concatenate([x.reshape(256, t_len) for x in xh], axis=0)
    attr, gram = pl.pallas_call(
        functools.partial(attributes_kernel, two_sided),
        out_shape=(
            jax.ShapeDtypeStruct((128, CHAN, 128), BF16),
            jax.ShapeDtypeStruct((CHAN, 128), F32),
        ),
        in_specs=[smem, smem] + [vmem] * 7,
        out_specs=(vmem, vmem),
        scratch_shapes=[
            pltpu.VMEM((768, 128), BF16),
            pltpu.VMEM((35, 256, 256), F32),
            pltpu.VMEM((24, 512, 128), F32),
            pltpu.VMEM((4, 256, 128), F32),
            pltpu.VMEM((TAPS, CHAN, 128), F32),
            pltpu.VMEM((TAPS, CHAN, 128), F32),
            pltpu.VMEM((48, 32, 256), BF16),
        ],
        compiler_params=pltpu.CompilerParams(vmem_limit_bytes=VMEM_LIMIT),
        name="attributes",
    )(
        place, trace_live, trace_live, taps, live.reshape(512, t_len),
        before.reshape(256, t_len), after.reshape(256, t_len), xrows, dh,
    )

    mine, other = summed(gram, ("depth", "xline", "inline"))
    out, factor = pl.pallas_call(
        whiten_kernel,
        grid=(4,),
        out_shape=(
            jax.ShapeDtypeStruct((CHAN, 8, 16, 128), BF16),
            jax.ShapeDtypeStruct((CHAN, CHAN), F32),
        ),
        in_specs=[vmem] * 3,
        out_specs=(
            pl.BlockSpec((CHAN, 2, 16, 128), lambda i: (0, i, 0, 0)),
            pl.BlockSpec((CHAN, CHAN), lambda i: (0, 0)),
        ),
        scratch_shapes=[pltpu.VMEM((CHAN, 128), F32), pltpu.VMEM((768, 768), BF16)],
        compiler_params=pltpu.CompilerParams(vmem_limit_bytes=VMEM_LIMIT),
        name="whiten",
    )(mine, other, attr)
    return out, factor


def solution(mesh):
    placed = (P(("survey", "inline"), "xline", "depth"), P(("survey", "inline"), "xline"), P())
    return jax.shard_map(
        local,
        mesh=mesh,
        in_specs=placed,
        out_specs=(P(None, ("survey", "inline"), "xline", "depth"), P("survey", None)),
        check_vma=False,
    )
```

```python
import functools
import math

import jax
import jax.numpy as jnp
from jax import lax
from jax.experimental import pallas as pl
from jax.experimental.pallas import tpu as pltpu
from jax.sharding import PartitionSpec as P

ORIENT = 32
TAPS = 5
CHAN = 96
REACH = 8
KEPT = 5
F32 = jnp.float32
BF16 = jnp.bfloat16
VMEM_LIMIT = 56 * 1024 * 1024


def iota(shape, dim):
    return lax.broadcasted_iota(jnp.int32, shape, dim)


def rounded(value):
    return value.astype(BF16).astype(F32)


def ones_where(mask):
    return jnp.where(mask, 1.0, 0.0).astype(BF16)


def dot(a, b):
    return jnp.dot(a, b, preferred_element_type=F32)


def shifted(value, axis, step):
    size = lax.axis_size(axis)
    return lax.ppermute(value, axis, [(i, i + step) for i in range(size) if 0 <= i + step < size])


def flipped(value, flips):
    axes = tuple(axis for axis, _ in flips)
    sizes = [lax.axis_size(axis) for axis in axes]
    pairs = []
    for source in range(math.prod(sizes)):
        target, rest, stride = 0, source, 1
        for size, (_, bit) in reversed(list(zip(sizes, flips))):
            target += ((rest % size) ^ bit) * stride
            rest, stride = rest // size, stride * size
        pairs.append((source, target))
    return lax.ppermute(value, axes, pairs)


def bits_of(axis):
    size = lax.axis_size(axis)
    assert size & (size - 1) == 0
    return [(axis, 2 ** i) for i in range(size.bit_length() - 1)]


def summed(value):
    x_bits, il_bits = bits_of("xline"), bits_of("inline")
    for bit in bits_of("depth") + x_bits[1:] + il_bits[2:]:
        value = value + flipped(value, [bit])
    one, two = il_bits[0], x_bits[0]
    a, b, c = flipped(value, [one]), flipped(value, [two]), flipped(value, [one, two])
    value = (value + a) + (b + c)
    return value, flipped(value, [il_bits[1]])


def halo_select(level, stored, x_left, depth_first):
    dilation = 2 ** level
    rows, cols = 256, TAPS * 128
    lane = iota((1, cols), 1)
    k = lane // 128
    within = lane % 128
    place = (within + 4) % 8 - 4
    q = ((within + 4) // 8) % 16
    j = 2 * q + dilation * (k - 2)
    slot = jnp.where(j < 0, 40 + j, j)
    if stored == 48:
        slot = jnp.where(j >= 32, j + 8, slot)
    else:
        slot = jnp.where((j < 0) & (x_left == 0), -999999, slot)
        slot = jnp.where((j >= 32) & (x_left == 1), -999999, slot)
    kept = jnp.where(place >= 0, place, place + 4)
    if level == 0:
        kept = jnp.where(place == -2, 4, kept)
    source = kept * stored + slot
    source = jnp.where((place >= 0) & (depth_first == 0), -1, source)
    source = jnp.where((place < 0) & (depth_first == 1), -1, source)
    return ones_where(iota((rows, cols), 0) == source)


def shift_matrix(shifts, odd):
    lane = iota((1, 128 * len(shifts)), 1)
    source = lane % 128
    for i, shift in enumerate(shifts):
        source = jnp.where(lane // 128 == i, source + shift, source)
    past = (source + 128) % 128 + 128 - (1 if odd else 0)
    source = jnp.where(source < 0, past, jnp.where(source >= 128, past, source))
    return ones_where(iota((256, 128 * len(shifts)), 0) == source)


def attributes_kernel(
    two_sided, place_ref, live_smem, live_ref, taps_ref, own_ref, before_ref, after_ref, xh_ref, dh_ref,
    attr_ref, gram_ref, bands, first0, first12, halo2, w2, w3, planes,
    moves0e, moves0o, moves1, moves2,
):
    x_left = place_ref[0]
    depth_first = place_ref[1]
    stored = 48 if two_sided else 40

    for k in range(TAPS):
        w2[k] = jnp.broadcast_to(taps_ref[1, :, k : k + 1], (CHAN, 128))
        w3[k] = jnp.broadcast_to(taps_ref[2, :, k : k + 1], (CHAN, 128))
    lane32 = iota((ORIENT, 128), 1)
    for level in range(3):
        cs = slice(level * ORIENT, (level + 1) * ORIENT)
        cols = [jnp.broadcast_to(taps_ref[0, cs, k : k + 1], (ORIENT, 128)) for k in range(TAPS)]
        for o in range(8):
            total = jnp.zeros((ORIENT, 128), F32)
            for k in range(TAPS):
                total = jnp.where(lane32 == REACH + 2 * o + 2 ** level * (k - 2), cols[k], total)
            bands[pl.ds(level * 256 + o * ORIENT, ORIENT), :] = total.astype(BF16)

    n = iota((256, 256), 1)
    pick = ones_where(iota((256, 256), 0) == jnp.where(n < 128, 2 * n, 2 * n - 255))
    r = iota((512, 512), 0)
    c = iota((512, 512), 1)
    turn = ones_where((c // 16 == r % 32) & (c % 16 == r // 32))
    own = dot(own_ref[...], pick).astype(BF16).reshape(16, 32, 256)
    before = dot(before_ref[...], pick).astype(BF16).reshape(8, 32, 256)
    after = dot(after_ref[...], pick).astype(BF16).reshape(8, 32, 256)
    for half in range(2):
        js = slice(half * 16, half * 16 + 16)
        block = jnp.concatenate([before[:, js], own[:, js], after[:, js]], axis=0).reshape(512, 256)
        planes[8 + half * 16 : 24 + half * 16] = dot(turn, block).astype(BF16).reshape(16, 32, 256)
    turn_x = ones_where((c % 256 // 8 == r % 32) & (c // 256 * 8 + c % 8 == r // 32))
    if two_sided:
        sides = dot(xh_ref[...], pick).astype(BF16)
    else:
        got = dot(xh_ref[...], pick)
        left = jnp.where(x_left == 1, 1.0, 0.0)
        sides = jnp.concatenate([got * left, got * (1.0 - left)], axis=0).astype(BF16)
    edges = dot(turn_x, sides).astype(BF16).reshape(16, 32, 256)
    planes[0:8] = edges[0:8]
    planes[40:48] = edges[8:16]

    a0 = bands[0:256, 0:32]
    a12 = bands[256:768, 0:32]

    def level0_first(j, _):
        first0[j] = rounded(dot(a0, planes[j + 6]))
        return 0

    lax.fori_loop(0, 35, level0_first, 0, unroll=7)

    def even_first(pair, _):
        both = jnp.concatenate([planes[4 * pair, :, 0:128], planes[4 * pair + 2, :, 0:128]], axis=1)
        out = rounded(dot(a12, both))
        first12[2 * pair] = out[:, 0:128]
        first12[2 * pair + 1] = out[:, 128:256]
        return 0

    lax.fori_loop(0, 12, even_first, 0, unroll=4)

    n = iota((1, 256), 1)
    kept = n // stored
    sample = 2 * kept - jnp.where(kept == 4, 1, 0) + jnp.where(depth_first == 1, 0, 120)
    sample = jnp.where(kept < KEPT, sample, -1)
    spread = ones_where(iota((128, 256), 0) == sample)
    rows = 32 * stored
    wide = dot(dh_ref[...].reshape(rows, 128), spread)
    wide = jnp.where(iota((rows, 256), 0) % stored == n % stored, wide, 0.0).astype(BF16)
    gather = ones_where(iota((32, rows), 1) // stored == iota((32, rows), 0))
    lanes = dot(gather, wide).astype(BF16)
    for level in range(3):
        cols = dot(lanes, halo_select(level, stored, x_left, depth_first)).astype(BF16)
        part = rounded(dot(bands[level * 256 : level * 256 + 256, 0:32], cols))
        cs = slice(level * ORIENT, (level + 1) * ORIENT)
        total = jnp.zeros((256, 128), F32)
        for k in range(TAPS):
            total = total + part[:, k * 128 : k * 128 + 128] * jnp.concatenate([w2[k, cs]] * 8, axis=0)
        halo2[level] = total.astype(BF16)

    moves0e[...] = shift_matrix((-1, 1), False)
    moves0o[...] = shift_matrix((-1,), True)
    moves1[...] = shift_matrix((-2, -1, 1, 2), False)
    moves2[...] = shift_matrix((-4, -2, 2, 4), False)

    def crossline(level, q, o):
        cs = slice(level * ORIENT, (level + 1) * ORIENT)
        s2 = [w2[k, cs] for k in range(TAPS)]
        if level == 0:
            rows = slice(o * ORIENT, (o + 1) * ORIENT)
            return [
                sum(s2[k] * first0[2 * q + k, rows, half] for k in range(TAPS)).astype(BF16)
                for half in (slice(0, 128), slice(128, 256))
            ]
        rows = slice((level - 1) * 256 + o * ORIENT, (level - 1) * 256 + (o + 1) * ORIENT)
        unit = 2 ** (level - 1)
        total = sum(s2[k] * first12[q + 4 + unit * (k - 2), rows, :] for k in range(TAPS))
        return [total.astype(BF16)]

    def one_q(q):
        lane = iota((1, 128), 1)
        place = jnp.where(lane < 4, lane, jnp.where(lane >= 124, lane - 128, -9999))
        source = jnp.where(place < -8, -1, (8 * q + place + 128) % 128)
        turn_q = ones_where(iota((128, 128), 0) == source)
        for level in range(3):
            cs = slice(level * ORIENT, (level + 1) * ORIENT)
            halo = dot(halo2[level], turn_q).astype(BF16)
            both = [crossline(level, q, o) for o in range(8)]
            even = jnp.concatenate([b[0] for b in both], axis=0)
            joined = jnp.concatenate([even, halo], axis=1)
            if level == 0:
                odd = jnp.concatenate([b[1] for b in both], axis=0)
                moved = dot(joined, moves0e[...])
                moved_odd = dot(jnp.concatenate([odd, halo], axis=1), moves0o[...])
            else:
                moved = dot(joined, (moves1 if level == 1 else moves2)[...])
            s3 = [w3[k, cs] for k in range(TAPS)]
            for o in range(8):
                rows = slice(o * ORIENT, (o + 1) * ORIENT)
                terms = [s3[2] * even[rows].astype(F32)]
                order = (0, 4) if level == 0 else (0, 1, 3, 4)
                for i, k in enumerate(order):
                    terms.append(s3[k] * moved[rows, i * 128 : i * 128 + 128])
                if level == 0:
                    terms.append(s3[1] * moved_odd[rows])
                    terms.append(s3[3] * odd[rows].astype(F32))
                total = sum(terms) * live_smem[2 * o, 2 * q].astype(F32)
                attr_ref[o * 16 + q, cs, :] = total.astype(BF16)

    def add_gram(q, total):
        for o in range(0, 8, 2):
            both = jnp.concatenate([attr_ref[o * 16 + q], attr_ref[o * 16 + 16 + q]], axis=1)
            total = total + lax.dot_general(
                both, both, (((1,), (1,)), ((), ())), preferred_element_type=F32
            )
        return total

    def next_q(q, total):
        total = add_gram(q - 1, total)
        one_q(q)
        return total

    one_q(0)
    gram = lax.fori_loop(1, 16, next_q, jnp.zeros((CHAN, CHAN), F32))
    gram = add_gram(15, gram)
    alive = live_ref[...]
    chosen = (iota(alive.shape, 0) % 2 == 0) & (iota(alive.shape, 1) % 2 == 0)
    count = jnp.sum(jnp.where(chosen, alive.astype(F32), 0.0)) * 128.0
    gram_ref[...] = jnp.full((CHAN, 128), count, F32)
    gram_ref[:, 0:CHAN] = gram


def whiten_kernel(mine_ref, other_ref, attr_ref, out_ref, factor_ref, inverse, kron):
    step = pl.program_id(0)

    @pl.when(step == 0)
    def _():
        total = mine_ref[...] + other_ref[...]
        lane = iota((8, 128), 1)
        sub = iota((8, 128), 0)
        count = jnp.broadcast_to(total[0:1, CHAN : CHAN + 1], (8, 128))
        blocks = []
        for g in range(CHAN // 8):
            blocks.append(jnp.where(lane < CHAN, total[8 * g : 8 * g + 8] / count, 0.0))
        row_lane = iota((1, 128), 1)

        def finish(j, row, pivot):
            scale = lax.rsqrt(pivot)
            factor_ref[j : j + 1, :] = (jnp.where(row_lane >= j, row, 0.0) * scale)[:, 0:CHAN]
            unit = jnp.where(row_lane == j, 1.0, row)
            inverse[j : j + 1, :] = jnp.where(row_lane <= j, unit, 0.0) * scale

        def spread_lane(block, j):
            return jnp.broadcast_to(block[:, j : j + 1], (8, 128))

        def spread_row(block, i):
            return jnp.broadcast_to(block[i : i + 1, :], (8, 128))

        for j in range(0, CHAN, 2):
            g, s = j // 8, j % 8
            top = blocks[g]
            col0, col1 = spread_lane(top, j), spread_lane(top, j + 1)
            row0, row1 = spread_row(top, s), spread_row(top, s + 1)
            a, b, c = spread_row(col0, s), spread_row(col0, s + 1), spread_row(col1, s + 1)
            recip = 1.0 / (a * c - b * b)
            ratio = b / a
            rest1 = row1 - ratio * jnp.where(lane == j, 1.0, row0)
            rest1 = jnp.where(lane == j, -ratio, rest1)
            finish(j, row0[0:1], a[0:1])
            finish(j + 1, rest1[0:1], (c - b * ratio)[0:1])
            if j == CHAN - 2:
                break
            unit0 = jnp.where(lane == j, 1.0, jnp.where(lane == j + 1, 0.0, row0))
            unit1 = jnp.where(lane == j, 0.0, jnp.where(lane == j + 1, 1.0, row1))
            up0 = (c * unit0 - b * unit1) * recip
            up1 = (a * unit1 - b * unit0) * recip
            for h in range(g, CHAN // 8):
                if h > g:
                    col0, col1 = spread_lane(blocks[h], j), spread_lane(blocks[h], j + 1)
                else:
                    col0 = jnp.where(sub > s + 1, col0, 0.0)
                    col1 = jnp.where(sub > s + 1, col1, 0.0)
                cleared = jnp.where((lane == j) | (lane == j + 1), 0.0, blocks[h])
                blocks[h] = cleared - (col0 * up0 + col1 * up1)
        low = inverse[:, 0:CHAN].astype(BF16)
        spread = ones_where(iota((CHAN, 768), 0) == iota((CHAN, 768), 1) % CHAN)
        wide = dot(low, spread).astype(BF16)
        tall = ones_where(iota((768, CHAN), 0) // 8 == iota((768, CHAN), 1))
        full = dot(tall, wide)
        keep = iota((768, 768), 0) % 8 == iota((768, 768), 1) // CHAN
        kron[...] = jnp.where(keep, full, 0.0).astype(BF16)

    weights = kron[...]
    halves = []
    for half in range(2):
        pair = [
            attr_ref[pl.ds((2 * step + i) * 16 + 8 * half, 8)].reshape(768, 128) for i in range(2)
        ]
        halves.append(dot(weights, jnp.concatenate(pair, axis=1)))
    for i in range(2):
        both = [half[:, i * 128 : i * 128 + 128].reshape(CHAN, 8, 128) for half in halves]
        out_ref[:, i] = jnp.concatenate(both, axis=1).astype(BF16)


def local(seismic, trace_live, filter_taps):
    il_len, xl_len, t_len = seismic.shape
    assert (il_len, xl_len, t_len) == (16, 32, 256) and lax.axis_size("depth") == 2
    live = seismic * trace_live.astype(BF16)[:, :, None]
    taps = filter_taps.astype(F32)
    x_index = lax.axis_index("xline")
    d_index = lax.axis_index("depth")
    two_sided = lax.axis_size("xline") > 2

    before = shifted(live[il_len - REACH :], "inline", 1)
    after = shifted(live[:REACH], "inline", -1)

    def stack(js):
        return jnp.concatenate([before[:, js], live[:, js], after[:, js]], axis=0)

    low, high = slice(0, REACH), slice(xl_len - REACH, xl_len)
    if two_sided:
        xh = [shifted(stack(high), "xline", 1), shifted(stack(low), "xline", -1)]
    else:
        xh = [flipped(jnp.where(x_index == 0, stack(high), stack(low)), [("xline", 1)])]
    def edge(ts):
        rows = jnp.concatenate([before[:, :, ts], live[:, :, ts], after[:, :, ts]], axis=0)
        return jnp.concatenate([rows] + [x[:, :, ts] for x in xh], axis=1)

    dh = jnp.where(d_index == 0, edge(slice(t_len - 128, t_len)), edge(slice(0, 128)))
    dh = flipped(dh, [("depth", 1)])

    place = jnp.stack([(x_index == 1).astype(jnp.int32), (d_index == 0).astype(jnp.int32)])
    vmem = pl.BlockSpec(memory_space=pltpu.VMEM)
    smem = pl.BlockSpec(memory_space=pltpu.SMEM)
    xrows = jnp.concatenate([x.reshape(256, t_len) for x in xh], axis=0)
    attr, gram = pl.pallas_call(
        functools.partial(attributes_kernel, two_sided),
        out_shape=(
            jax.ShapeDtypeStruct((128, CHAN, 128), BF16),
            jax.ShapeDtypeStruct((CHAN, 128), F32),
        ),
        in_specs=[smem, smem] + [vmem] * 7,
        out_specs=(vmem, vmem),
        scratch_shapes=[
            pltpu.VMEM((768, 128), BF16),
            pltpu.VMEM((35, 256, 256), F32),
            pltpu.VMEM((24, 512, 128), F32),
            pltpu.VMEM((3, 256, 128), BF16),
            pltpu.VMEM((TAPS, CHAN, 128), F32),
            pltpu.VMEM((TAPS, CHAN, 128), F32),
            pltpu.VMEM((48, 32, 256), BF16),
            pltpu.VMEM((256, 256), BF16),
            pltpu.VMEM((256, 128), BF16),
            pltpu.VMEM((256, 512), BF16),
            pltpu.VMEM((256, 512), BF16),
        ],
        compiler_params=pltpu.CompilerParams(vmem_limit_bytes=VMEM_LIMIT),
        name="attributes",
    )(
        place, trace_live, trace_live, taps, live.reshape(512, t_len),
        before.reshape(256, t_len), after.reshape(256, t_len), xrows, dh,
    )

    mine, other = summed(gram)
    out, factor = pl.pallas_call(
        whiten_kernel,
        grid=(4,),
        out_shape=(
            jax.ShapeDtypeStruct((CHAN, 8, 16, 128), BF16),
            jax.ShapeDtypeStruct((CHAN, CHAN), F32),
        ),
        in_specs=[vmem] * 3,
        out_specs=(
            pl.BlockSpec((CHAN, 2, 16, 128), lambda i: (0, i, 0, 0)),
            pl.BlockSpec((CHAN, CHAN), lambda i: (0, 0)),
        ),
        scratch_shapes=[pltpu.VMEM((CHAN, 128), F32), pltpu.VMEM((768, 768), BF16)],
        compiler_params=pltpu.CompilerParams(vmem_limit_bytes=VMEM_LIMIT),
        name="whiten",
    )(mine, other, attr)
    return out, factor


def solution(mesh):
    placed = (P(("survey", "inline"), "xline", "depth"), P(("survey", "inline"), "xline"), P())
    return jax.shard_map(
        local,
        mesh=mesh,
        in_specs=placed,
        out_specs=(P(None, ("survey", "inline"), "xline", "depth"), P("survey", None)),
        check_vma=False,
    )
```

```python
import functools
import math

import jax
import jax.numpy as jnp
from jax import lax
from jax.experimental import pallas as pl
from jax.experimental.pallas import tpu as pltpu
from jax.sharding import PartitionSpec as P

ORIENT = 32
TAPS = 5
CHAN = 96
REACH = 8
KEPT = 5
F32 = jnp.float32
BF16 = jnp.bfloat16
ATTR_VMEM = 30 * 1024 * 1024
WHITEN_VMEM = 14 * 1024 * 1024


def iota(shape, dim):
    return lax.broadcasted_iota(jnp.int32, shape, dim)


def rounded(value):
    return value.astype(BF16).astype(F32)


def ones_where(mask):
    return jnp.where(mask, 1.0, 0.0).astype(BF16)


def dot(a, b):
    return jnp.dot(a, b, preferred_element_type=F32)


def shifted(value, axis, step):
    size = lax.axis_size(axis)
    return lax.ppermute(value, axis, [(i, i + step) for i in range(size) if 0 <= i + step < size])


def flipped(value, flips):
    axes = tuple(axis for axis, _ in flips)
    sizes = [lax.axis_size(axis) for axis in axes]
    pairs = []
    for source in range(math.prod(sizes)):
        target, rest, stride = 0, source, 1
        for size, (_, bit) in reversed(list(zip(sizes, flips))):
            target += ((rest % size) ^ bit) * stride
            rest, stride = rest // size, stride * size
        pairs.append((source, target))
    return lax.ppermute(value, axes, pairs)


def bits_of(axis):
    size = lax.axis_size(axis)
    assert size & (size - 1) == 0
    return [(axis, 2 ** i) for i in range(size.bit_length() - 1)]


def summed(value):
    x_bits, il_bits = bits_of("xline"), bits_of("inline")
    for bit in bits_of("depth") + x_bits[1:] + il_bits[2:]:
        value = value + flipped(value, [bit])
    one, two = il_bits[0], x_bits[0]
    a, b, c = flipped(value, [one]), flipped(value, [two]), flipped(value, [one, two])
    value = (value + a) + (b + c)
    return value, flipped(value, [il_bits[1]])


def halo_select(level, stored, x_left, depth_first):
    dilation = 2 ** level
    rows, cols = 256, TAPS * 128
    lane = iota((1, cols), 1)
    k = lane // 128
    within = lane % 128
    place = (within + 4) % 8 - 4
    q = ((within + 4) // 8) % 16
    j = 2 * q + dilation * (k - 2)
    slot = jnp.where(j < 0, 40 + j, j)
    if stored == 48:
        slot = jnp.where(j >= 32, j + 8, slot)
    else:
        slot = jnp.where((j < 0) & (x_left == 0), -999999, slot)
        slot = jnp.where((j >= 32) & (x_left == 1), -999999, slot)
    kept = jnp.where(place >= 0, place, place + 4)
    if level == 0:
        kept = jnp.where(place == -2, 4, kept)
    source = kept * stored + slot
    source = jnp.where((place >= 0) & (depth_first == 0), -1, source)
    source = jnp.where((place < 0) & (depth_first == 1), -1, source)
    return ones_where(iota((rows, cols), 0) == source)


def shift_matrix(shifts):
    lane = iota((1, 128 * len(shifts)), 1)
    source = lane % 128
    for i, shift in enumerate(shifts):
        source = jnp.where(lane // 128 == i, source + shift, source)
    past = (source + 128) % 128 + 128
    source = jnp.where(source < 0, past, jnp.where(source >= 128, past, source))
    return ones_where(iota((256, 128 * len(shifts)), 0) == source)


def attributes_kernel(
    two_sided, place_ref, live_smem, live_ref, taps_ref, own_ref, before_ref, after_ref, xh_ref, dh_ref,
    attr_ref, gram_ref, bands, first0, first12, halo2, w2, w3, planes,
    moves1, moves2,
):
    x_left = place_ref[0]
    depth_first = place_ref[1]
    stored = 48 if two_sided else 40

    for k in range(TAPS):
        w2[k] = jnp.broadcast_to(taps_ref[1, :, k : k + 1], (CHAN, 128))
        w3[k] = jnp.broadcast_to(taps_ref[2, :, k : k + 1], (CHAN, 128))
    lane32 = iota((ORIENT, 128), 1)
    for level in range(3):
        cs = slice(level * ORIENT, (level + 1) * ORIENT)
        cols = [jnp.broadcast_to(taps_ref[0, cs, k : k + 1], (ORIENT, 128)) for k in range(TAPS)]
        for o in range(8):
            total = jnp.zeros((ORIENT, 128), F32)
            for k in range(TAPS):
                total = jnp.where(lane32 == REACH + 2 * o + 2 ** level * (k - 2), cols[k], total)
            bands[pl.ds(level * 256 + o * ORIENT, ORIENT), :] = total.astype(BF16)

    n = iota((256, 256), 1)
    pick = ones_where(iota((256, 256), 0) == jnp.where(n < 128, 2 * n, 2 * n - 255))
    r = iota((512, 512), 0)
    c = iota((512, 512), 1)
    turn = ones_where((c // 16 == r % 32) & (c % 16 == r // 32))
    own = dot(own_ref[...], pick).astype(BF16).reshape(16, 32, 256)
    before = dot(before_ref[...], pick).astype(BF16).reshape(8, 32, 256)
    after = dot(after_ref[...], pick).astype(BF16).reshape(8, 32, 256)
    for half in range(2):
        js = slice(half * 16, half * 16 + 16)
        block = jnp.concatenate([before[:, js], own[:, js], after[:, js]], axis=0).reshape(512, 256)
        planes[8 + half * 16 : 24 + half * 16] = dot(turn, block).astype(BF16).reshape(16, 32, 256)
    turn_x = ones_where((c % 256 // 8 == r % 32) & (c // 256 * 8 + c % 8 == r // 32))
    if two_sided:
        sides = dot(xh_ref[...], pick).astype(BF16)
    else:
        got = dot(xh_ref[...], pick)
        left = jnp.where(x_left == 1, 1.0, 0.0)
        sides = jnp.concatenate([got * left, got * (1.0 - left)], axis=0).astype(BF16)
    edges = dot(turn_x, sides).astype(BF16).reshape(16, 32, 256)
    planes[0:8] = edges[0:8]
    planes[40:48] = edges[8:16]

    a0 = bands[0:256, 0:32]
    a12 = bands[256:768, 0:32]

    def level0_first(j, _):
        first0[j] = rounded(dot(a0, planes[j + 6]))
        return 0

    lax.fori_loop(0, 35, level0_first, 0, unroll=7)

    def even_first(pair, _):
        both = jnp.concatenate([planes[4 * pair, :, 0:128], planes[4 * pair + 2, :, 0:128]], axis=1)
        out = rounded(dot(a12, both))
        first12[2 * pair] = out[:, 0:128]
        first12[2 * pair + 1] = out[:, 128:256]
        return 0

    lax.fori_loop(0, 12, even_first, 0, unroll=4)

    n = iota((1, 256), 1)
    kept = n // stored
    sample = 2 * kept - jnp.where(kept == 4, 1, 0) + jnp.where(depth_first == 1, 0, 120)
    sample = jnp.where(kept < KEPT, sample, -1)
    spread = ones_where(iota((128, 256), 0) == sample)
    rows = 32 * stored
    wide = dot(dh_ref[...].reshape(rows, 128), spread)
    wide = jnp.where(iota((rows, 256), 0) % stored == n % stored, wide, 0.0).astype(BF16)
    gather = ones_where(iota((32, rows), 1) // stored == iota((32, rows), 0))
    lanes = dot(gather, wide).astype(BF16)
    for level in range(3):
        cols = dot(lanes, halo_select(level, stored, x_left, depth_first)).astype(BF16)
        part = rounded(dot(bands[level * 256 : level * 256 + 256, 0:32], cols))
        cs = slice(level * ORIENT, (level + 1) * ORIENT)
        total = jnp.zeros((256, 128), F32)
        for k in range(TAPS):
            total = total + part[:, k * 128 : k * 128 + 128] * jnp.concatenate([w2[k, cs]] * 8, axis=0)
        total = rounded(total)
        if level == 0:
            w3_0, w3_1, w3_4 = [jnp.concatenate([w3[k, cs]] * 8, axis=0) for k in (0, 1, 4)]
            before_first = total * w3_0 + pltpu.roll(total, 1, 1) * w3_1
            total = jnp.where(iota((256, 128), 1) % 8 == 7, before_first, total * w3_4)
        halo2[level] = total

    moves1[...] = shift_matrix((-2, -1, 1, 2))
    moves2[...] = shift_matrix((-4, -2, 2, 4))

    def crossline(level, q, o, half=0):
        cs = slice(level * ORIENT, (level + 1) * ORIENT)
        s2 = [w2[k, cs] for k in range(TAPS)]
        if level == 0:
            rows = slice(o * ORIENT, (o + 1) * ORIENT)
            ts = slice(half * 128, half * 128 + 128)
            return sum(s2[k] * first0[2 * q + k, rows, ts] for k in range(TAPS))
        rows = slice((level - 1) * 256 + o * ORIENT, (level - 1) * 256 + (o + 1) * ORIENT)
        unit = 2 ** (level - 1)
        return sum(s2[k] * first12[q + 4 + unit * (k - 2), rows, :] for k in range(TAPS))

    def one_q(q):
        align = jnp.where(q == 0, 0, 128 - 8 * q)

        def put(o, level, total):
            total = total * live_smem[2 * o, 2 * q].astype(F32)
            attr_ref[o * 16 + q, level * ORIENT : (level + 1) * ORIENT, :] = total.astype(BF16)

        for level in (1, 2):
            halo = pltpu.roll(halo2[level], align, 1).astype(BF16)
            value = jnp.concatenate([crossline(level, q, o).astype(BF16) for o in range(8)], axis=0)
            joined = jnp.concatenate([value, halo], axis=1)
            moved = dot(joined, (moves1 if level == 1 else moves2)[...])
            s3 = [w3[k, level * ORIENT : (level + 1) * ORIENT] for k in range(TAPS)]
            for o in range(8):
                rows = slice(o * ORIENT, (o + 1) * ORIENT)
                total = s3[2] * value[rows].astype(F32)
                for i, k in enumerate((0, 1, 3, 4)):
                    total = total + s3[k] * moved[rows, i * 128 : i * 128 + 128]
                put(o, level, total)
        lane = iota((ORIENT, 128), 1)
        s3 = [w3[k, 0:ORIENT] for k in range(TAPS)]
        for o in range(8):
            even, odd = rounded(crossline(0, q, o, 0)), rounded(crossline(0, q, o, 1))
            halo = pltpu.roll(halo2[0, o * ORIENT : (o + 1) * ORIENT], align, 1)
            back = jnp.where(lane == 127, halo, s3[0] * even + s3[1] * odd)
            ahead = jnp.where(lane == 0, halo, s3[4] * even)
            moved = pltpu.roll(back, 1, 1) + pltpu.roll(ahead, 127, 1)
            put(o, 0, s3[2] * even + s3[3] * odd + moved)

    def add_gram(q, total):
        for o in range(0, 8, 2):
            both = jnp.concatenate([attr_ref[o * 16 + q], attr_ref[o * 16 + 16 + q]], axis=1)
            total = total + lax.dot_general(
                both, both, (((1,), (1,)), ((), ())), preferred_element_type=F32
            )
        return total

    def next_q(q, total):
        total = add_gram(q - 1, total)
        one_q(q)
        return total

    one_q(0)
    gram = lax.fori_loop(1, 16, next_q, jnp.zeros((CHAN, CHAN), F32))
    gram = add_gram(15, gram)
    alive = live_ref[...]
    chosen = (iota(alive.shape, 0) % 2 == 0) & (iota(alive.shape, 1) % 2 == 0)
    count = jnp.sum(jnp.where(chosen, alive.astype(F32), 0.0)) * 128.0
    gram_ref[...] = jnp.full((CHAN, 128), count, F32)
    gram_ref[:, 0:CHAN] = gram


def whiten_kernel(mine_ref, other_ref, attr_ref, out_ref, factor_ref, inverse, kron):
    step = pl.program_id(0)

    @pl.when(step == 0)
    def _():
        total = mine_ref[...] + other_ref[...]
        lane = iota((8, 128), 1)
        sub = iota((8, 128), 0)
        count = jnp.broadcast_to(total[0:1, CHAN : CHAN + 1], (8, 128))
        blocks = []
        for g in range(CHAN // 8):
            blocks.append(jnp.where(lane < CHAN, total[8 * g : 8 * g + 8] / count, 0.0))
        row_lane = iota((1, 128), 1)

        def finish(j, row, inv_row, pivot):
            scale = lax.rsqrt(pivot)
            factor_ref[j : j + 1, :] = (jnp.where(row_lane >= j, row, 0.0) * scale)[:, 0:CHAN]
            inverse[j : j + 1, :] = jnp.where(row_lane <= j, inv_row, 0.0) * scale

        def spread_lane(block, j):
            return jnp.broadcast_to(block[:, j : j + 1], (8, 128))

        def spread_row(block, i):
            return jnp.broadcast_to(block[i : i + 1, :], (8, 128))

        for j in range(0, CHAN, 4):
            g, s = j // 8, j % 8
            top = blocks[g]
            cols = [spread_lane(top, j + i) for i in range(4)]
            rows = [spread_row(top, s + i) for i in range(4)]
            d = [[spread_row(cols[min(m, i)], s + max(m, i)) for i in range(4)] for m in range(4)]
            p_inv = 1.0 / (d[0][0] * d[1][1] - d[0][1] * d[0][1])
            adj = [[d[1][1], -d[0][1]], [-d[0][1], d[0][0]]]
            h = [
                [(d[2 + m][0] * adj[0][i] + d[2 + m][1] * adj[1][i]) * p_inv for i in range(2)]
                for m in range(2)
            ]
            t = [
                [d[2 + m][2 + i] - (h[m][0] * d[0][2 + i] + h[m][1] * d[1][2 + i]) for i in range(2)]
                for m in range(2)
            ]
            t01 = t[1][0]
            t_inv = 1.0 / (t[0][0] * t[1][1] - t01 * t01)
            unit = []
            for i in range(4):
                value = rows[i]
                for m in range(4):
                    value = jnp.where(lane == j + m, 1.0 if m == i else 0.0, value)
                unit.append(value)
            below = [unit[2 + m] - (h[m][0] * unit[0] + h[m][1] * unit[1]) for m in range(2)]
            up2 = (t[1][1] * below[0] - t01 * below[1]) * t_inv
            up3 = (t[0][0] * below[1] - t01 * below[0]) * t_inv
            inner = [unit[0] * d[1][1] - unit[1] * d[0][1], unit[1] * d[0][0] - unit[0] * d[0][1]]
            up0 = inner[0] * p_inv - (h[0][0] * up2 + h[1][0] * up3)
            up1 = inner[1] * p_inv - (h[0][1] * up2 + h[1][1] * up3)
            ups = (up0, up1, up2, up3)
            ratio0 = d[0][1] / d[0][0]
            ratio1 = t01 / t[0][0]
            mix0 = rows[2] - (h[0][0] * rows[0] + h[0][1] * rows[1])
            mix1 = rows[3] - (h[1][0] * rows[0] + h[1][1] * rows[1])
            solved = [rows[0], rows[1] - ratio0 * rows[0], mix0, mix1 - ratio1 * mix0]
            inv_solved = [unit[0], unit[1] - ratio0 * unit[0], below[0], below[1] - ratio1 * below[0]]
            pivots = [d[0][0], d[1][1] - d[0][1] * ratio0, t[0][0], t[1][1] - t01 * ratio1]
            for i in range(4):
                finish(j + i, solved[i][0:1], inv_solved[i][0:1], pivots[i][0:1])
            if j == CHAN - 4:
                break
            inside = (lane >= j) & (lane < j + 4)
            for k in range(g, CHAN // 8):
                if k > g:
                    cols = [spread_lane(blocks[k], j + i) for i in range(4)]
                else:
                    if s == 4:
                        continue
                    cols = [jnp.where(sub > s + 3, col, 0.0) for col in cols]
                change = (cols[0] * ups[0] + cols[1] * ups[1]) + (cols[2] * ups[2] + cols[3] * ups[3])
                blocks[k] = jnp.where(inside, 0.0, blocks[k]) - change
        low = inverse[:, 0:CHAN].astype(BF16)
        spread = ones_where(iota((CHAN, 768), 0) == iota((CHAN, 768), 1) % CHAN)
        wide = dot(low, spread).astype(BF16)
        tall = ones_where(iota((768, CHAN), 0) // 8 == iota((768, CHAN), 1))
        full = dot(tall, wide)
        keep = iota((768, 768), 0) % 8 == iota((768, 768), 1) // CHAN
        kron[...] = jnp.where(keep, full, 0.0).astype(BF16)

    weights = kron[...]
    halves = []
    for half in range(2):
        pair = [
            attr_ref[pl.ds((2 * step + i) * 16 + 8 * half, 8)].reshape(768, 128) for i in range(2)
        ]
        halves.append(dot(weights, jnp.concatenate(pair, axis=1)))
    for i in range(2):
        both = [half[:, i * 128 : i * 128 + 128].reshape(CHAN, 8, 128) for half in halves]
        out_ref[:, i] = jnp.concatenate(both, axis=1).astype(BF16)


def local(seismic, trace_live, filter_taps):
    il_len, xl_len, t_len = seismic.shape
    assert (il_len, xl_len, t_len) == (16, 32, 256) and lax.axis_size("depth") == 2
    live = seismic * trace_live.astype(BF16)[:, :, None]
    taps = filter_taps.astype(F32)
    x_index = lax.axis_index("xline")
    d_index = lax.axis_index("depth")
    two_sided = lax.axis_size("xline") > 2

    before = shifted(live[il_len - REACH :], "inline", 1)
    after = shifted(live[:REACH], "inline", -1)

    def stack(js):
        return jnp.concatenate([before[:, js], live[:, js], after[:, js]], axis=0)

    low, high = slice(0, REACH), slice(xl_len - REACH, xl_len)
    if two_sided:
        xh = [shifted(stack(high), "xline", 1), shifted(stack(low), "xline", -1)]
    else:
        xh = [flipped(jnp.where(x_index == 0, stack(high), stack(low)), [("xline", 1)])]
    def edge(ts):
        rows = jnp.concatenate([before[:, :, ts], live[:, :, ts], after[:, :, ts]], axis=0)
        return jnp.concatenate([rows] + [x[:, :, ts] for x in xh], axis=1)

    dh = jnp.where(d_index == 0, edge(slice(t_len - 128, t_len)), edge(slice(0, 128)))
    dh = flipped(dh, [("depth", 1)])

    place = jnp.stack([(x_index == 1).astype(jnp.int32), (d_index == 0).astype(jnp.int32)])
    vmem = pl.BlockSpec(memory_space=pltpu.VMEM)
    smem = pl.BlockSpec(memory_space=pltpu.SMEM)
    xrows = jnp.concatenate([x.reshape(256, t_len) for x in xh], axis=0)
    attr, gram = pl.pallas_call(
        functools.partial(attributes_kernel, two_sided),
        out_shape=(
            jax.ShapeDtypeStruct((128, CHAN, 128), BF16),
            jax.ShapeDtypeStruct((CHAN, 128), F32),
        ),
        in_specs=[smem, smem] + [vmem] * 7,
        out_specs=(vmem, vmem),
        scratch_shapes=[
            pltpu.VMEM((768, 128), BF16),
            pltpu.VMEM((35, 256, 256), F32),
            pltpu.VMEM((24, 512, 128), F32),
            pltpu.VMEM((3, 256, 128), F32),
            pltpu.VMEM((TAPS, CHAN, 128), F32),
            pltpu.VMEM((TAPS, CHAN, 128), F32),
            pltpu.VMEM((48, 32, 256), BF16),
            pltpu.VMEM((256, 512), BF16),
            pltpu.VMEM((256, 512), BF16),
        ],
        compiler_params=pltpu.CompilerParams(vmem_limit_bytes=ATTR_VMEM),
        name="attributes",
    )(
        place, trace_live, trace_live, taps, live.reshape(512, t_len),
        before.reshape(256, t_len), after.reshape(256, t_len), xrows, dh,
    )

    mine, other = summed(gram)
    out, factor = pl.pallas_call(
        whiten_kernel,
        grid=(4,),
        out_shape=(
            jax.ShapeDtypeStruct((CHAN, 8, 16, 128), BF16),
            jax.ShapeDtypeStruct((CHAN, CHAN), F32),
        ),
        in_specs=[vmem] * 3,
        out_specs=(
            pl.BlockSpec((CHAN, 2, 16, 128), lambda i: (0, i, 0, 0)),
            pl.BlockSpec((CHAN, CHAN), lambda i: (0, 0)),
        ),
        scratch_shapes=[pltpu.VMEM((CHAN, 128), F32), pltpu.VMEM((768, 768), BF16)],
        compiler_params=pltpu.CompilerParams(vmem_limit_bytes=WHITEN_VMEM),
        name="whiten",
    )(mine, other, attr)
    return out, factor


def solution(mesh):
    placed = (P(("survey", "inline"), "xline", "depth"), P(("survey", "inline"), "xline"), P())
    return jax.shard_map(
        local,
        mesh=mesh,
        in_specs=placed,
        out_specs=(P(None, ("survey", "inline"), "xline", "depth"), P("survey", None)),
        check_vma=False,
    )
```

```python
import functools
import math

import jax
import jax.numpy as jnp
from jax import lax
from jax.experimental import pallas as pl
from jax.experimental.pallas import tpu as pltpu
from jax.sharding import PartitionSpec as P

ORIENT = 32
TAPS = 5
CHAN = 96
REACH = 8
KEPT = 5
F32 = jnp.float32
BF16 = jnp.bfloat16
LIVE_VMEM = 4 * 1024 * 1024
INLINE_VMEM = 22 * 1024 * 1024
CROSS_VMEM = 16 * 1024 * 1024
ATTR_VMEM = 22 * 1024 * 1024
WHITEN_VMEM = 14 * 1024 * 1024


def iota(shape, dim):
    return lax.broadcasted_iota(jnp.int32, shape, dim)


def rounded(value):
    return value.astype(BF16).astype(F32)


def ones_where(mask):
    return jnp.where(mask, 1.0, 0.0).astype(BF16)


def dot(a, b):
    return jnp.dot(a, b, preferred_element_type=F32)


def shifted(value, axis, step):
    size = lax.axis_size(axis)
    return lax.ppermute(value, axis, [(i, i + step) for i in range(size) if 0 <= i + step < size])


def flipped(value, flips):
    axes = tuple(axis for axis, _ in flips)
    sizes = [lax.axis_size(axis) for axis in axes]
    pairs = []
    for source in range(math.prod(sizes)):
        target, rest, stride = 0, source, 1
        for size, (_, bit) in reversed(list(zip(sizes, flips))):
            target += ((rest % size) ^ bit) * stride
            rest, stride = rest // size, stride * size
        pairs.append((source, target))
    return lax.ppermute(value, axes, pairs)


def bits_of(axis):
    size = lax.axis_size(axis)
    assert size & (size - 1) == 0
    return [(axis, 2 ** i) for i in range(size.bit_length() - 1)]


def summed(value):
    x_bits, il_bits = bits_of("xline"), bits_of("inline")
    for bit in bits_of("depth") + x_bits[1:] + il_bits[2:]:
        value = value + flipped(value, [bit])
    one, two = il_bits[0], x_bits[0]
    a, b, c = flipped(value, [one]), flipped(value, [two]), flipped(value, [one, two])
    value = (value + a) + (b + c)
    return value, flipped(value, [il_bits[1]])


def halo_select(level, stored, x_left, depth_first):
    dilation = 2 ** level
    rows, cols = 256, TAPS * 128
    lane = iota((1, cols), 1)
    k = lane // 128
    within = lane % 128
    place = (within + 4) % 8 - 4
    q = ((within + 4) // 8) % 16
    j = 2 * q + dilation * (k - 2)
    slot = jnp.where(j < 0, 40 + j, j)
    if stored == 48:
        slot = jnp.where(j >= 32, j + 8, slot)
    else:
        slot = jnp.where((j < 0) & (x_left == 0), -999999, slot)
        slot = jnp.where((j >= 32) & (x_left == 1), -999999, slot)
    kept = jnp.where(place >= 0, place, place + 4)
    if level == 0:
        kept = jnp.where(place == -2, 4, kept)
    source = kept * stored + slot
    source = jnp.where((place >= 0) & (depth_first == 0), -1, source)
    source = jnp.where((place < 0) & (depth_first == 1), -1, source)
    return ones_where(iota((rows, cols), 0) == source)


def shift_matrix(shifts):
    lane = iota((1, 128 * len(shifts)), 1)
    source = lane % 128
    for i, shift in enumerate(shifts):
        source = jnp.where(lane // 128 == i, source + shift, source)
    past = (source + 128) % 128 + 128
    source = jnp.where(source < 0, past, jnp.where(source >= 128, past, source))
    return ones_where(iota((256, 128 * len(shifts)), 0) == source)


def side_flags():
    x_left = jnp.where(lax.axis_index("xline") == 1, 1, 0)
    depth_first = jnp.where(lax.axis_index("depth") == 0, 1, 0)
    return x_left, depth_first, lax.axis_index("inline") % 2


def live_kernel(trace_ref, seismic_ref, live_ref, near_ref, far_ref):
    n_il, n_xl, _ = seismic_ref.shape
    eye = iota((n_xl, n_xl), 0) == iota((n_xl, n_xl), 1)
    for p in range(n_il):
        row = jnp.broadcast_to(trace_ref[p : p + 1, :].astype(F32), (n_xl, n_xl))
        kept = dot(jnp.where(eye, row, 0.0).astype(BF16), seismic_ref[p])
        live_ref[p * n_xl : (p + 1) * n_xl, :] = kept.astype(BF16)
    count = REACH * n_xl
    start = (n_il - REACH) * n_xl
    odd = side_flags()[2]

    @pl.when(odd == 1)
    def _():
        near_ref[...] = live_ref[0:count]
        far_ref[...] = live_ref[start : start + count]

    @pl.when(odd == 0)
    def _():
        near_ref[...] = live_ref[start : start + count]
        far_ref[...] = live_ref[0:count]


def banded(level, taps_ref, bands, il_odd):
    lane = iota((ORIENT, 128), 1)
    cs = slice(level * ORIENT, (level + 1) * ORIENT)
    cols = [jnp.broadcast_to(taps_ref[0, cs, k : k + 1], (ORIENT, 128)) for k in range(TAPS)]
    for o in range(8):
        total = jnp.zeros((ORIENT, 128), F32)
        for k in range(TAPS):
            p = 2 * o + 2 ** level * (k - 2)
            if p < 0:
                place = p + 32 - 8 * il_odd
            elif p >= 16:
                place = p + 8 * il_odd
            else:
                place = p
            total = jnp.where(lane == place, cols[k], total)
        bands[pl.ds(level * 256 + o * ORIENT, ORIENT), :] = total.astype(BF16)


def phase_pick():
    n = iota((256, 256), 1)
    return ones_where(iota((256, 256), 0) == jnp.where(n < 128, 2 * n, 2 * n - 255))


def inline_kernel(
    taps_ref, own_ref, near_ref, far_ref, bands, w2, w3, first0, first12, edge_ref, planes
):
    _, depth_first, il_odd = side_flags()

    def put_edge(ts):
        for at, ref in ((0, own_ref), (512, near_ref), (768, far_ref)):
            edge_ref[at : at + ref.shape[0], :] = ref[:, ts]

    pl.when(depth_first == 1)(lambda: put_edge(slice(128, 256)))
    pl.when(depth_first == 0)(lambda: put_edge(slice(0, 128)))
    for k in range(TAPS):
        w2[k] = jnp.broadcast_to(taps_ref[1, :, k : k + 1], (CHAN, 128))
        w3[k] = jnp.broadcast_to(taps_ref[2, :, k : k + 1], (CHAN, 128))
    for level in range(3):
        banded(level, taps_ref, bands, il_odd)

    pick = phase_pick()
    r = iota((512, 512), 0)
    c = iota((512, 512), 1)
    turn = ones_where((c // 16 == r % 32) & (c % 16 == r // 32))
    own = dot(own_ref[...], pick).astype(BF16).reshape(16, 32, 256)
    near = dot(near_ref[...], pick).astype(BF16).reshape(8, 32, 256)
    far = dot(far_ref[...], pick).astype(BF16).reshape(8, 32, 256)
    for half in range(2):
        js = slice(half * 16, half * 16 + 16)
        block = jnp.concatenate([own[:, js], near[:, js], far[:, js]], axis=0).reshape(512, 256)
        planes[half * 16 : half * 16 + 16] = dot(turn, block).astype(BF16).reshape(16, 32, 256)

    a0 = bands[0:256, 0:32]
    a12 = bands[256:768, 0:32]
    for j in (0, 1, 34):
        first0[j] = jnp.zeros((256, 256), F32)
    for j in (0, 1, 2, 3, 20, 21, 22, 23):
        first12[j] = jnp.zeros((512, 128), F32)

    def level0_first(j, _):
        first0[j + 2] = rounded(dot(a0, planes[j]))
        return 0

    lax.fori_loop(0, 32, level0_first, 0, unroll=8)

    def even_first(pair, _):
        both = jnp.concatenate([planes[4 * pair, :, 0:128], planes[4 * pair + 2, :, 0:128]], axis=1)
        out = rounded(dot(a12, both))
        first12[2 * pair + 4] = out[:, 0:128]
        first12[2 * pair + 5] = out[:, 128:256]
        return 0

    lax.fori_loop(0, 8, even_first, 0, unroll=4)


def tall(ref, level, k):
    return jnp.concatenate([ref[k, level * ORIENT : (level + 1) * ORIENT]] * 8, axis=0)


def crossline_kernel(
    two_sided, bands, w2, first12, xh_ref, extra0, second12, edges, extra1, extra2
):
    x_left = side_flags()[0]

    r = iota((512, 512), 0)
    c = iota((512, 512), 1)
    turn_x = ones_where((c % 256 // 8 == r % 32) & (c // 256 * 8 + c % 8 == r // 32))
    got = dot(xh_ref[...], phase_pick())
    if not two_sided:
        left = jnp.where(x_left == 1, 1.0, 0.0)
        got = jnp.concatenate([got * left, got * (1.0 - left)], axis=0)
    edges[...] = dot(turn_x, got.astype(BF16)).astype(BF16).reshape(16, 32, 256)
    a0 = bands[0:256, 0:32]
    a12 = bands[256:768, 0:32]
    out0 = {j: rounded(dot(a0, edges[slot])) for j, slot in ((-2, 6), (-1, 7), (32, 8))}
    out12 = {}
    for slot in (0, 4, 8, 12):
        both = jnp.concatenate([edges[slot, :, 0:128], edges[slot + 2, :, 0:128]], axis=1)
        out = rounded(dot(a12, both))
        e = slot // 2 - 4 if slot < 8 else slot // 2 + 12
        out12[e], out12[e + 1] = out[:, 0:128], out[:, 128:256]

    extra0[0] = jnp.zeros((256, 256), F32)
    for slot, q in ((1, 0), (2, 15)):
        total = jnp.zeros((256, 256), F32)
        for k in range(TAPS):
            if 2 * q + k - 2 in out0:
                total = total + jnp.concatenate([tall(w2, 0, k)] * 2, axis=1) * out0[2 * q + k - 2]
        extra0[slot] = total
    for level, extra in ((1, extra1), (2, extra2)):
        reach = 2 * level
        extra[0] = jnp.zeros((256, 128), F32)
        for slot in range(2 * reach):
            q = slot if slot < reach else 16 - 2 * reach + slot
            total = jnp.zeros((256, 128), F32)
            for k in range(TAPS):
                e = q + level * (k - 2)
                if e in out12:
                    total = total + tall(w2, level, k) * out12[e][(level - 1) * 256 : level * 256]
            extra[slot + 1] = total

    def one_q(q, _):
        for level in (1, 2):
            extra = extra1 if level == 1 else extra2
            reach = 2 * level
            slot = jnp.where(q < reach, q + 1, jnp.where(q >= 16 - reach, q + 2 * reach - 15, 0))
            for c16 in range(2):
                start = level * ORIENT + c16 * 16
                s2 = [w2[k, start : start + 16] for k in range(TAPS)]
                for o in range(8):
                    row = o * ORIENT + c16 * 16
                    here = slice((level - 1) * 256 + row, (level - 1) * 256 + row + 16)
                    total = extra[slot, row : row + 16, :]
                    for k in range(TAPS):
                        total = total + s2[k] * first12[q + 4 + level * (k - 2), here, :]
                    second12[q, here, :] = total.astype(BF16)
        return 0

    lax.fori_loop(0, 16, one_q, 0)


def attributes_kernel(
    two_sided, live_smem, live_ref, bands, w2, w3, first0, extra0, second12, dh_ref,
    attr_ref, gram_ref, halo2, moves1, moves2,
):
    x_left, depth_first, _ = side_flags()
    stored = 48 if two_sided else 40

    n = iota((1, 256), 1)
    kept = n // stored
    sample = 2 * kept - jnp.where(kept == 4, 1, 0) + jnp.where(depth_first == 1, 0, 120)
    sample = jnp.where(kept < KEPT, sample, -1)
    spread = ones_where(iota((128, 256), 0) == sample)
    rows = 32 * stored
    wide = dot(dh_ref[...].reshape(rows, 128), spread)
    wide = jnp.where(iota((rows, 256), 0) % stored == n % stored, wide, 0.0).astype(BF16)
    gather = ones_where(iota((32, rows), 1) // stored == iota((32, rows), 0))
    lanes = dot(gather, wide).astype(BF16)
    for level in range(3):
        cols = dot(lanes, halo_select(level, stored, x_left, depth_first)).astype(BF16)
        part = rounded(dot(bands[level * 256 : level * 256 + 256, 0:32], cols))
        total = jnp.zeros((256, 128), F32)
        for k in range(TAPS):
            total = total + part[:, k * 128 : k * 128 + 128] * tall(w2, level, k)
        total = rounded(total)
        if level == 0:
            w3_0, w3_1, w3_4 = [tall(w3, 0, k) for k in (0, 1, 4)]
            before_first = total * w3_0 + pltpu.roll(total, 1, 1) * w3_1
            total = jnp.where(iota((256, 128), 1) % 8 == 7, before_first, total * w3_4)
        halo2[level] = total

    moves1[...] = shift_matrix((-2, -1, 1, 2))
    moves2[...] = shift_matrix((-4, -2, 2, 4))

    def one_q(q):
        align = jnp.where(q == 0, 0, 128 - 8 * q)
        live_q = [live_smem[2 * o, 2 * q].astype(F32) for o in range(8)]
        lane = iota((16, 128), 1)

        def put(o, start, total):
            attr_ref[o * 16 + q, start : start + 16, :] = (total * live_q[o]).astype(BF16)

        for level in (1, 2):
            halo = pltpu.roll(halo2[level], align, 1).astype(BF16)
            value = second12[q, (level - 1) * 256 : level * 256, :]
            moved = dot(jnp.concatenate([value, halo], axis=1), (moves1 if level == 1 else moves2)[...])
            for c16 in range(2):
                start = level * ORIENT + c16 * 16
                s3 = [w3[k, start : start + 16] for k in range(TAPS)]
                for o in range(8):
                    rows = slice(o * ORIENT + c16 * 16, o * ORIENT + c16 * 16 + 16)
                    total = s3[2] * value[rows].astype(F32)
                    for i, k in enumerate((0, 1, 3, 4)):
                        total = total + s3[k] * moved[rows, i * 128 : i * 128 + 128]
                    put(o, start, total)
        slot = jnp.where(q == 0, 1, jnp.where(q == 15, 2, 0))
        for c16 in range(2):
            s2 = [w2[k, c16 * 16 : c16 * 16 + 16] for k in range(TAPS)]
            s3 = [w3[k, c16 * 16 : c16 * 16 + 16] for k in range(TAPS)]
            for o in range(8):
                rows = slice(o * ORIENT + c16 * 16, o * ORIENT + c16 * 16 + 16)
                both = []
                for ts in (slice(0, 128), slice(128, 256)):
                    total = extra0[slot, rows, ts]
                    for k in range(TAPS):
                        total = total + s2[k] * first0[2 * q + k, rows, ts]
                    both.append(rounded(total))
                even, odd = both
                halo = pltpu.roll(halo2[0, rows], align, 1)
                back = jnp.where(lane == 127, halo, s3[0] * even + s3[1] * odd)
                ahead = jnp.where(lane == 0, halo, s3[4] * even)
                moved = pltpu.roll(back, 1, 1) + pltpu.roll(ahead, 127, 1)
                put(o, c16 * 16, s3[2] * even + s3[3] * odd + moved)

    def add_gram(q, total):
        for o in range(0, 8, 2):
            both = jnp.concatenate([attr_ref[o * 16 + q], attr_ref[o * 16 + 16 + q]], axis=1)
            total = total + lax.dot_general(
                both, both, (((1,), (1,)), ((), ())), preferred_element_type=F32
            )
        return total

    def next_q(q, total):
        total = add_gram(q - 1, total)
        one_q(q)
        return total

    one_q(0)
    gram = lax.fori_loop(1, 16, next_q, jnp.zeros((CHAN, CHAN), F32))
    gram = add_gram(15, gram)
    alive = live_ref[...]
    chosen = (iota(alive.shape, 0) % 2 == 0) & (iota(alive.shape, 1) % 2 == 0)
    count = jnp.sum(jnp.where(chosen, alive.astype(F32), 0.0)) * 128.0
    gram_ref[...] = jnp.full((CHAN, 128), count, F32)
    gram_ref[:, 0:CHAN] = gram


def whiten_kernel(mine_ref, other_ref, attr_ref, out_ref, factor_ref, inverse, kron):
    step = pl.program_id(0)

    @pl.when(step == 0)
    def _():
        total = mine_ref[...] + other_ref[...]
        lane = iota((8, 128), 1)
        sub = iota((8, 128), 0)
        count = jnp.broadcast_to(total[0:1, CHAN : CHAN + 1], (8, 128))
        blocks = []
        for g in range(CHAN // 8):
            blocks.append(jnp.where(lane < CHAN, total[8 * g : 8 * g + 8] / count, 0.0))
        row_lane = iota((1, 128), 1)

        def finish(j, row, inv_row, pivot):
            scale = lax.rsqrt(pivot)
            factor_ref[j : j + 1, :] = (jnp.where(row_lane >= j, row, 0.0) * scale)[:, 0:CHAN]
            inverse[j : j + 1, :] = jnp.where(row_lane <= j, inv_row, 0.0) * scale

        def spread_lane(block, j):
            return jnp.broadcast_to(block[:, j : j + 1], (8, 128))

        def spread_row(block, i):
            return jnp.broadcast_to(block[i : i + 1, :], (8, 128))

        for j in range(0, CHAN, 4):
            g, s = j // 8, j % 8
            top = blocks[g]
            cols = [spread_lane(top, j + i) for i in range(4)]
            rows = [spread_row(top, s + i) for i in range(4)]
            d = [[spread_row(cols[min(m, i)], s + max(m, i)) for i in range(4)] for m in range(4)]
            p_inv = 1.0 / (d[0][0] * d[1][1] - d[0][1] * d[0][1])
            adj = [[d[1][1], -d[0][1]], [-d[0][1], d[0][0]]]
            h = [
                [(d[2 + m][0] * adj[0][i] + d[2 + m][1] * adj[1][i]) * p_inv for i in range(2)]
                for m in range(2)
            ]
            t = [
                [d[2 + m][2 + i] - (h[m][0] * d[0][2 + i] + h[m][1] * d[1][2 + i]) for i in range(2)]
                for m in range(2)
            ]
            t01 = t[1][0]
            t_inv = 1.0 / (t[0][0] * t[1][1] - t01 * t01)
            unit = []
            for i in range(4):
                value = rows[i]
                for m in range(4):
                    value = jnp.where(lane == j + m, 1.0 if m == i else 0.0, value)
                unit.append(value)
            below = [unit[2 + m] - (h[m][0] * unit[0] + h[m][1] * unit[1]) for m in range(2)]
            up2 = (t[1][1] * below[0] - t01 * below[1]) * t_inv
            up3 = (t[0][0] * below[1] - t01 * below[0]) * t_inv
            inner = [unit[0] * d[1][1] - unit[1] * d[0][1], unit[1] * d[0][0] - unit[0] * d[0][1]]
            up0 = inner[0] * p_inv - (h[0][0] * up2 + h[1][0] * up3)
            up1 = inner[1] * p_inv - (h[0][1] * up2 + h[1][1] * up3)
            ups = (up0, up1, up2, up3)
            ratio0 = d[0][1] / d[0][0]
            ratio1 = t01 / t[0][0]
            mix0 = rows[2] - (h[0][0] * rows[0] + h[0][1] * rows[1])
            mix1 = rows[3] - (h[1][0] * rows[0] + h[1][1] * rows[1])
            solved = [rows[0], rows[1] - ratio0 * rows[0], mix0, mix1 - ratio1 * mix0]
            inv_solved = [unit[0], unit[1] - ratio0 * unit[0], below[0], below[1] - ratio1 * below[0]]
            pivots = [d[0][0], d[1][1] - d[0][1] * ratio0, t[0][0], t[1][1] - t01 * ratio1]
            for i in range(4):
                finish(j + i, solved[i][0:1], inv_solved[i][0:1], pivots[i][0:1])
            if j == CHAN - 4:
                break
            inside = (lane >= j) & (lane < j + 4)
            for k in range(g, CHAN // 8):
                if k > g:
                    cols = [spread_lane(blocks[k], j + i) for i in range(4)]
                else:
                    if s == 4:
                        continue
                    cols = [jnp.where(sub > s + 3, col, 0.0) for col in cols]
                change = (cols[0] * ups[0] + cols[1] * ups[1]) + (cols[2] * ups[2] + cols[3] * ups[3])
                blocks[k] = jnp.where(inside, 0.0, blocks[k]) - change
        low = inverse[:, 0:CHAN].astype(BF16)
        spread = ones_where(iota((CHAN, 768), 0) == iota((CHAN, 768), 1) % CHAN)
        wide = dot(low, spread).astype(BF16)
        tall = ones_where(iota((768, CHAN), 0) // 8 == iota((768, CHAN), 1))
        full = dot(tall, wide)
        keep = iota((768, 768), 0) % 8 == iota((768, 768), 1) // CHAN
        kron[...] = jnp.where(keep, full, 0.0).astype(BF16)

    weights = kron[...]
    halves = []
    for half in range(2):
        pair = [
            attr_ref[pl.ds((2 * step + i) * 16 + 8 * half, 8)].reshape(768, 128) for i in range(2)
        ]
        halves.append(dot(weights, jnp.concatenate(pair, axis=1)))
    for i in range(2):
        both = [half[:, i * 128 : i * 128 + 128].reshape(CHAN, 8, 128) for half in halves]
        out_ref[:, i] = jnp.concatenate(both, axis=1).astype(BF16)


def local(seismic, trace_live, filter_taps):
    il_len, xl_len, t_len = seismic.shape
    assert (il_len, xl_len, t_len) == (16, 32, 256) and lax.axis_size("depth") == 2
    taps = filter_taps.astype(F32)
    x_index = lax.axis_index("xline")
    d_index = lax.axis_index("depth")
    two_sided = lax.axis_size("xline") > 2
    vmem = pl.BlockSpec(memory_space=pltpu.VMEM)
    smem = pl.BlockSpec(memory_space=pltpu.SMEM)

    live, near, far = pl.pallas_call(
        live_kernel,
        out_shape=(
            jax.ShapeDtypeStruct((il_len * xl_len, t_len), BF16),
            jax.ShapeDtypeStruct((REACH * xl_len, t_len), BF16),
            jax.ShapeDtypeStruct((REACH * xl_len, t_len), BF16),
        ),
        in_specs=[vmem] * 2,
        out_specs=(vmem,) * 3,
        compiler_params=pltpu.CompilerParams(vmem_limit_bytes=LIVE_VMEM),
        name="live",
    )(trace_live, seismic)
    il_size = lax.axis_size("inline")
    near_pairs = [(i, i ^ 1) for i in range(il_size) if i ^ 1 < il_size]
    far_pairs = [(i, i - 1 if i % 2 == 0 else i + 1) for i in range(1, il_size)]
    far_pairs = [(i, j) for i, j in far_pairs if j < il_size]
    near = lax.ppermute(near, "inline", near_pairs)
    far = lax.ppermute(far, "inline", far_pairs)
    parts = [v.reshape(-1, xl_len, t_len) for v in (live, near, far)]

    def stack(js):
        return jnp.concatenate([v[:, js] for v in parts], axis=0)

    low, high = slice(0, REACH), slice(xl_len - REACH, xl_len)
    if two_sided:
        xh = [shifted(stack(high), "xline", 1), shifted(stack(low), "xline", -1)]
    else:
        xh = [flipped(jnp.where(x_index == 0, stack(high), stack(low)), [("xline", 1)])]
    bands, w2, w3, first0, first12, edge = pl.pallas_call(
        inline_kernel,
        out_shape=(
            jax.ShapeDtypeStruct((3 * 256, 128), BF16),
            jax.ShapeDtypeStruct((TAPS, CHAN, 128), F32),
            jax.ShapeDtypeStruct((TAPS, CHAN, 128), F32),
            jax.ShapeDtypeStruct((35, 256, 256), F32),
            jax.ShapeDtypeStruct((24, 512, 128), F32),
            jax.ShapeDtypeStruct((32 * xl_len, 128), BF16),
        ),
        in_specs=[vmem] * 4,
        out_specs=(vmem,) * 6,
        scratch_shapes=[pltpu.VMEM((32, 32, 256), BF16)],
        compiler_params=pltpu.CompilerParams(vmem_limit_bytes=INLINE_VMEM),
        cost_estimate=pl.CostEstimate(flops=4 * 10**9, bytes_accessed=16 * 10**6, transcendentals=0),
        name="inline",
    )(taps, live, near, far)

    def side(x):
        return jnp.where(d_index == 0, x[:, :, t_len - 128 :], x[:, :, :128])

    dh = jnp.concatenate([edge.reshape(32, xl_len, 128)] + [side(x) for x in xh], axis=1)
    dh = flipped(dh, [("depth", 1)])
    xrows = jnp.concatenate([x.reshape(256, t_len) for x in xh], axis=0)
    extra0, second12 = pl.pallas_call(
        functools.partial(crossline_kernel, two_sided),
        out_shape=(
            jax.ShapeDtypeStruct((3, 256, 256), F32),
            jax.ShapeDtypeStruct((16, 512, 128), BF16),
        ),
        in_specs=[vmem] * 4,
        out_specs=(vmem,) * 2,
        scratch_shapes=[
            pltpu.VMEM((16, 32, 256), BF16),
            pltpu.VMEM((5, 256, 128), F32),
            pltpu.VMEM((9, 256, 128), F32),
        ],
        compiler_params=pltpu.CompilerParams(vmem_limit_bytes=CROSS_VMEM),
        cost_estimate=pl.CostEstimate(flops=3 * 10**9, bytes_accessed=9 * 10**6, transcendentals=0),
        name="crossline",
    )(bands, w2, first12, xrows)
    attr, gram = pl.pallas_call(
        functools.partial(attributes_kernel, two_sided),
        out_shape=(
            jax.ShapeDtypeStruct((128, CHAN, 128), BF16),
            jax.ShapeDtypeStruct((CHAN, 128), F32),
        ),
        in_specs=[smem] + [vmem] * 8,
        out_specs=(vmem, vmem),
        scratch_shapes=[
            pltpu.VMEM((3, 256, 128), F32),
            pltpu.VMEM((256, 512), BF16),
            pltpu.VMEM((256, 512), BF16),
        ],
        compiler_params=pltpu.CompilerParams(vmem_limit_bytes=ATTR_VMEM),
        name="attributes",
    )(trace_live, trace_live, bands, w2, w3, first0, extra0, second12, dh)

    mine, other = summed(gram)
    out, factor = pl.pallas_call(
        whiten_kernel,
        grid=(4,),
        out_shape=(
            jax.ShapeDtypeStruct((CHAN, 8, 16, 128), BF16),
            jax.ShapeDtypeStruct((CHAN, CHAN), F32),
        ),
        in_specs=[vmem] * 3,
        out_specs=(
            pl.BlockSpec((CHAN, 2, 16, 128), lambda i: (0, i, 0, 0)),
            pl.BlockSpec((CHAN, CHAN), lambda i: (0, 0)),
        ),
        scratch_shapes=[pltpu.VMEM((CHAN, 128), F32), pltpu.VMEM((768, 768), BF16)],
        compiler_params=pltpu.CompilerParams(vmem_limit_bytes=WHITEN_VMEM),
        name="whiten",
    )(mine, other, attr)
    return out, factor


def solution(mesh):
    placed = (P(("survey", "inline"), "xline", "depth"), P(("survey", "inline"), "xline"), P())
    return jax.shard_map(
        local,
        mesh=mesh,
        in_specs=placed,
        out_specs=(P(None, ("survey", "inline"), "xline", "depth"), P("survey", None)),
        check_vma=False,
    )
```

```python
import functools
import math

import jax
import jax.numpy as jnp
from jax import lax
from jax.experimental import pallas as pl
from jax.experimental.pallas import tpu as pltpu
from jax.sharding import PartitionSpec as P

ORIENT = 32
TAPS = 5
CHAN = 96
REACH = 8
KEPT = 5
F32 = jnp.float32
BF16 = jnp.bfloat16
LIVE_VMEM = 4 * 1024 * 1024
INLINE_VMEM = 22 * 1024 * 1024
CROSS_VMEM = 16 * 1024 * 1024
ATTR_VMEM = 22 * 1024 * 1024
WHITEN_VMEM = 14 * 1024 * 1024


def iota(shape, dim):
    return lax.broadcasted_iota(jnp.int32, shape, dim)


def rounded(value):
    return value.astype(BF16).astype(F32)


def ones_where(mask):
    return jnp.where(mask, 1.0, 0.0).astype(BF16)


def dot(a, b):
    return jnp.dot(a, b, preferred_element_type=F32)


def shifted(value, axis, step):
    size = lax.axis_size(axis)
    return lax.ppermute(value, axis, [(i, i + step) for i in range(size) if 0 <= i + step < size])


def flipped(value, flips):
    axes = tuple(axis for axis, _ in flips)
    sizes = [lax.axis_size(axis) for axis in axes]
    pairs = []
    for source in range(math.prod(sizes)):
        target, rest, stride = 0, source, 1
        for size, (_, bit) in reversed(list(zip(sizes, flips))):
            target += ((rest % size) ^ bit) * stride
            rest, stride = rest // size, stride * size
        pairs.append((source, target))
    return lax.ppermute(value, axes, pairs)


def bits_of(axis):
    size = lax.axis_size(axis)
    assert size & (size - 1) == 0
    return [(axis, 2 ** i) for i in range(size.bit_length() - 1)]


def summed(value):
    x_bits, il_bits = bits_of("xline"), bits_of("inline")
    for bit in bits_of("depth") + x_bits[1:] + il_bits[2:]:
        value = value + flipped(value, [bit])
    one, two = il_bits[0], x_bits[0]
    a, b, c = flipped(value, [one]), flipped(value, [two]), flipped(value, [one, two])
    value = (value + a) + (b + c)
    return value, flipped(value, [il_bits[1]])


def halo_select(level, stored, x_left, depth_first):
    dilation = 2 ** level
    rows, cols = 256, TAPS * 128
    lane = iota((1, cols), 1)
    k = lane // 128
    within = lane % 128
    place = (within + 4) % 8 - 4
    q = ((within + 4) // 8) % 16
    j = 2 * q + dilation * (k - 2)
    slot = jnp.where(j < 0, 40 + j, j)
    if stored == 48:
        slot = jnp.where(j >= 32, j + 8, slot)
    else:
        slot = jnp.where((j < 0) & (x_left == 0), -999999, slot)
        slot = jnp.where((j >= 32) & (x_left == 1), -999999, slot)
    kept = jnp.where(place >= 0, place, place + 4)
    if level == 0:
        kept = jnp.where(place == -2, 4, kept)
    source = kept * stored + slot
    source = jnp.where((place >= 0) & (depth_first == 0), -1, source)
    source = jnp.where((place < 0) & (depth_first == 1), -1, source)
    return ones_where(iota((rows, cols), 0) == source)


def shift_matrix(shifts):
    lane = iota((1, 128 * len(shifts)), 1)
    source = lane % 128
    for i, shift in enumerate(shifts):
        source = jnp.where(lane // 128 == i, source + shift, source)
    past = (source + 128) % 128 + 128
    source = jnp.where(source < 0, past, jnp.where(source >= 128, past, source))
    return ones_where(iota((256, 128 * len(shifts)), 0) == source)


def side_flags():
    x_left = jnp.where(lax.axis_index("xline") == 1, 1, 0)
    depth_first = jnp.where(lax.axis_index("depth") == 0, 1, 0)
    return x_left, depth_first, lax.axis_index("inline") % 2


def live_kernel(trace_ref, seismic_ref, live_ref, near_ref, far_ref):
    n_il, n_xl, _ = seismic_ref.shape
    eye = iota((n_xl, n_xl), 0) == iota((n_xl, n_xl), 1)
    for p in range(n_il):
        row = jnp.broadcast_to(trace_ref[p : p + 1, :], (n_xl, n_xl))
        kept = dot(jnp.where(eye, row, 0.0).astype(BF16), seismic_ref[p])
        live_ref[p * n_xl : (p + 1) * n_xl, :] = kept.astype(BF16)
    count = REACH * n_xl
    start = (n_il - REACH) * n_xl
    odd = side_flags()[2]

    @pl.when(odd == 1)
    def _():
        near_ref[...] = live_ref[0:count]
        far_ref[...] = live_ref[start : start + count]

    @pl.when(odd == 0)
    def _():
        near_ref[...] = live_ref[start : start + count]
        far_ref[...] = live_ref[0:count]


def banded(level, taps_ref, bands, il_odd):
    lane = iota((ORIENT, 128), 1)
    cs = slice(level * ORIENT, (level + 1) * ORIENT)
    cols = [jnp.broadcast_to(taps_ref[0, cs, k : k + 1], (ORIENT, 128)) for k in range(TAPS)]
    for o in range(8):
        total = jnp.zeros((ORIENT, 128), F32)
        for k in range(TAPS):
            p = 2 * o + 2 ** level * (k - 2)
            if p < 0:
                place = p + 32 - 8 * il_odd
            elif p >= 16:
                place = p + 8 * il_odd
            else:
                place = p
            total = jnp.where(lane == place, cols[k], total)
        bands[pl.ds(level * 256 + o * ORIENT, ORIENT), :] = total.astype(BF16)


def phase_pick():
    n = iota((256, 256), 1)
    return ones_where(iota((256, 256), 0) == jnp.where(n < 128, 2 * n, 2 * n - 255))


def inline_kernel(
    taps_ref, own_ref, near_ref, far_ref, bands, w2, w3, first0, first12, edge_ref, planes
):
    _, depth_first, il_odd = side_flags()

    def put_edge(ts):
        for at, ref in ((0, own_ref), (512, near_ref), (768, far_ref)):
            edge_ref[at : at + ref.shape[0], :] = ref[:, ts]

    pl.when(depth_first == 1)(lambda: put_edge(slice(128, 256)))
    pl.when(depth_first == 0)(lambda: put_edge(slice(0, 128)))
    for k in range(TAPS):
        w2[k] = jnp.broadcast_to(taps_ref[1, :, k : k + 1], (CHAN, 128))
        w3[k] = jnp.broadcast_to(taps_ref[2, :, k : k + 1], (CHAN, 128))
    for level in range(3):
        banded(level, taps_ref, bands, il_odd)

    pick = phase_pick()
    r = iota((512, 512), 0)
    c = iota((512, 512), 1)
    turn = ones_where((c // 16 == r % 32) & (c % 16 == r // 32))
    own = dot(own_ref[...], pick).astype(BF16).reshape(16, 32, 256)
    near = dot(near_ref[...], pick).astype(BF16).reshape(8, 32, 256)
    far = dot(far_ref[...], pick).astype(BF16).reshape(8, 32, 256)
    for half in range(2):
        js = slice(half * 16, half * 16 + 16)
        block = jnp.concatenate([own[:, js], near[:, js], far[:, js]], axis=0).reshape(512, 256)
        planes[half * 16 : half * 16 + 16] = dot(turn, block).astype(BF16).reshape(16, 32, 256)

    a0 = bands[0:256, 0:32]
    a12 = bands[256:768, 0:32]
    def level0_first(j, _):
        first0[j] = rounded(dot(a0, planes[j]))
        return 0

    lax.fori_loop(0, 32, level0_first, 0, unroll=8)

    def even_first(pair, _):
        both = jnp.concatenate([planes[4 * pair, :, 0:128], planes[4 * pair + 2, :, 0:128]], axis=1)
        out = rounded(dot(a12, both))
        first12[2 * pair] = out[:, 0:128]
        first12[2 * pair + 1] = out[:, 128:256]
        return 0

    lax.fori_loop(0, 8, even_first, 0, unroll=4)


def tall(ref, level, k):
    return jnp.concatenate([ref[k, level * ORIENT : (level + 1) * ORIENT]] * 8, axis=0)


def crossline_kernel(
    two_sided, bands, w2, first12, xh_ref, edge0, second12, edges, edge12
):
    x_left = side_flags()[0]

    r = iota((512, 512), 0)
    c = iota((512, 512), 1)
    turn_x = ones_where((c % 256 // 8 == r % 32) & (c // 256 * 8 + c % 8 == r // 32))
    got = dot(xh_ref[...], phase_pick())
    if not two_sided:
        left = jnp.where(x_left == 1, 1.0, 0.0)
        got = jnp.concatenate([got * left, got * (1.0 - left)], axis=0)
    edges[...] = dot(turn_x, got.astype(BF16)).astype(BF16).reshape(16, 32, 256)
    a0 = bands[0:256, 0:32]
    a12 = bands[256:768, 0:32]
    for i, slot in enumerate((6, 7, 8)):
        edge0[i] = rounded(dot(a0, edges[slot]))
    for i in range(4):
        both = jnp.concatenate([edges[4 * i, :, 0:128], edges[4 * i + 2, :, 0:128]], axis=1)
        out = rounded(dot(a12, both))
        edge12[2 * i], edge12[2 * i + 1] = out[:, 0:128], out[:, 128:256]

    def filtered(level, q, plane):
        for c16 in range(2):
            start = level * ORIENT + c16 * 16
            s2 = [w2[k, start : start + 16] for k in range(TAPS)]
            for o in range(8):
                row = (level - 1) * 256 + o * ORIENT + c16 * 16
                here = slice(row, row + 16)
                total = sum(s2[k] * plane(q + level * (k - 2), here) for k in range(TAPS))
                second12[q, here, :] = total.astype(BF16)

    def own_plane(e, here):
        return first12[e, here, :]

    def any_plane(e, here):
        if 0 <= e < 16:
            return first12[e, here, :]
        return edge12[e + 4 if e < 0 else e - 12, here, :]

    for level in (1, 2):
        reach = 2 * level

        def inner(q, _, level=level):
            filtered(level, q, own_plane)
            return 0

        lax.fori_loop(reach, 16 - reach, inner, 0)
        for i in range(reach):
            filtered(level, i, any_plane)
            filtered(level, 15 - i, any_plane)


def attributes_kernel(
    two_sided, live_smem, live_ref, bands, w2, w3, first0, edge0, second12, dh_ref,
    attr_ref, gram_ref, halo2, moves1, moves2,
):
    x_left, depth_first, _ = side_flags()
    stored = 48 if two_sided else 40

    n = iota((1, 256), 1)
    kept = n // stored
    sample = 2 * kept - jnp.where(kept == 4, 1, 0) + jnp.where(depth_first == 1, 0, 120)
    sample = jnp.where(kept < KEPT, sample, -1)
    spread = ones_where(iota((128, 256), 0) == sample)
    rows = 32 * stored
    wide = dot(dh_ref[...].reshape(rows, 128), spread)
    wide = jnp.where(iota((rows, 256), 0) % stored == n % stored, wide, 0.0).astype(BF16)
    gather = ones_where(iota((32, rows), 1) // stored == iota((32, rows), 0))
    lanes = dot(gather, wide).astype(BF16)
    for level in range(3):
        cols = dot(lanes, halo_select(level, stored, x_left, depth_first)).astype(BF16)
        part = rounded(dot(bands[level * 256 : level * 256 + 256, 0:32], cols))
        total = jnp.zeros((256, 128), F32)
        for k in range(TAPS):
            total = total + part[:, k * 128 : k * 128 + 128] * tall(w2, level, k)
        total = rounded(total)
        if level == 0:
            w3_0, w3_1, w3_4 = [tall(w3, 0, k) for k in (0, 1, 4)]
            before_first = total * w3_0 + pltpu.roll(total, 1, 1) * w3_1
            total = jnp.where(iota((256, 128), 1) % 8 == 7, before_first, total * w3_4)
        halo2[level] = total

    moves1[...] = shift_matrix((-2, -1, 1, 2))
    moves2[...] = shift_matrix((-4, -2, 2, 4))

    def one_q(q, plane):
        align = (128 - 8 * q) % 128
        live_q = [live_smem[2 * o, 2 * q].astype(F32) for o in range(8)]
        lane = iota((16, 128), 1)

        def put(o, start, total):
            at = start % ORIENT
            attr_ref[2 * o + q // 8, start // ORIENT, q % 8, at : at + 16, :] = (total * live_q[o]).astype(BF16)

        for level in (1, 2):
            halo = pltpu.roll(halo2[level], align, 1).astype(BF16)
            value = second12[q, (level - 1) * 256 : level * 256, :]
            moved = dot(jnp.concatenate([value, halo], axis=1), (moves1 if level == 1 else moves2)[...])
            for c16 in range(2):
                start = level * ORIENT + c16 * 16
                s3 = [w3[k, start : start + 16] for k in range(TAPS)]
                for o in range(8):
                    rows = slice(o * ORIENT + c16 * 16, o * ORIENT + c16 * 16 + 16)
                    total = s3[2] * value[rows].astype(F32)
                    for i, k in enumerate((0, 1, 3, 4)):
                        total = total + s3[k] * moved[rows, i * 128 : i * 128 + 128]
                    put(o, start, total)
        for c16 in range(2):
            s2 = [w2[k, c16 * 16 : c16 * 16 + 16] for k in range(TAPS)]
            s3 = [w3[k, c16 * 16 : c16 * 16 + 16] for k in range(TAPS)]
            for o in range(8):
                rows = slice(o * ORIENT + c16 * 16, o * ORIENT + c16 * 16 + 16)
                both = []
                for ts in (slice(0, 128), slice(128, 256)):
                    total = sum(s2[k] * plane(2 * q + k - 2, rows, ts) for k in range(TAPS))
                    both.append(rounded(total))
                even, odd = both
                halo = pltpu.roll(halo2[0, rows], align, 1)
                back = jnp.where(lane == 127, halo, s3[0] * even + s3[1] * odd)
                ahead = jnp.where(lane == 0, halo, s3[4] * even)
                moved = pltpu.roll(back, 1, 1) + pltpu.roll(ahead, 127, 1)
                put(o, c16 * 16, s3[2] * even + s3[3] * odd + moved)

    def add_gram(q, total):
        for o in range(0, 8, 2):
            both = jnp.concatenate(
                [
                    jnp.concatenate([attr_ref[2 * i + q // 8, level, q % 8] for level in range(3)], axis=0)
                    for i in (o, o + 1)
                ],
                axis=1,
            )
            total = total + lax.dot_general(
                both, both, (((1,), (1,)), ((), ())), preferred_element_type=F32
            )
        return total

    def own_plane(j, rows, ts):
        return first0[j, rows, ts]

    def any_plane(j, rows, ts):
        if 0 <= j < 32:
            return first0[j, rows, ts]
        return edge0[j + 2 if j < 0 else 2, rows, ts]

    def next_q(q, total):
        total = add_gram(q - 1, total)
        one_q(q, own_plane)
        return total

    one_q(0, any_plane)
    gram = lax.fori_loop(1, 15, next_q, jnp.zeros((CHAN, CHAN), F32))
    gram = add_gram(14, gram)
    one_q(15, any_plane)
    gram = add_gram(15, gram)
    alive = live_ref[...]
    chosen = (iota(alive.shape, 0) % 2 == 0) & (iota(alive.shape, 1) % 2 == 0)
    count = jnp.sum(jnp.where(chosen, alive.astype(F32), 0.0)) * 128.0
    gram_ref[...] = jnp.full((CHAN, 128), count, F32)
    gram_ref[:, 0:CHAN] = gram


def whiten_kernel(mine_ref, other_ref, attr_ref, out_hbm, factor_ref, inverse, kron, out_ref, sems):
    total = mine_ref[...] + other_ref[...]
    lane = iota((8, 128), 1)
    sub = iota((8, 128), 0)
    count = jnp.broadcast_to(total[0:1, CHAN : CHAN + 1], (8, 128))
    blocks = []
    for g in range(CHAN // 8):
        blocks.append(jnp.where(lane < CHAN, total[8 * g : 8 * g + 8] / count, 0.0))

    n = iota((CHAN, 768), 1)
    spread = ones_where(iota((CHAN, 768), 0) == n // 256 * ORIENT + n % ORIENT)
    tall = ones_where(iota((256, ORIENT), 0) // 8 == iota((256, ORIENT), 1))

    def spread_inverse(level):
        depth = 256 * (level + 1)
        low = inverse[level * ORIENT : (level + 1) * ORIENT, 0:CHAN].astype(BF16)
        full = dot(tall, dot(low, spread[:, 0:depth]).astype(BF16))
        keep = iota((256, depth), 0) % 8 == iota((256, depth), 1) // ORIENT % 8
        kron[level, :, 0:depth] = jnp.where(keep, full, 0.0).astype(BF16)

    def sent(level):
        cs = slice(level * ORIENT, (level + 1) * ORIENT)
        return pltpu.make_async_copy(out_ref.at[cs], out_hbm.at[cs], sems.at[level])

    def whiten_pair(level, pair):
        depth = 256 * (level + 1)
        halves = []
        for half in range(2):
            rows = [
                attr_ref[2 * (2 * pair + i) + half, 0 : level + 1].reshape(depth, 128) for i in range(2)
            ]
            halves.append(dot(kron[level, :, 0:depth], jnp.concatenate(rows, axis=1)))
        for i in range(2):
            both = [half[:, i * 128 : i * 128 + 128].reshape(ORIENT, 8, 128) for half in halves]
            out_ref[level * ORIENT : (level + 1) * ORIENT, 2 * pair + i] = jnp.concatenate(
                both, axis=1
            ).astype(BF16)
        if pair == 3:
            sent(level).start()

    row_lane = iota((1, 128), 1)

    def finish(j, row, inv_row, pivot):
        scale = lax.rsqrt(pivot)
        factor_ref[j : j + 1, :] = (jnp.where(row_lane >= j, row, 0.0) * scale)[:, 0:CHAN]
        inverse[j : j + 1, :] = jnp.where(row_lane <= j, inv_row, 0.0) * scale

    def spread_lane(block, j):
        return jnp.broadcast_to(block[:, j : j + 1], (8, 128))

    def spread_row(block, i):
        return jnp.broadcast_to(block[i : i + 1, :], (8, 128))

    for j in range(0, CHAN, 4):
        g, s = j // 8, j % 8
        top = blocks[g]
        cols = [spread_lane(top, j + i) for i in range(4)]
        rows = [spread_row(top, s + i) for i in range(4)]
        d = [[spread_row(cols[min(m, i)], s + max(m, i)) for i in range(4)] for m in range(4)]
        p_inv = 1.0 / (d[0][0] * d[1][1] - d[0][1] * d[0][1])
        adj = [[d[1][1], -d[0][1]], [-d[0][1], d[0][0]]]
        h = [
            [(d[2 + m][0] * adj[0][i] + d[2 + m][1] * adj[1][i]) * p_inv for i in range(2)]
            for m in range(2)
        ]
        t = [
            [d[2 + m][2 + i] - (h[m][0] * d[0][2 + i] + h[m][1] * d[1][2 + i]) for i in range(2)]
            for m in range(2)
        ]
        t01 = t[1][0]
        t_inv = 1.0 / (t[0][0] * t[1][1] - t01 * t01)
        unit = []
        for i in range(4):
            value = rows[i]
            for m in range(4):
                value = jnp.where(lane == j + m, 1.0 if m == i else 0.0, value)
            unit.append(value)
        below = [unit[2 + m] - (h[m][0] * unit[0] + h[m][1] * unit[1]) for m in range(2)]
        up2 = (t[1][1] * below[0] - t01 * below[1]) * t_inv
        up3 = (t[0][0] * below[1] - t01 * below[0]) * t_inv
        inner = [unit[0] * d[1][1] - unit[1] * d[0][1], unit[1] * d[0][0] - unit[0] * d[0][1]]
        up0 = inner[0] * p_inv - (h[0][0] * up2 + h[1][0] * up3)
        up1 = inner[1] * p_inv - (h[0][1] * up2 + h[1][1] * up3)
        ups = (up0, up1, up2, up3)
        ratio0 = d[0][1] / d[0][0]
        ratio1 = t01 / t[0][0]
        mix0 = rows[2] - (h[0][0] * rows[0] + h[0][1] * rows[1])
        mix1 = rows[3] - (h[1][0] * rows[0] + h[1][1] * rows[1])
        solved = [rows[0], rows[1] - ratio0 * rows[0], mix0, mix1 - ratio1 * mix0]
        inv_solved = [unit[0], unit[1] - ratio0 * unit[0], below[0], below[1] - ratio1 * below[0]]
        pivots = [d[0][0], d[1][1] - d[0][1] * ratio0, t[0][0], t[1][1] - t01 * ratio1]
        for i in range(4):
            finish(j + i, solved[i][0:1], inv_solved[i][0:1], pivots[i][0:1])
        if j % ORIENT == ORIENT - 4:
            spread_inverse(j // ORIENT)
        if j >= ORIENT and j % 8 == 4:
            whiten_pair(j // ORIENT - 1, j % ORIENT // 8)
        if j == CHAN - 4:
            break
        inside = (lane >= j) & (lane < j + 4)
        for k in range(g, CHAN // 8):
            if k > g:
                cols = [spread_lane(blocks[k], j + i) for i in range(4)]
            else:
                if s == 4:
                    continue
                cols = [jnp.where(sub > s + 3, col, 0.0) for col in cols]
            change = (cols[0] * ups[0] + cols[1] * ups[1]) + (cols[2] * ups[2] + cols[3] * ups[3])
            blocks[k] = jnp.where(inside, 0.0, blocks[k]) - change

    for pair in range(4):
        whiten_pair(2, pair)
    for level in range(3):
        sent(level).wait()


def local(seismic, trace_live, filter_taps):
    il_len, xl_len, t_len = seismic.shape
    assert (il_len, xl_len, t_len) == (16, 32, 256) and lax.axis_size("depth") == 2
    taps = filter_taps.astype(F32)
    x_index = lax.axis_index("xline")
    d_index = lax.axis_index("depth")
    two_sided = lax.axis_size("xline") > 2
    vmem = pl.BlockSpec(memory_space=pltpu.VMEM)
    smem = pl.BlockSpec(memory_space=pltpu.SMEM)

    live, near, far = pl.pallas_call(
        live_kernel,
        out_shape=(
            jax.ShapeDtypeStruct((il_len * xl_len, t_len), BF16),
            jax.ShapeDtypeStruct((REACH * xl_len, t_len), BF16),
            jax.ShapeDtypeStruct((REACH * xl_len, t_len), BF16),
        ),
        in_specs=[vmem] * 2,
        out_specs=(vmem,) * 3,
        compiler_params=pltpu.CompilerParams(vmem_limit_bytes=LIVE_VMEM),
        name="live",
    )(trace_live.astype(F32), seismic)
    il_size = lax.axis_size("inline")
    near_pairs = [(i, i ^ 1) for i in range(il_size) if i ^ 1 < il_size]
    far_pairs = [(i, i - 1 if i % 2 == 0 else i + 1) for i in range(1, il_size)]
    far_pairs = [(i, j) for i, j in far_pairs if j < il_size]
    near = lax.ppermute(near, "inline", near_pairs)
    far = lax.ppermute(far, "inline", far_pairs)
    parts = [v.reshape(-1, xl_len, t_len) for v in (live, near, far)]

    def stack(js):
        return jnp.concatenate([v[:, js] for v in parts], axis=0)

    low, high = slice(0, REACH), slice(xl_len - REACH, xl_len)
    if two_sided:
        xh = [shifted(stack(high), "xline", 1), shifted(stack(low), "xline", -1)]
    else:
        xh = [flipped(jnp.where(x_index == 0, stack(high), stack(low)), [("xline", 1)])]
    bands, w2, w3, first0, first12, edge = pl.pallas_call(
        inline_kernel,
        out_shape=(
            jax.ShapeDtypeStruct((3 * 256, 128), BF16),
            jax.ShapeDtypeStruct((TAPS, CHAN, 128), F32),
            jax.ShapeDtypeStruct((TAPS, CHAN, 128), F32),
            jax.ShapeDtypeStruct((xl_len, 256, 256), F32),
            jax.ShapeDtypeStruct((xl_len // 2, 512, 128), F32),
            jax.ShapeDtypeStruct((32 * xl_len, 128), BF16),
        ),
        in_specs=[vmem] * 4,
        out_specs=(vmem,) * 6,
        scratch_shapes=[pltpu.VMEM((32, 32, 256), BF16)],
        compiler_params=pltpu.CompilerParams(vmem_limit_bytes=INLINE_VMEM),
        cost_estimate=pl.CostEstimate(flops=4 * 10**9, bytes_accessed=16 * 10**6, transcendentals=0),
        name="inline",
    )(taps, live, near, far)

    def side(x):
        return jnp.where(d_index == 0, x[:, :, t_len - 128 :], x[:, :, :128])

    dh = jnp.concatenate([edge.reshape(32, xl_len, 128)] + [side(x) for x in xh], axis=1)
    dh = flipped(dh, [("depth", 1)])
    xrows = jnp.concatenate([x.reshape(256, t_len) for x in xh], axis=0)
    edge0, second12 = pl.pallas_call(
        functools.partial(crossline_kernel, two_sided),
        out_shape=(
            jax.ShapeDtypeStruct((3, 256, 256), F32),
            jax.ShapeDtypeStruct((16, 512, 128), BF16),
        ),
        in_specs=[vmem] * 4,
        out_specs=(vmem,) * 2,
        scratch_shapes=[
            pltpu.VMEM((16, 32, 256), BF16),
            pltpu.VMEM((8, 512, 128), F32),
        ],
        compiler_params=pltpu.CompilerParams(vmem_limit_bytes=CROSS_VMEM),
        cost_estimate=pl.CostEstimate(flops=3 * 10**9, bytes_accessed=9 * 10**6, transcendentals=0),
        name="crossline",
    )(bands, w2, first12, xrows)
    attr, gram = pl.pallas_call(
        functools.partial(attributes_kernel, two_sided),
        out_shape=(
            jax.ShapeDtypeStruct((16, 3, 8, ORIENT, 128), BF16),
            jax.ShapeDtypeStruct((CHAN, 128), F32),
        ),
        in_specs=[smem] + [vmem] * 8,
        out_specs=(vmem, vmem),
        scratch_shapes=[
            pltpu.VMEM((3, 256, 128), F32),
            pltpu.VMEM((256, 512), BF16),
            pltpu.VMEM((256, 512), BF16),
        ],
        compiler_params=pltpu.CompilerParams(vmem_limit_bytes=ATTR_VMEM),
        name="attributes",
    )(trace_live, trace_live, bands, w2, w3, first0, edge0, second12, dh)

    mine, other = summed(gram)
    out, factor = pl.pallas_call(
        whiten_kernel,
        out_shape=(
            jax.ShapeDtypeStruct((CHAN, 8, 16, 128), BF16),
            jax.ShapeDtypeStruct((CHAN, CHAN), F32),
        ),
        in_specs=[vmem] * 3,
        out_specs=(pl.BlockSpec(memory_space=pl.ANY), vmem),
        scratch_shapes=[
            pltpu.VMEM((CHAN, 128), F32),
            pltpu.VMEM((3, 256, 768), BF16),
            pltpu.VMEM((CHAN, 8, 16, 128), BF16),
            pltpu.SemaphoreType.DMA((3,)),
        ],
        compiler_params=pltpu.CompilerParams(vmem_limit_bytes=WHITEN_VMEM),
        name="whiten",
    )(mine, other, attr)
    return out, factor


def solution(mesh):
    placed = (P(("survey", "inline"), "xline", "depth"), P(("survey", "inline"), "xline"), P())
    return jax.shard_map(
        local,
        mesh=mesh,
        in_specs=placed,
        out_specs=(P(None, ("survey", "inline"), "xline", "depth"), P("survey", None)),
        check_vma=False,
    )
```

```python
import functools
import math

import jax
import jax.numpy as jnp
from jax import lax
from jax.experimental import pallas as pl
from jax.experimental.pallas import tpu as pltpu
from jax.sharding import PartitionSpec as P

ORIENT = 32
TAPS = 5
CHAN = 96
REACH = 8
KEPT = 5
F32 = jnp.float32
BF16 = jnp.bfloat16
LIVE_VMEM = 4 * 1024 * 1024
PREPARE_VMEM = 8 * 1024 * 1024
INLINE_VMEM = 22 * 1024 * 1024
CROSS_VMEM = 16 * 1024 * 1024
ATTR_VMEM = 22 * 1024 * 1024
WHITEN_VMEM = 14 * 1024 * 1024


def iota(shape, dim):
    return lax.broadcasted_iota(jnp.int32, shape, dim)


def rounded(value):
    return value.astype(BF16).astype(F32)


def ones_where(mask):
    return jnp.where(mask, 1.0, 0.0).astype(BF16)


def dot(a, b):
    return jnp.dot(a, b, preferred_element_type=F32)


def shifted(value, axis, step):
    size = lax.axis_size(axis)
    return lax.ppermute(value, axis, [(i, i + step) for i in range(size) if 0 <= i + step < size])


def flipped(value, flips):
    axes = tuple(axis for axis, _ in flips)
    sizes = [lax.axis_size(axis) for axis in axes]
    pairs = []
    for source in range(math.prod(sizes)):
        target, rest, stride = 0, source, 1
        for size, (_, bit) in reversed(list(zip(sizes, flips))):
            target += ((rest % size) ^ bit) * stride
            rest, stride = rest // size, stride * size
        pairs.append((source, target))
    return lax.ppermute(value, axes, pairs)


def bits_of(axis):
    size = lax.axis_size(axis)
    assert size & (size - 1) == 0
    return [(axis, 2 ** i) for i in range(size.bit_length() - 1)]


def summed(value):
    x_bits, il_bits = bits_of("xline"), bits_of("inline")
    for bit in bits_of("depth") + x_bits[1:] + il_bits[2:]:
        value = value + flipped(value, [bit])
    one, two = il_bits[0], x_bits[0]
    a, b, c = flipped(value, [one]), flipped(value, [two]), flipped(value, [one, two])
    value = (value + a) + (b + c)
    return value, flipped(value, [il_bits[1]])


def halo_select(level, stored, x_left, depth_first):
    dilation = 2 ** level
    rows, cols = 256, TAPS * 128
    lane = iota((1, cols), 1)
    k = lane // 128
    within = lane % 128
    place = (within + 4) % 8 - 4
    q = ((within + 4) // 8) % 16
    j = 2 * q + dilation * (k - 2)
    slot = jnp.where(j < 0, 40 + j, j)
    if stored == 48:
        slot = jnp.where(j >= 32, j + 8, slot)
    else:
        slot = jnp.where((j < 0) & (x_left == 0), -999999, slot)
        slot = jnp.where((j >= 32) & (x_left == 1), -999999, slot)
    kept = jnp.where(place >= 0, place, place + 4)
    if level == 0:
        kept = jnp.where(place == -2, 4, kept)
    source = kept * stored + slot
    source = jnp.where((place >= 0) & (depth_first == 0), -1, source)
    source = jnp.where((place < 0) & (depth_first == 1), -1, source)
    return ones_where(iota((rows, cols), 0) == source)


def shift_matrix(shifts):
    lane = iota((1, 128 * len(shifts)), 1)
    source = lane % 128
    for i, shift in enumerate(shifts):
        source = jnp.where(lane // 128 == i, source + shift, source)
    past = (source + 128) % 128 + 128
    source = jnp.where(source < 0, past, jnp.where(source >= 128, past, source))
    return ones_where(iota((256, 128 * len(shifts)), 0) == source)


def side_flags():
    x_left = jnp.where(lax.axis_index("xline") == 1, 1, 0)
    depth_first = jnp.where(lax.axis_index("depth") == 0, 1, 0)
    return x_left, depth_first, lax.axis_index("inline") % 2


def live_kernel(trace_ref, seismic_ref, live_ref, near_ref, far_ref):
    n_il, n_xl, _ = seismic_ref.shape
    eye = iota((n_xl, n_xl), 0) == iota((n_xl, n_xl), 1)
    for p in range(n_il):
        row = jnp.broadcast_to(trace_ref[p : p + 1, :], (n_xl, n_xl))
        kept = dot(jnp.where(eye, row, 0.0).astype(BF16), seismic_ref[p])
        live_ref[p * n_xl : (p + 1) * n_xl, :] = kept.astype(BF16)
    count = REACH * n_xl
    start = (n_il - REACH) * n_xl
    odd = side_flags()[2]

    @pl.when(odd == 1)
    def _():
        near_ref[...] = live_ref[0:count]
        far_ref[...] = live_ref[start : start + count]

    @pl.when(odd == 0)
    def _():
        near_ref[...] = live_ref[start : start + count]
        far_ref[...] = live_ref[0:count]


def banded(level, taps_ref, bands, il_odd):
    lane = iota((ORIENT, 128), 1)
    cs = slice(level * ORIENT, (level + 1) * ORIENT)
    cols = [jnp.broadcast_to(taps_ref[0, cs, k : k + 1], (ORIENT, 128)) for k in range(TAPS)]
    for o in range(8):
        total = jnp.zeros((ORIENT, 128), F32)
        for k in range(TAPS):
            p = 2 * o + 2 ** level * (k - 2)
            if p < 0:
                place = p + 32 - 8 * il_odd
            elif p >= 16:
                place = p + 8 * il_odd
            else:
                place = p
            total = jnp.where(lane == place, cols[k], total)
        bands[pl.ds(level * 256 + o * ORIENT, ORIENT), :] = total.astype(BF16)


def phase_pick():
    n = iota((256, 256), 1)
    return ones_where(iota((256, 256), 0) == jnp.where(n < 128, 2 * n, 2 * n - 255))


def prepare_kernel(
    stored, taps_ref, own_ref, bands, w2, w3, pick, turn, turn_x, own_out, moves1, moves2, select, gather
):
    x_left, depth_first, il_odd = side_flags()
    for k in range(TAPS):
        w2[k] = jnp.broadcast_to(taps_ref[1, :, k : k + 1], (CHAN, 128))
        w3[k] = jnp.broadcast_to(taps_ref[2, :, k : k + 1], (CHAN, 128))
    for level in range(3):
        banded(level, taps_ref, bands, il_odd)
        select[level] = halo_select(level, stored, x_left, depth_first)
    pick[...] = phase_pick()
    own_out[...] = dot(own_ref[...], pick[...]).astype(BF16)
    r = iota((512, 512), 0)
    c = iota((512, 512), 1)
    turn[...] = ones_where(c == r % 32 * 16 + r // 32)
    turn_x[...] = ones_where(c == r // 256 * 256 + r % 32 * 8 + r // 32 % 8)
    moves1[...] = shift_matrix((-2, -1, 1, 2))
    moves2[...] = shift_matrix((-4, -2, 2, 4))
    rows = 32 * stored
    gather[...] = ones_where(iota((32, rows), 1) // stored == iota((32, rows), 0))


def inline_kernel(
    bands, pick, turn, own_ref, own_phases, near_ref, far_ref, first0, first12, edge_ref, planes
):
    depth_first = side_flags()[1]

    def put_edge(ts):
        for at, ref in ((0, own_ref), (512, near_ref), (768, far_ref)):
            edge_ref[at : at + ref.shape[0], :] = ref[:, ts]

    pl.when(depth_first == 1)(lambda: put_edge(slice(128, 256)))
    pl.when(depth_first == 0)(lambda: put_edge(slice(0, 128)))

    own = own_phases[...].reshape(16, 32, 256)
    near = dot(near_ref[...], pick[...]).astype(BF16).reshape(8, 32, 256)
    far = dot(far_ref[...], pick[...]).astype(BF16).reshape(8, 32, 256)
    for half in range(2):
        js = slice(half * 16, half * 16 + 16)
        block = jnp.concatenate([own[:, js], near[:, js], far[:, js]], axis=0).reshape(512, 256)
        planes[half * 16 : half * 16 + 16] = dot(turn[...], block).astype(BF16).reshape(16, 32, 256)

    a0 = bands[0:256, 0:32]
    a12 = bands[256:768, 0:32]
    def level0_first(j, _):
        first0[j] = rounded(dot(a0, planes[j]))
        return 0

    lax.fori_loop(0, 32, level0_first, 0, unroll=8)

    def even_first(pair, _):
        both = jnp.concatenate([planes[4 * pair, :, 0:128], planes[4 * pair + 2, :, 0:128]], axis=1)
        out = rounded(dot(a12, both))
        first12[2 * pair] = out[:, 0:128]
        first12[2 * pair + 1] = out[:, 128:256]
        return 0

    lax.fori_loop(0, 8, even_first, 0, unroll=4)


def tall(ref, level, k):
    return jnp.concatenate([ref[k, level * ORIENT : (level + 1) * ORIENT]] * 8, axis=0)


def crossline_kernel(
    two_sided, bands, w2, pick, turn_x, first12, xh_ref, edge0, second12, edges, edge12
):
    x_left = side_flags()[0]

    got = dot(xh_ref[...], pick[...])
    if not two_sided:
        left = jnp.where(x_left == 1, 1.0, 0.0)
        got = jnp.concatenate([got * left, got * (1.0 - left)], axis=0)
    edges[...] = dot(turn_x[...], got.astype(BF16)).astype(BF16).reshape(16, 32, 256)
    a0 = bands[0:256, 0:32]
    a12 = bands[256:768, 0:32]
    for i, slot in enumerate((6, 7, 8)):
        edge0[i] = rounded(dot(a0, edges[slot]))
    for i in range(4):
        both = jnp.concatenate([edges[4 * i, :, 0:128], edges[4 * i + 2, :, 0:128]], axis=1)
        out = rounded(dot(a12, both))
        edge12[2 * i], edge12[2 * i + 1] = out[:, 0:128], out[:, 128:256]

    def filtered(level, q, plane):
        for c16 in range(2):
            start = level * ORIENT + c16 * 16
            s2 = [w2[k, start : start + 16] for k in range(TAPS)]
            for o in range(8):
                row = (level - 1) * 256 + o * ORIENT + c16 * 16
                here = slice(row, row + 16)
                total = sum(s2[k] * plane(q + level * (k - 2), here) for k in range(TAPS))
                second12[q, here, :] = total.astype(BF16)

    def own_plane(e, here):
        return first12[e, here, :]

    def any_plane(e, here):
        if 0 <= e < 16:
            return first12[e, here, :]
        return edge12[e + 4 if e < 0 else e - 12, here, :]

    for level in (1, 2):
        reach = 2 * level

        def inner(q, _, level=level):
            filtered(level, q, own_plane)
            return 0

        lax.fori_loop(reach, 16 - reach, inner, 0)
        for i in range(reach):
            filtered(level, i, any_plane)
            filtered(level, 15 - i, any_plane)


def attributes_kernel(
    two_sided, live_smem, live_ref, bands, w2, w3, moves1, moves2, select, gather, first0, edge0,
    second12, dh_ref, attr_ref, gram_ref, halo2,
):
    depth_first = side_flags()[1]
    stored = 48 if two_sided else 40

    n = iota((1, 256), 1)
    kept = n // stored
    sample = 2 * kept - jnp.where(kept == 4, 1, 0) + jnp.where(depth_first == 1, 0, 120)
    sample = jnp.where(kept < KEPT, sample, -1)
    spread = ones_where(iota((128, 256), 0) == sample)
    rows = 32 * stored
    wide = dot(dh_ref[...].reshape(rows, 128), spread)
    wide = jnp.where(iota((rows, 256), 0) % stored == n % stored, wide, 0.0).astype(BF16)
    lanes = dot(gather[...], wide).astype(BF16)
    for level in range(3):
        cols = dot(lanes, select[level]).astype(BF16)
        part = rounded(dot(bands[level * 256 : level * 256 + 256, 0:32], cols))
        total = jnp.zeros((256, 128), F32)
        for k in range(TAPS):
            total = total + part[:, k * 128 : k * 128 + 128] * tall(w2, level, k)
        total = rounded(total)
        if level == 0:
            w3_0, w3_1, w3_4 = [tall(w3, 0, k) for k in (0, 1, 4)]
            before_first = total * w3_0 + pltpu.roll(total, 1, 1) * w3_1
            total = jnp.where(iota((256, 128), 1) % 8 == 7, before_first, total * w3_4)
        halo2[level] = total


    def one_q(q, plane):
        align = (128 - 8 * q) % 128
        live_q = [live_smem[2 * o, 2 * q].astype(F32) for o in range(8)]
        lane = iota((16, 128), 1)

        def put(o, start, total):
            at = start % ORIENT
            attr_ref[2 * o + q // 8, start // ORIENT, q % 8, at : at + 16, :] = (total * live_q[o]).astype(BF16)

        for level in (1, 2):
            halo = pltpu.roll(halo2[level], align, 1).astype(BF16)
            value = second12[q, (level - 1) * 256 : level * 256, :]
            moved = dot(jnp.concatenate([value, halo], axis=1), (moves1 if level == 1 else moves2)[...])
            for c16 in range(2):
                start = level * ORIENT + c16 * 16
                s3 = [w3[k, start : start + 16] for k in range(TAPS)]
                for o in range(8):
                    rows = slice(o * ORIENT + c16 * 16, o * ORIENT + c16 * 16 + 16)
                    total = s3[2] * value[rows].astype(F32)
                    for i, k in enumerate((0, 1, 3, 4)):
                        total = total + s3[k] * moved[rows, i * 128 : i * 128 + 128]
                    put(o, start, total)
        for c16 in range(2):
            s2 = [w2[k, c16 * 16 : c16 * 16 + 16] for k in range(TAPS)]
            s3 = [w3[k, c16 * 16 : c16 * 16 + 16] for k in range(TAPS)]
            for o in range(8):
                rows = slice(o * ORIENT + c16 * 16, o * ORIENT + c16 * 16 + 16)
                both = []
                for ts in (slice(0, 128), slice(128, 256)):
                    total = sum(s2[k] * plane(2 * q + k - 2, rows, ts) for k in range(TAPS))
                    both.append(rounded(total))
                even, odd = both
                halo = pltpu.roll(halo2[0, rows], align, 1)
                back = jnp.where(lane == 127, halo, s3[0] * even + s3[1] * odd)
                ahead = jnp.where(lane == 0, halo, s3[4] * even)
                moved = pltpu.roll(back, 1, 1) + pltpu.roll(ahead, 127, 1)
                put(o, c16 * 16, s3[2] * even + s3[3] * odd + moved)

    def add_gram(q, total):
        for o in range(0, 8, 2):
            both = jnp.concatenate(
                [
                    jnp.concatenate([attr_ref[2 * i + q // 8, level, q % 8] for level in range(3)], axis=0)
                    for i in (o, o + 1)
                ],
                axis=1,
            )
            total = total + lax.dot_general(
                both, both, (((1,), (1,)), ((), ())), preferred_element_type=F32
            )
        return total

    def own_plane(j, rows, ts):
        return first0[j, rows, ts]

    def any_plane(j, rows, ts):
        if 0 <= j < 32:
            return first0[j, rows, ts]
        return edge0[j + 2 if j < 0 else 2, rows, ts]

    def next_q(q, total):
        total = add_gram(q - 1, total)
        one_q(q, own_plane)
        return total

    one_q(0, any_plane)
    gram = lax.fori_loop(1, 15, next_q, jnp.zeros((CHAN, CHAN), F32))
    gram = add_gram(14, gram)
    one_q(15, any_plane)
    gram = add_gram(15, gram)
    alive = live_ref[...]
    chosen = (iota(alive.shape, 0) % 2 == 0) & (iota(alive.shape, 1) % 2 == 0)
    count = jnp.sum(jnp.where(chosen, alive.astype(F32), 0.0)) * 128.0
    gram_ref[...] = jnp.full((CHAN, 128), count, F32)
    gram_ref[:, 0:CHAN] = gram


def whiten_kernel(mine_ref, other_ref, attr_ref, out_hbm, factor_ref, inverse, kron, out_ref, sems):
    total = mine_ref[...] + other_ref[...]
    lane = iota((8, 128), 1)
    sub = iota((8, 128), 0)
    count = jnp.broadcast_to(total[0:1, CHAN : CHAN + 1], (8, 128))
    blocks = []
    for g in range(CHAN // 8):
        blocks.append(jnp.where(lane < CHAN, total[8 * g : 8 * g + 8] / count, 0.0))

    n = iota((CHAN, 768), 1)
    spread = ones_where(iota((CHAN, 768), 0) == n // 256 * ORIENT + n % ORIENT)
    tall = ones_where(iota((256, ORIENT), 0) // 8 == iota((256, ORIENT), 1))

    def spread_inverse(level):
        depth = 256 * (level + 1)
        low = inverse[level * ORIENT : (level + 1) * ORIENT, 0:CHAN].astype(BF16)
        full = dot(tall, dot(low, spread[:, 0:depth]).astype(BF16))
        keep = iota((256, depth), 0) % 8 == iota((256, depth), 1) // ORIENT % 8
        kron[level, :, 0:depth] = jnp.where(keep, full, 0.0).astype(BF16)

    def sent(level):
        cs = slice(level * ORIENT, (level + 1) * ORIENT)
        return pltpu.make_async_copy(out_ref.at[cs], out_hbm.at[cs], sems.at[level])

    def whiten_pair(level, pair):
        depth = 256 * (level + 1)
        halves = []
        for half in range(2):
            rows = [
                attr_ref[2 * (2 * pair + i) + half, 0 : level + 1].reshape(depth, 128) for i in range(2)
            ]
            halves.append(dot(kron[level, :, 0:depth], jnp.concatenate(rows, axis=1)))
        for i in range(2):
            both = [half[:, i * 128 : i * 128 + 128].reshape(ORIENT, 8, 128) for half in halves]
            out_ref[level * ORIENT : (level + 1) * ORIENT, 2 * pair + i] = jnp.concatenate(
                both, axis=1
            ).astype(BF16)
        if pair == 3:
            sent(level).start()

    row_lane = iota((1, 128), 1)

    def finish(j, row, inv_row, pivot):
        scale = lax.rsqrt(pivot)
        factor_ref[j : j + 1, :] = (jnp.where(row_lane >= j, row, 0.0) * scale)[:, 0:CHAN]
        inverse[j : j + 1, :] = jnp.where(row_lane <= j, inv_row, 0.0) * scale

    def spread_lane(block, j):
        return jnp.broadcast_to(block[:, j : j + 1], (8, 128))

    def spread_row(block, i):
        return jnp.broadcast_to(block[i : i + 1, :], (8, 128))

    for j in range(0, CHAN, 4):
        g, s = j // 8, j % 8
        top = blocks[g]
        cols = [spread_lane(top, j + i) for i in range(4)]
        rows = [spread_row(top, s + i) for i in range(4)]
        d = [[spread_row(cols[min(m, i)], s + max(m, i)) for i in range(4)] for m in range(4)]
        p_inv = 1.0 / (d[0][0] * d[1][1] - d[0][1] * d[0][1])
        adj = [[d[1][1], -d[0][1]], [-d[0][1], d[0][0]]]
        h = [
            [(d[2 + m][0] * adj[0][i] + d[2 + m][1] * adj[1][i]) * p_inv for i in range(2)]
            for m in range(2)
        ]
        t = [
            [d[2 + m][2 + i] - (h[m][0] * d[0][2 + i] + h[m][1] * d[1][2 + i]) for i in range(2)]
            for m in range(2)
        ]
        t01 = t[1][0]
        t_inv = 1.0 / (t[0][0] * t[1][1] - t01 * t01)
        unit = []
        for i in range(4):
            value = rows[i]
            for m in range(4):
                value = jnp.where(lane == j + m, 1.0 if m == i else 0.0, value)
            unit.append(value)
        below = [unit[2 + m] - (h[m][0] * unit[0] + h[m][1] * unit[1]) for m in range(2)]
        up2 = (t[1][1] * below[0] - t01 * below[1]) * t_inv
        up3 = (t[0][0] * below[1] - t01 * below[0]) * t_inv
        inner = [unit[0] * d[1][1] - unit[1] * d[0][1], unit[1] * d[0][0] - unit[0] * d[0][1]]
        up0 = inner[0] * p_inv - (h[0][0] * up2 + h[1][0] * up3)
        up1 = inner[1] * p_inv - (h[0][1] * up2 + h[1][1] * up3)
        ups = (up0, up1, up2, up3)
        ratio0 = d[0][1] / d[0][0]
        ratio1 = t01 / t[0][0]
        mix0 = rows[2] - (h[0][0] * rows[0] + h[0][1] * rows[1])
        mix1 = rows[3] - (h[1][0] * rows[0] + h[1][1] * rows[1])
        solved = [rows[0], rows[1] - ratio0 * rows[0], mix0, mix1 - ratio1 * mix0]
        inv_solved = [unit[0], unit[1] - ratio0 * unit[0], below[0], below[1] - ratio1 * below[0]]
        pivots = [d[0][0], d[1][1] - d[0][1] * ratio0, t[0][0], t[1][1] - t01 * ratio1]
        for i in range(4):
            finish(j + i, solved[i][0:1], inv_solved[i][0:1], pivots[i][0:1])
        if j % ORIENT == ORIENT - 4:
            spread_inverse(j // ORIENT)
        if j >= ORIENT and j % 8 == 4:
            whiten_pair(j // ORIENT - 1, j % ORIENT // 8)
        if j == CHAN - 4:
            break
        inside = (lane >= j) & (lane < j + 4)
        for k in range(g, CHAN // 8):
            if k > g:
                cols = [spread_lane(blocks[k], j + i) for i in range(4)]
            else:
                if s == 4:
                    continue
                cols = [jnp.where(sub > s + 3, col, 0.0) for col in cols]
            change = (cols[0] * ups[0] + cols[1] * ups[1]) + (cols[2] * ups[2] + cols[3] * ups[3])
            blocks[k] = jnp.where(inside, 0.0, blocks[k]) - change

    for pair in range(4):
        whiten_pair(2, pair)
    for level in range(3):
        sent(level).wait()


def local(seismic, trace_live, filter_taps):
    il_len, xl_len, t_len = seismic.shape
    assert (il_len, xl_len, t_len) == (16, 32, 256) and lax.axis_size("depth") == 2
    taps = filter_taps.astype(F32)
    x_index = lax.axis_index("xline")
    d_index = lax.axis_index("depth")
    two_sided = lax.axis_size("xline") > 2
    vmem = pl.BlockSpec(memory_space=pltpu.VMEM)
    smem = pl.BlockSpec(memory_space=pltpu.SMEM)

    live, near, far = pl.pallas_call(
        live_kernel,
        out_shape=(
            jax.ShapeDtypeStruct((il_len * xl_len, t_len), BF16),
            jax.ShapeDtypeStruct((REACH * xl_len, t_len), BF16),
            jax.ShapeDtypeStruct((REACH * xl_len, t_len), BF16),
        ),
        in_specs=[vmem] * 2,
        out_specs=(vmem,) * 3,
        compiler_params=pltpu.CompilerParams(vmem_limit_bytes=LIVE_VMEM),
        name="live",
    )(trace_live.astype(F32), seismic)
    il_size = lax.axis_size("inline")
    near_pairs = [(i, i ^ 1) for i in range(il_size) if i ^ 1 < il_size]
    far_pairs = [(i, i - 1 if i % 2 == 0 else i + 1) for i in range(1, il_size)]
    far_pairs = [(i, j) for i, j in far_pairs if j < il_size]
    near = lax.ppermute(near, "inline", near_pairs)
    far = lax.ppermute(far, "inline", far_pairs)
    parts = [v.reshape(-1, xl_len, t_len) for v in (live, near, far)]
    stored = 48 if two_sided else 40
    bands, w2, w3, pick, turn, turn_x, own_phases, moves1, moves2, select, gather = pl.pallas_call(
        functools.partial(prepare_kernel, stored),
        out_shape=(
            jax.ShapeDtypeStruct((3 * 256, 128), BF16),
            jax.ShapeDtypeStruct((TAPS, CHAN, 128), F32),
            jax.ShapeDtypeStruct((TAPS, CHAN, 128), F32),
            jax.ShapeDtypeStruct((256, 256), BF16),
            jax.ShapeDtypeStruct((512, 512), BF16),
            jax.ShapeDtypeStruct((512, 512), BF16),
            jax.ShapeDtypeStruct((512, 256), BF16),
            jax.ShapeDtypeStruct((256, 512), BF16),
            jax.ShapeDtypeStruct((256, 512), BF16),
            jax.ShapeDtypeStruct((3, 256, TAPS * 128), BF16),
            jax.ShapeDtypeStruct((32, 32 * stored), BF16),
        ),
        in_specs=[vmem] * 2,
        out_specs=(vmem,) * 11,
        compiler_params=pltpu.CompilerParams(vmem_limit_bytes=PREPARE_VMEM),
        cost_estimate=pl.CostEstimate(flops=10**9, bytes_accessed=4 * 10**6, transcendentals=0),
        name="prepare",
    )(taps, live)

    def stack(js):
        return jnp.concatenate([v[:, js] for v in parts], axis=0)

    low, high = slice(0, REACH), slice(xl_len - REACH, xl_len)
    if two_sided:
        xh = [shifted(stack(high), "xline", 1), shifted(stack(low), "xline", -1)]
    else:
        xh = [flipped(jnp.where(x_index == 0, stack(high), stack(low)), [("xline", 1)])]
    first0, first12, edge = pl.pallas_call(
        inline_kernel,
        out_shape=(
            jax.ShapeDtypeStruct((xl_len, 256, 256), F32),
            jax.ShapeDtypeStruct((xl_len // 2, 512, 128), F32),
            jax.ShapeDtypeStruct((32 * xl_len, 128), BF16),
        ),
        in_specs=[vmem] * 7,
        out_specs=(vmem,) * 3,
        scratch_shapes=[pltpu.VMEM((32, 32, 256), BF16)],
        compiler_params=pltpu.CompilerParams(vmem_limit_bytes=INLINE_VMEM),
        cost_estimate=pl.CostEstimate(flops=4 * 10**9, bytes_accessed=16 * 10**6, transcendentals=0),
        name="inline",
    )(bands, pick, turn, live, own_phases, near, far)

    def side(x):
        return jnp.where(d_index == 0, x[:, :, t_len - 128 :], x[:, :, :128])

    dh = jnp.concatenate([edge.reshape(32, xl_len, 128)] + [side(x) for x in xh], axis=1)
    dh = flipped(dh, [("depth", 1)])
    xrows = jnp.concatenate([x.reshape(256, t_len) for x in xh], axis=0)
    edge0, second12 = pl.pallas_call(
        functools.partial(crossline_kernel, two_sided),
        out_shape=(
            jax.ShapeDtypeStruct((3, 256, 256), F32),
            jax.ShapeDtypeStruct((16, 512, 128), BF16),
        ),
        in_specs=[vmem] * 6,
        out_specs=(vmem,) * 2,
        scratch_shapes=[
            pltpu.VMEM((16, 32, 256), BF16),
            pltpu.VMEM((8, 512, 128), F32),
        ],
        compiler_params=pltpu.CompilerParams(vmem_limit_bytes=CROSS_VMEM),
        cost_estimate=pl.CostEstimate(flops=3 * 10**9, bytes_accessed=9 * 10**6, transcendentals=0),
        name="crossline",
    )(bands, w2, pick, turn_x, first12, xrows)
    attr, gram = pl.pallas_call(
        functools.partial(attributes_kernel, two_sided),
        out_shape=(
            jax.ShapeDtypeStruct((16, 3, 8, ORIENT, 128), BF16),
            jax.ShapeDtypeStruct((CHAN, 128), F32),
        ),
        in_specs=[smem] + [vmem] * 12,
        out_specs=(vmem, vmem),
        scratch_shapes=[pltpu.VMEM((3, 256, 128), F32)],
        compiler_params=pltpu.CompilerParams(vmem_limit_bytes=ATTR_VMEM),
        name="attributes",
    )(
        trace_live, trace_live, bands, w2, w3, moves1, moves2, select, gather, first0, edge0,
        second12, dh,
    )

    mine, other = summed(gram)
    out, factor = pl.pallas_call(
        whiten_kernel,
        out_shape=(
            jax.ShapeDtypeStruct((CHAN, 8, 16, 128), BF16),
            jax.ShapeDtypeStruct((CHAN, CHAN), F32),
        ),
        in_specs=[vmem] * 3,
        out_specs=(pl.BlockSpec(memory_space=pl.ANY), vmem),
        scratch_shapes=[
            pltpu.VMEM((CHAN, 128), F32),
            pltpu.VMEM((3, 256, 768), BF16),
            pltpu.VMEM((CHAN, 8, 16, 128), BF16),
            pltpu.SemaphoreType.DMA((3,)),
        ],
        compiler_params=pltpu.CompilerParams(vmem_limit_bytes=WHITEN_VMEM),
        name="whiten",
    )(mine, other, attr)
    return out, factor


def solution(mesh):
    placed = (P(("survey", "inline"), "xline", "depth"), P(("survey", "inline"), "xline"), P())
    return jax.shard_map(
        local,
        mesh=mesh,
        in_specs=placed,
        out_specs=(P(None, ("survey", "inline"), "xline", "depth"), P("survey", None)),
        check_vma=False,
    )
```

```python
import functools
import math

import jax
import jax.numpy as jnp
from jax import lax
from jax.experimental import pallas as pl
from jax.experimental.pallas import tpu as pltpu
from jax.sharding import PartitionSpec as P

ORIENT = 32
TAPS = 5
CHAN = 96
REACH = 8
LAST_ROWS = (8, 10, 12, 14, 15)
FIRST_ROWS = (0, 2, 4, 6, 7)
SENT = 5
ROWS = 16 + 2 * SENT
KEPT = 5
F32 = jnp.float32
BF16 = jnp.bfloat16
LIVE_VMEM = 4 * 1024 * 1024
PREPARE_VMEM = 8 * 1024 * 1024
INLINE_VMEM = 22 * 1024 * 1024
CROSS_VMEM = 16 * 1024 * 1024
ATTR_VMEM = 22 * 1024 * 1024
WHITEN_VMEM = 14 * 1024 * 1024


def iota(shape, dim):
    return lax.broadcasted_iota(jnp.int32, shape, dim)


def rounded(value):
    return value.astype(BF16).astype(F32)


def ones_where(mask):
    return jnp.where(mask, 1.0, 0.0).astype(BF16)


def dot(a, b):
    return jnp.dot(a, b, preferred_element_type=F32)


def shifted(value, axis, step):
    size = lax.axis_size(axis)
    return lax.ppermute(value, axis, [(i, i + step) for i in range(size) if 0 <= i + step < size])


def flipped(value, flips):
    axes = tuple(axis for axis, _ in flips)
    sizes = [lax.axis_size(axis) for axis in axes]
    pairs = []
    for source in range(math.prod(sizes)):
        target, rest, stride = 0, source, 1
        for size, (_, bit) in reversed(list(zip(sizes, flips))):
            target += ((rest % size) ^ bit) * stride
            rest, stride = rest // size, stride * size
        pairs.append((source, target))
    return lax.ppermute(value, axes, pairs)


def bits_of(axis):
    size = lax.axis_size(axis)
    assert size & (size - 1) == 0
    return [(axis, 2 ** i) for i in range(size.bit_length() - 1)]


def summed(value):
    x_bits, il_bits = bits_of("xline"), bits_of("inline")
    for bit in bits_of("depth") + x_bits[1:] + il_bits[2:]:
        value = value + flipped(value, [bit])
    one, two = il_bits[0], x_bits[0]
    a, b, c = flipped(value, [one]), flipped(value, [two]), flipped(value, [one, two])
    value = (value + a) + (b + c)
    return value, flipped(value, [il_bits[1]])


def halo_select(level, stored, x_left, depth_first):
    dilation = 2 ** level
    rows, cols = 256, TAPS * 128
    lane = iota((1, cols), 1)
    k = lane // 128
    within = lane % 128
    place = (within + 4) % 8 - 4
    q = ((within + 4) // 8) % 16
    j = 2 * q + dilation * (k - 2)
    slot = jnp.where(j < 0, 40 + j, j)
    if stored == 48:
        slot = jnp.where(j >= 32, j + 8, slot)
    else:
        slot = jnp.where((j < 0) & (x_left == 0), -999999, slot)
        slot = jnp.where((j >= 32) & (x_left == 1), -999999, slot)
    kept = jnp.where(place >= 0, place, place + 4)
    if level == 0:
        kept = jnp.where(place == -2, 4, kept)
    source = kept * stored + slot
    source = jnp.where((place >= 0) & (depth_first == 0), -1, source)
    source = jnp.where((place < 0) & (depth_first == 1), -1, source)
    return ones_where(iota((rows, cols), 0) == source)


def shift_matrix(shifts):
    lane = iota((1, 128 * len(shifts)), 1)
    source = lane % 128
    for i, shift in enumerate(shifts):
        source = jnp.where(lane // 128 == i, source + shift, source)
    past = (source + 128) % 128 + 128
    source = jnp.where(source < 0, past, jnp.where(source >= 128, past, source))
    return ones_where(iota((256, 128 * len(shifts)), 0) == source)


def side_flags():
    x_left = jnp.where(lax.axis_index("xline") == 1, 1, 0)
    depth_first = jnp.where(lax.axis_index("depth") == 0, 1, 0)
    return x_left, depth_first, lax.axis_index("inline") % 2


def live_kernel(trace_ref, seismic_ref, live_ref, near_ref, far_ref):
    n_il, n_xl, _ = seismic_ref.shape
    eye = iota((n_xl, n_xl), 0) == iota((n_xl, n_xl), 1)
    for p in range(n_il):
        row = jnp.broadcast_to(trace_ref[p : p + 1, :], (n_xl, n_xl))
        kept = dot(jnp.where(eye, row, 0.0).astype(BF16), seismic_ref[p])
        live_ref[p * n_xl : (p + 1) * n_xl, :] = kept.astype(BF16)
    odd = side_flags()[2]

    def put(ref, rows):
        for i, p in enumerate(rows):
            ref[i * n_xl : (i + 1) * n_xl] = live_ref[p * n_xl : (p + 1) * n_xl]

    @pl.when(odd == 1)
    def _():
        put(near_ref, FIRST_ROWS)
        put(far_ref, LAST_ROWS)

    @pl.when(odd == 0)
    def _():
        put(near_ref, LAST_ROWS)
        put(far_ref, FIRST_ROWS)


def banded(level, taps_ref, bands, il_odd):
    lane = iota((ORIENT, 128), 1)
    cs = slice(level * ORIENT, (level + 1) * ORIENT)
    cols = [jnp.broadcast_to(taps_ref[0, cs, k : k + 1], (ORIENT, 128)) for k in range(TAPS)]
    for o in range(8):
        total = jnp.zeros((ORIENT, 128), F32)
        for k in range(TAPS):
            p = 2 * o + 2 ** level * (k - 2)
            if p < 0:
                place = 16 + SENT + LAST_ROWS.index(p + 16) - SENT * il_odd
            elif p >= 16:
                place = 16 + FIRST_ROWS.index(p - 16) + SENT * il_odd
            else:
                place = p
            total = jnp.where(lane == place, cols[k], total)
        bands[pl.ds(level * 256 + o * ORIENT, ORIENT), :] = total.astype(BF16)


def phase_pick():
    n = iota((256, 256), 1)
    return ones_where(iota((256, 256), 0) == jnp.where(n < 128, 2 * n, 2 * n - 255))


def prepare_kernel(
    stored, taps_ref, own_ref, bands, w2, w3, pick, turn, turn_x, own_out, moves1, moves2, select, gather
):
    x_left, depth_first, il_odd = side_flags()
    for k in range(TAPS):
        w2[k] = jnp.broadcast_to(taps_ref[1, :, k : k + 1], (CHAN, 128))
        w3[k] = jnp.broadcast_to(taps_ref[2, :, k : k + 1], (CHAN, 128))
    for level in range(3):
        banded(level, taps_ref, bands, il_odd)
        select[level] = halo_select(level, stored, x_left, depth_first)
    pick[...] = phase_pick()
    own_out[...] = dot(own_ref[...], pick[...]).astype(BF16)
    r = iota((512, 512), 0)
    c = iota((512, 512), 1)
    turn[...] = ones_where(c == r % 32 * 16 + r // 32)
    source = r // 256 * (8 * ROWS) + r % 32 * 8 + r // 32 % 8
    turn_x[...] = ones_where(jnp.where(r % 32 < ROWS, source, -1) == c)
    moves1[...] = shift_matrix((-2, -1, 1, 2))
    moves2[...] = shift_matrix((-4, -2, 2, 4))
    rows = 32 * stored
    gather[...] = ones_where(iota((32, rows), 1) // stored == iota((32, rows), 0))


def inline_kernel(
    bands, pick, turn, own_ref, own_phases, near_ref, far_ref, first0, first12, edge_ref, planes
):
    depth_first = side_flags()[1]

    def put_edge(ts):
        for at, ref in ((0, own_ref), (512, near_ref), (512 + near_ref.shape[0], far_ref)):
            edge_ref[at : at + ref.shape[0], :] = ref[:, ts]

    pl.when(depth_first == 1)(lambda: put_edge(slice(128, 256)))
    pl.when(depth_first == 0)(lambda: put_edge(slice(0, 128)))

    own = own_phases[...].reshape(16, 32, 256)
    near = dot(near_ref[...], pick[...]).astype(BF16).reshape(SENT, 32, 256)
    far = dot(far_ref[...], pick[...]).astype(BF16).reshape(SENT, 32, 256)
    none = jnp.zeros((32 - ROWS, 16, 256), BF16)
    for half in range(2):
        js = slice(half * 16, half * 16 + 16)
        block = jnp.concatenate([own[:, js], near[:, js], far[:, js], none], axis=0).reshape(512, 256)
        planes[half * 16 : half * 16 + 16] = dot(turn[...], block).astype(BF16).reshape(16, 32, 256)

    a0 = bands[0:256, 0:32]
    a12 = bands[256:768, 0:32]
    def level0_first(j, _):
        first0[j] = rounded(dot(a0, planes[j]))
        return 0

    lax.fori_loop(0, 32, level0_first, 0, unroll=8)

    def even_first(pair, _):
        both = jnp.concatenate([planes[4 * pair, :, 0:128], planes[4 * pair + 2, :, 0:128]], axis=1)
        out = rounded(dot(a12, both))
        first12[2 * pair] = out[:, 0:128]
        first12[2 * pair + 1] = out[:, 128:256]
        return 0

    lax.fori_loop(0, 8, even_first, 0, unroll=4)


def tall(ref, level, k):
    return jnp.concatenate([ref[k, level * ORIENT : (level + 1) * ORIENT]] * 8, axis=0)


def crossline_kernel(
    two_sided, bands, w2, pick, turn_x, first12, xh_ref, edge0, second12, edges, edge12
):
    x_left = side_flags()[0]

    got = dot(xh_ref[...], pick[...])
    if not two_sided:
        left = jnp.where(x_left == 1, 1.0, 0.0)
        got = jnp.concatenate([got * left, got * (1.0 - left)], axis=0)
    got = jnp.concatenate([got.astype(BF16), jnp.zeros((512 - 16 * ROWS, 256), BF16)], axis=0)
    edges[...] = dot(turn_x[...], got).astype(BF16).reshape(16, 32, 256)
    a0 = bands[0:256, 0:32]
    a12 = bands[256:768, 0:32]
    for i, slot in enumerate((6, 7, 8)):
        edge0[i] = rounded(dot(a0, edges[slot]))
    for i in range(4):
        both = jnp.concatenate([edges[4 * i, :, 0:128], edges[4 * i + 2, :, 0:128]], axis=1)
        out = rounded(dot(a12, both))
        edge12[2 * i], edge12[2 * i + 1] = out[:, 0:128], out[:, 128:256]

    def filtered(level, q, plane):
        for c16 in range(2):
            start = level * ORIENT + c16 * 16
            s2 = [w2[k, start : start + 16] for k in range(TAPS)]
            for o in range(8):
                row = (level - 1) * 256 + o * ORIENT + c16 * 16
                here = slice(row, row + 16)
                total = sum(s2[k] * plane(q + level * (k - 2), here) for k in range(TAPS))
                second12[q, here, :] = total.astype(BF16)

    def own_plane(e, here):
        return first12[e, here, :]

    def any_plane(e, here):
        if 0 <= e < 16:
            return first12[e, here, :]
        return edge12[e + 4 if e < 0 else e - 12, here, :]

    for level in (1, 2):
        reach = 2 * level

        def inner(q, _, level=level):
            filtered(level, q, own_plane)
            return 0

        lax.fori_loop(reach, 16 - reach, inner, 0)
        for i in range(reach):
            filtered(level, i, any_plane)
            filtered(level, 15 - i, any_plane)


def attributes_kernel(
    two_sided, live_smem, live_ref, bands, w2, w3, moves1, moves2, select, gather, first0, edge0,
    second12, dh_ref, attr_ref, gram_ref, halo2,
):
    depth_first = side_flags()[1]
    stored = 48 if two_sided else 40

    n = iota((1, 256), 1)
    kept = n // stored
    sample = 2 * kept - jnp.where(kept == 4, 1, 0) + jnp.where(depth_first == 1, 0, 120)
    sample = jnp.where(kept < KEPT, sample, -1)
    spread = ones_where(iota((128, 256), 0) == sample)
    rows = 32 * stored
    got = dh_ref[...].reshape(ROWS * stored, 128)
    got = jnp.concatenate([got, jnp.zeros((rows - ROWS * stored, 128), BF16)], axis=0)
    wide = dot(got, spread)
    wide = jnp.where(iota((rows, 256), 0) % stored == n % stored, wide, 0.0).astype(BF16)
    lanes = dot(gather[...], wide).astype(BF16)
    for level in range(3):
        cols = dot(lanes, select[level]).astype(BF16)
        part = rounded(dot(bands[level * 256 : level * 256 + 256, 0:32], cols))
        total = jnp.zeros((256, 128), F32)
        for k in range(TAPS):
            total = total + part[:, k * 128 : k * 128 + 128] * tall(w2, level, k)
        total = rounded(total)
        if level == 0:
            w3_0, w3_1, w3_4 = [tall(w3, 0, k) for k in (0, 1, 4)]
            before_first = total * w3_0 + pltpu.roll(total, 1, 1) * w3_1
            total = jnp.where(iota((256, 128), 1) % 8 == 7, before_first, total * w3_4)
        halo2[level] = total


    def one_q(q, plane):
        align = (128 - 8 * q) % 128
        live_q = [live_smem[2 * o, 2 * q].astype(F32) for o in range(8)]
        lane = iota((16, 128), 1)

        def put(o, start, total):
            at = start % ORIENT
            attr_ref[2 * o + q // 8, start // ORIENT, q % 8, at : at + 16, :] = (total * live_q[o]).astype(BF16)

        for level in (1, 2):
            halo = pltpu.roll(halo2[level], align, 1).astype(BF16)
            value = second12[q, (level - 1) * 256 : level * 256, :]
            moved = dot(jnp.concatenate([value, halo], axis=1), (moves1 if level == 1 else moves2)[...])
            for c16 in range(2):
                start = level * ORIENT + c16 * 16
                s3 = [w3[k, start : start + 16] for k in range(TAPS)]
                for o in range(8):
                    rows = slice(o * ORIENT + c16 * 16, o * ORIENT + c16 * 16 + 16)
                    total = s3[2] * value[rows].astype(F32)
                    for i, k in enumerate((0, 1, 3, 4)):
                        total = total + s3[k] * moved[rows, i * 128 : i * 128 + 128]
                    put(o, start, total)
        for c16 in range(2):
            s2 = [w2[k, c16 * 16 : c16 * 16 + 16] for k in range(TAPS)]
            s3 = [w3[k, c16 * 16 : c16 * 16 + 16] for k in range(TAPS)]
            for o in range(8):
                rows = slice(o * ORIENT + c16 * 16, o * ORIENT + c16 * 16 + 16)
                both = []
                for ts in (slice(0, 128), slice(128, 256)):
                    total = sum(s2[k] * plane(2 * q + k - 2, rows, ts) for k in range(TAPS))
                    both.append(rounded(total))
                even, odd = both
                halo = pltpu.roll(halo2[0, rows], align, 1)
                back = jnp.where(lane == 127, halo, s3[0] * even + s3[1] * odd)
                ahead = jnp.where(lane == 0, halo, s3[4] * even)
                moved = pltpu.roll(back, 1, 1) + pltpu.roll(ahead, 127, 1)
                put(o, c16 * 16, s3[2] * even + s3[3] * odd + moved)

    def add_gram(q, total):
        for o in range(0, 8, 2):
            both = jnp.concatenate(
                [
                    jnp.concatenate([attr_ref[2 * i + q // 8, level, q % 8] for level in range(3)], axis=0)
                    for i in (o, o + 1)
                ],
                axis=1,
            )
            total = total + lax.dot_general(
                both, both, (((1,), (1,)), ((), ())), preferred_element_type=F32
            )
        return total

    def own_plane(j, rows, ts):
        return first0[j, rows, ts]

    def any_plane(j, rows, ts):
        if 0 <= j < 32:
            return first0[j, rows, ts]
        return edge0[j + 2 if j < 0 else 2, rows, ts]

    def next_q(q, total):
        total = add_gram(q - 1, total)
        one_q(q, own_plane)
        return total

    one_q(0, any_plane)
    gram = lax.fori_loop(1, 15, next_q, jnp.zeros((CHAN, CHAN), F32))
    gram = add_gram(14, gram)
    one_q(15, any_plane)
    gram = add_gram(15, gram)
    alive = live_ref[...]
    chosen = (iota(alive.shape, 0) % 2 == 0) & (iota(alive.shape, 1) % 2 == 0)
    count = jnp.sum(jnp.where(chosen, alive.astype(F32), 0.0)) * 128.0
    gram_ref[...] = jnp.full((CHAN, 128), count, F32)
    gram_ref[:, 0:CHAN] = gram


def whiten_kernel(mine_ref, other_ref, attr_ref, out_hbm, factor_ref, inverse, kron, out_ref, sems):
    total = mine_ref[...] + other_ref[...]
    lane = iota((8, 128), 1)
    sub = iota((8, 128), 0)
    count = jnp.broadcast_to(total[0:1, CHAN : CHAN + 1], (8, 128))
    blocks = []
    for g in range(CHAN // 8):
        blocks.append(jnp.where(lane < CHAN, total[8 * g : 8 * g + 8] / count, 0.0))

    n = iota((CHAN, 768), 1)
    spread = ones_where(iota((CHAN, 768), 0) == n // 256 * ORIENT + n % ORIENT)
    tall = ones_where(iota((256, ORIENT), 0) // 8 == iota((256, ORIENT), 1))

    def spread_inverse(level):
        depth = 256 * (level + 1)
        low = inverse[level * ORIENT : (level + 1) * ORIENT, 0:CHAN].astype(BF16)
        full = dot(tall, dot(low, spread[:, 0:depth]).astype(BF16))
        keep = iota((256, depth), 0) % 8 == iota((256, depth), 1) // ORIENT % 8
        kron[level, :, 0:depth] = jnp.where(keep, full, 0.0).astype(BF16)

    def sent(level):
        cs = slice(level * ORIENT, (level + 1) * ORIENT)
        return pltpu.make_async_copy(out_ref.at[cs], out_hbm.at[cs], sems.at[level])

    def whiten_pair(level, pair):
        depth = 256 * (level + 1)
        halves = []
        for half in range(2):
            rows = [
                attr_ref[2 * (2 * pair + i) + half, 0 : level + 1].reshape(depth, 128) for i in range(2)
            ]
            halves.append(dot(kron[level, :, 0:depth], jnp.concatenate(rows, axis=1)))
        for i in range(2):
            both = [half[:, i * 128 : i * 128 + 128].reshape(ORIENT, 8, 128) for half in halves]
            out_ref[level * ORIENT : (level + 1) * ORIENT, 2 * pair + i] = jnp.concatenate(
                both, axis=1
            ).astype(BF16)
        if pair == 3:
            sent(level).start()

    row_lane = iota((1, 128), 1)

    def finish(j, row, inv_row, pivot):
        scale = lax.rsqrt(pivot)
        factor_ref[j : j + 1, :] = (jnp.where(row_lane >= j, row, 0.0) * scale)[:, 0:CHAN]
        inverse[j : j + 1, :] = jnp.where(row_lane <= j, inv_row, 0.0) * scale

    def spread_lane(block, j):
        return jnp.broadcast_to(block[:, j : j + 1], (8, 128))

    def spread_row(block, i):
        return jnp.broadcast_to(block[i : i + 1, :], (8, 128))

    for j in range(0, CHAN, 4):
        g, s = j // 8, j % 8
        top = blocks[g]
        cols = [spread_lane(top, j + i) for i in range(4)]
        rows = [spread_row(top, s + i) for i in range(4)]
        d = [[spread_row(cols[min(m, i)], s + max(m, i)) for i in range(4)] for m in range(4)]
        p_inv = 1.0 / (d[0][0] * d[1][1] - d[0][1] * d[0][1])
        adj = [[d[1][1], -d[0][1]], [-d[0][1], d[0][0]]]
        h = [
            [(d[2 + m][0] * adj[0][i] + d[2 + m][1] * adj[1][i]) * p_inv for i in range(2)]
            for m in range(2)
        ]
        t = [
            [d[2 + m][2 + i] - (h[m][0] * d[0][2 + i] + h[m][1] * d[1][2 + i]) for i in range(2)]
            for m in range(2)
        ]
        t01 = t[1][0]
        t_inv = 1.0 / (t[0][0] * t[1][1] - t01 * t01)
        unit = []
        for i in range(4):
            value = rows[i]
            for m in range(4):
                value = jnp.where(lane == j + m, 1.0 if m == i else 0.0, value)
            unit.append(value)
        below = [unit[2 + m] - (h[m][0] * unit[0] + h[m][1] * unit[1]) for m in range(2)]
        up2 = (t[1][1] * below[0] - t01 * below[1]) * t_inv
        up3 = (t[0][0] * below[1] - t01 * below[0]) * t_inv
        inner = [unit[0] * d[1][1] - unit[1] * d[0][1], unit[1] * d[0][0] - unit[0] * d[0][1]]
        up0 = inner[0] * p_inv - (h[0][0] * up2 + h[1][0] * up3)
        up1 = inner[1] * p_inv - (h[0][1] * up2 + h[1][1] * up3)
        ups = (up0, up1, up2, up3)
        ratio0 = d[0][1] / d[0][0]
        ratio1 = t01 / t[0][0]
        mix0 = rows[2] - (h[0][0] * rows[0] + h[0][1] * rows[1])
        mix1 = rows[3] - (h[1][0] * rows[0] + h[1][1] * rows[1])
        solved = [rows[0], rows[1] - ratio0 * rows[0], mix0, mix1 - ratio1 * mix0]
        inv_solved = [unit[0], unit[1] - ratio0 * unit[0], below[0], below[1] - ratio1 * below[0]]
        pivots = [d[0][0], d[1][1] - d[0][1] * ratio0, t[0][0], t[1][1] - t01 * ratio1]
        for i in range(4):
            finish(j + i, solved[i][0:1], inv_solved[i][0:1], pivots[i][0:1])
        if j % ORIENT == ORIENT - 4:
            spread_inverse(j // ORIENT)
        if j >= ORIENT and j % 8 == 4:
            whiten_pair(j // ORIENT - 1, j % ORIENT // 8)
        if j == CHAN - 4:
            break
        inside = (lane >= j) & (lane < j + 4)
        for k in range(g, CHAN // 8):
            if k > g:
                cols = [spread_lane(blocks[k], j + i) for i in range(4)]
            else:
                if s == 4:
                    continue
                cols = [jnp.where(sub > s + 3, col, 0.0) for col in cols]
            change = (cols[0] * ups[0] + cols[1] * ups[1]) + (cols[2] * ups[2] + cols[3] * ups[3])
            blocks[k] = jnp.where(inside, 0.0, blocks[k]) - change

    for pair in range(4):
        whiten_pair(2, pair)
    for level in range(3):
        sent(level).wait()


def local(seismic, trace_live, filter_taps):
    il_len, xl_len, t_len = seismic.shape
    assert (il_len, xl_len, t_len) == (16, 32, 256) and lax.axis_size("depth") == 2
    taps = filter_taps.astype(F32)
    x_index = lax.axis_index("xline")
    d_index = lax.axis_index("depth")
    two_sided = lax.axis_size("xline") > 2
    vmem = pl.BlockSpec(memory_space=pltpu.VMEM)
    smem = pl.BlockSpec(memory_space=pltpu.SMEM)

    live, near, far = pl.pallas_call(
        live_kernel,
        out_shape=(
            jax.ShapeDtypeStruct((il_len * xl_len, t_len), BF16),
            jax.ShapeDtypeStruct((SENT * xl_len, t_len), BF16),
            jax.ShapeDtypeStruct((SENT * xl_len, t_len), BF16),
        ),
        in_specs=[vmem] * 2,
        out_specs=(vmem,) * 3,
        compiler_params=pltpu.CompilerParams(vmem_limit_bytes=LIVE_VMEM),
        name="live",
    )(trace_live.astype(F32), seismic)
    il_size = lax.axis_size("inline")
    near_pairs = [(i, i ^ 1) for i in range(il_size) if i ^ 1 < il_size]
    far_pairs = [(i, i - 1 if i % 2 == 0 else i + 1) for i in range(1, il_size)]
    far_pairs = [(i, j) for i, j in far_pairs if j < il_size]
    near = lax.ppermute(near, "inline", near_pairs)
    far = lax.ppermute(far, "inline", far_pairs)
    parts = [v.reshape(-1, xl_len, t_len) for v in (live, near, far)]
    stored = 48 if two_sided else 40
    bands, w2, w3, pick, turn, turn_x, own_phases, moves1, moves2, select, gather = pl.pallas_call(
        functools.partial(prepare_kernel, stored),
        out_shape=(
            jax.ShapeDtypeStruct((3 * 256, 128), BF16),
            jax.ShapeDtypeStruct((TAPS, CHAN, 128), F32),
            jax.ShapeDtypeStruct((TAPS, CHAN, 128), F32),
            jax.ShapeDtypeStruct((256, 256), BF16),
            jax.ShapeDtypeStruct((512, 512), BF16),
            jax.ShapeDtypeStruct((512, 512), BF16),
            jax.ShapeDtypeStruct((512, 256), BF16),
            jax.ShapeDtypeStruct((256, 512), BF16),
            jax.ShapeDtypeStruct((256, 512), BF16),
            jax.ShapeDtypeStruct((3, 256, TAPS * 128), BF16),
            jax.ShapeDtypeStruct((32, 32 * stored), BF16),
        ),
        in_specs=[vmem] * 2,
        out_specs=(vmem,) * 11,
        compiler_params=pltpu.CompilerParams(vmem_limit_bytes=PREPARE_VMEM),
        cost_estimate=pl.CostEstimate(flops=10**9, bytes_accessed=4 * 10**6, transcendentals=0),
        name="prepare",
    )(taps, live)

    def stack(js):
        return jnp.concatenate([v[:, js] for v in parts], axis=0)

    low, high = slice(0, REACH), slice(xl_len - REACH, xl_len)
    if two_sided:
        xh = [shifted(stack(high), "xline", 1), shifted(stack(low), "xline", -1)]
    else:
        xh = [flipped(jnp.where(x_index == 0, stack(high), stack(low)), [("xline", 1)])]
    first0, first12, edge = pl.pallas_call(
        inline_kernel,
        out_shape=(
            jax.ShapeDtypeStruct((xl_len, 256, 256), F32),
            jax.ShapeDtypeStruct((xl_len // 2, 512, 128), F32),
            jax.ShapeDtypeStruct((ROWS * xl_len, 128), BF16),
        ),
        in_specs=[vmem] * 7,
        out_specs=(vmem,) * 3,
        scratch_shapes=[pltpu.VMEM((32, 32, 256), BF16)],
        compiler_params=pltpu.CompilerParams(vmem_limit_bytes=INLINE_VMEM),
        cost_estimate=pl.CostEstimate(flops=4 * 10**9, bytes_accessed=16 * 10**6, transcendentals=0),
        name="inline",
    )(bands, pick, turn, live, own_phases, near, far)

    def side(x):
        return jnp.where(d_index == 0, x[:, :, t_len - 128 :], x[:, :, :128])

    dh = jnp.concatenate([edge.reshape(ROWS, xl_len, 128)] + [side(x) for x in xh], axis=1)
    dh = flipped(dh, [("depth", 1)])
    xrows = jnp.concatenate([x.reshape(REACH * ROWS, t_len) for x in xh], axis=0)
    edge0, second12 = pl.pallas_call(
        functools.partial(crossline_kernel, two_sided),
        out_shape=(
            jax.ShapeDtypeStruct((3, 256, 256), F32),
            jax.ShapeDtypeStruct((16, 512, 128), BF16),
        ),
        in_specs=[vmem] * 6,
        out_specs=(vmem,) * 2,
        scratch_shapes=[
            pltpu.VMEM((16, 32, 256), BF16),
            pltpu.VMEM((8, 512, 128), F32),
        ],
        compiler_params=pltpu.CompilerParams(vmem_limit_bytes=CROSS_VMEM),
        cost_estimate=pl.CostEstimate(flops=3 * 10**9, bytes_accessed=9 * 10**6, transcendentals=0),
        name="crossline",
    )(bands, w2, pick, turn_x, first12, xrows)
    attr, gram = pl.pallas_call(
        functools.partial(attributes_kernel, two_sided),
        out_shape=(
            jax.ShapeDtypeStruct((16, 3, 8, ORIENT, 128), BF16),
            jax.ShapeDtypeStruct((CHAN, 128), F32),
        ),
        in_specs=[smem] + [vmem] * 12,
        out_specs=(vmem, vmem),
        scratch_shapes=[pltpu.VMEM((3, 256, 128), F32)],
        compiler_params=pltpu.CompilerParams(vmem_limit_bytes=ATTR_VMEM),
        name="attributes",
    )(
        trace_live, trace_live, bands, w2, w3, moves1, moves2, select, gather, first0, edge0,
        second12, dh,
    )

    mine, other = summed(gram)
    out, factor = pl.pallas_call(
        whiten_kernel,
        out_shape=(
            jax.ShapeDtypeStruct((CHAN, 8, 16, 128), BF16),
            jax.ShapeDtypeStruct((CHAN, CHAN), F32),
        ),
        in_specs=[vmem] * 3,
        out_specs=(pl.BlockSpec(memory_space=pl.ANY), vmem),
        scratch_shapes=[
            pltpu.VMEM((CHAN, 128), F32),
            pltpu.VMEM((3, 256, 768), BF16),
            pltpu.VMEM((CHAN, 8, 16, 128), BF16),
            pltpu.SemaphoreType.DMA((3,)),
        ],
        compiler_params=pltpu.CompilerParams(vmem_limit_bytes=WHITEN_VMEM),
        name="whiten",
    )(mine, other, attr)
    return out, factor


def solution(mesh):
    placed = (P(("survey", "inline"), "xline", "depth"), P(("survey", "inline"), "xline"), P())
    return jax.shard_map(
        local,
        mesh=mesh,
        in_specs=placed,
        out_specs=(P(None, ("survey", "inline"), "xline", "depth"), P("survey", None)),
        check_vma=False,
    )
```

```python
import functools
import math

import jax
import jax.numpy as jnp
from jax import lax
from jax.experimental import pallas as pl
from jax.experimental.pallas import tpu as pltpu
from jax.sharding import PartitionSpec as P

ORIENT = 32
TAPS = 5
CHAN = 96
REACH = 8
LAST_ROWS = (8, 10, 12, 14, 15)
FIRST_ROWS = (0, 2, 4, 6, 7)
SENT = 5
ROWS = 16 + 2 * SENT
KEPT = 5
F32 = jnp.float32
BF16 = jnp.bfloat16
LIVE_VMEM = 4 * 1024 * 1024
PREPARE_VMEM = 8 * 1024 * 1024
INLINE_VMEM = 22 * 1024 * 1024
CROSS_VMEM = 16 * 1024 * 1024
ATTR_VMEM = 22 * 1024 * 1024
WHITEN_VMEM = 14 * 1024 * 1024


def iota(shape, dim):
    return lax.broadcasted_iota(jnp.int32, shape, dim)


def rounded(value):
    return value.astype(BF16).astype(F32)


def ones_where(mask):
    return jnp.where(mask, 1.0, 0.0).astype(BF16)


def dot(a, b):
    return jnp.dot(a, b, preferred_element_type=F32)


def shifted(value, axis, step):
    size = lax.axis_size(axis)
    return lax.ppermute(value, axis, [(i, i + step) for i in range(size) if 0 <= i + step < size])


def flipped(value, flips):
    axes = tuple(axis for axis, _ in flips)
    sizes = [lax.axis_size(axis) for axis in axes]
    pairs = []
    for source in range(math.prod(sizes)):
        target, rest, stride = 0, source, 1
        for size, (_, bit) in reversed(list(zip(sizes, flips))):
            target += ((rest % size) ^ bit) * stride
            rest, stride = rest // size, stride * size
        pairs.append((source, target))
    return lax.ppermute(value, axes, pairs)


def bits_of(axis):
    size = lax.axis_size(axis)
    assert size & (size - 1) == 0
    return [(axis, 2 ** i) for i in range(size.bit_length() - 1)]


def summed(value):
    x_bits, il_bits = bits_of("xline"), bits_of("inline")
    for bit in bits_of("depth") + x_bits[1:] + il_bits[2:]:
        value = value + flipped(value, [bit])
    one, two = il_bits[0], x_bits[0]
    a, b, c = flipped(value, [one]), flipped(value, [two]), flipped(value, [one, two])
    value = (value + a) + (b + c)
    return value, flipped(value, [il_bits[1]])


def halo_select(level, stored, x_left, depth_first):
    dilation = 2 ** level
    rows, cols = 256, TAPS * 128
    lane = iota((1, cols), 1)
    k = lane // 128
    within = lane % 128
    place = (within + 4) % 8 - 4
    q = ((within + 4) // 8) % 16
    j = 2 * q + dilation * (k - 2)
    slot = jnp.where(j < 0, 40 + j, j)
    if stored == 48:
        slot = jnp.where(j >= 32, j + 8, slot)
    else:
        slot = jnp.where((j < 0) & (x_left == 0), -999999, slot)
        slot = jnp.where((j >= 32) & (x_left == 1), -999999, slot)
    kept = jnp.where(place >= 0, place, place + 4)
    if level == 0:
        kept = jnp.where(place == -2, 4, kept)
    source = kept * stored + slot
    source = jnp.where((place >= 0) & (depth_first == 0), -1, source)
    source = jnp.where((place < 0) & (depth_first == 1), -1, source)
    return ones_where(iota((rows, cols), 0) == source)


def shift_matrix(shifts):
    lane = iota((1, 128 * len(shifts)), 1)
    source = lane % 128
    for i, shift in enumerate(shifts):
        source = jnp.where(lane // 128 == i, source + shift, source)
    past = (source + 128) % 128 + 128
    source = jnp.where(source < 0, past, jnp.where(source >= 128, past, source))
    return ones_where(iota((256, 128 * len(shifts)), 0) == source)


def side_flags():
    x_left = jnp.where(lax.axis_index("xline") == 1, 1, 0)
    depth_first = jnp.where(lax.axis_index("depth") == 0, 1, 0)
    return x_left, depth_first, lax.axis_index("inline") % 2


def live_kernel(trace_ref, seismic_ref, live_ref, near_ref, far_ref):
    n_il, n_xl, _ = seismic_ref.shape
    eye = iota((n_xl, n_xl), 0) == iota((n_xl, n_xl), 1)
    for p in range(n_il):
        row = jnp.broadcast_to(trace_ref[p : p + 1, :], (n_xl, n_xl))
        kept = dot(jnp.where(eye, row, 0.0).astype(BF16), seismic_ref[p])
        live_ref[p * n_xl : (p + 1) * n_xl, :] = kept.astype(BF16)
    odd = side_flags()[2]

    def put(ref, rows):
        for i, p in enumerate(rows):
            ref[i * n_xl : (i + 1) * n_xl] = live_ref[p * n_xl : (p + 1) * n_xl]

    @pl.when(odd == 1)
    def _():
        put(near_ref, FIRST_ROWS)
        put(far_ref, LAST_ROWS)

    @pl.when(odd == 0)
    def _():
        put(near_ref, LAST_ROWS)
        put(far_ref, FIRST_ROWS)


def banded(level, taps_ref, bands, il_odd):
    lane = iota((ORIENT, 128), 1)
    cs = slice(level * ORIENT, (level + 1) * ORIENT)
    cols = [jnp.broadcast_to(taps_ref[0, cs, k : k + 1], (ORIENT, 128)) for k in range(TAPS)]
    for o in range(8):
        total = jnp.zeros((ORIENT, 128), F32)
        for k in range(TAPS):
            p = 2 * o + 2 ** level * (k - 2)
            if p < 0:
                place = 16 + SENT + LAST_ROWS.index(p + 16) - SENT * il_odd
            elif p >= 16:
                place = 16 + FIRST_ROWS.index(p - 16) + SENT * il_odd
            else:
                place = p
            total = jnp.where(lane == place, cols[k], total)
        bands[pl.ds(level * 256 + o * ORIENT, ORIENT), :] = total.astype(BF16)


def phase_pick():
    n = iota((256, 256), 1)
    return ones_where(iota((256, 256), 0) == jnp.where(n < 128, 2 * n, 2 * n - 255))


def prepare_kernel(
    taps_ref, own_ref, bands, w2, w3, pick, turn, own_out
):
    il_odd = side_flags()[2]
    for k in range(TAPS):
        w2[k] = jnp.broadcast_to(taps_ref[1, :, k : k + 1], (CHAN, 128))
        w3[k] = jnp.broadcast_to(taps_ref[2, :, k : k + 1], (CHAN, 128))
    for level in range(3):
        banded(level, taps_ref, bands, il_odd)
    pick[...] = phase_pick()
    own_out[...] = dot(own_ref[...], pick[...]).astype(BF16)
    r = iota((512, 512), 0)
    c = iota((512, 512), 1)
    turn[...] = ones_where(c == r % 32 * 16 + r // 32)


def inline_kernel(
    stored, bands, pick, turn, own_ref, own_phases, near_ref, far_ref, first0, first12, edge_ref,
    turn_x, moves1, moves2, select, gather, planes,
):
    x_left, depth_first, _ = side_flags()
    r = iota((512, 512), 0)
    c = iota((512, 512), 1)
    source = r // 256 * (8 * ROWS) + r % 32 * 8 + r // 32 % 8
    turn_x[...] = ones_where(jnp.where(r % 32 < ROWS, source, -1) == c)
    moves1[...] = shift_matrix((-2, -1, 1, 2))
    moves2[...] = shift_matrix((-4, -2, 2, 4))
    rows = 32 * stored
    gather[...] = ones_where(iota((32, rows), 1) // stored == iota((32, rows), 0))
    for level in range(3):
        select[level] = halo_select(level, stored, x_left, depth_first)

    def put_edge(ts):
        for at, ref in ((0, own_ref), (512, near_ref), (512 + near_ref.shape[0], far_ref)):
            edge_ref[at : at + ref.shape[0], :] = ref[:, ts]

    pl.when(depth_first == 1)(lambda: put_edge(slice(128, 256)))
    pl.when(depth_first == 0)(lambda: put_edge(slice(0, 128)))

    own = own_phases[...].reshape(16, 32, 256)
    near = dot(near_ref[...], pick[...]).astype(BF16).reshape(SENT, 32, 256)
    far = dot(far_ref[...], pick[...]).astype(BF16).reshape(SENT, 32, 256)
    none = jnp.zeros((32 - ROWS, 16, 256), BF16)
    for half in range(2):
        js = slice(half * 16, half * 16 + 16)
        block = jnp.concatenate([own[:, js], near[:, js], far[:, js], none], axis=0).reshape(512, 256)
        planes[half * 16 : half * 16 + 16] = dot(turn[...], block).astype(BF16).reshape(16, 32, 256)

    a0 = bands[0:256, 0:32]
    a12 = bands[256:768, 0:32]
    def level0_first(j, _):
        first0[j] = rounded(dot(a0, planes[j]))
        return 0

    lax.fori_loop(0, 32, level0_first, 0, unroll=16)

    def even_first(pair, _):
        both = jnp.concatenate([planes[4 * pair, :, 0:128], planes[4 * pair + 2, :, 0:128]], axis=1)
        out = rounded(dot(a12, both))
        first12[2 * pair] = out[:, 0:128]
        first12[2 * pair + 1] = out[:, 128:256]
        return 0

    lax.fori_loop(0, 8, even_first, 0, unroll=8)


def tall(ref, level, k):
    return jnp.concatenate([ref[k, level * ORIENT : (level + 1) * ORIENT]] * 8, axis=0)


def crossline_kernel(
    two_sided, bands, w2, pick, turn_x, first12, xh_ref, edge0, second12, edges, edge12
):
    x_left = side_flags()[0]

    got = dot(xh_ref[...], pick[...])
    if not two_sided:
        left = jnp.where(x_left == 1, 1.0, 0.0)
        got = jnp.concatenate([got * left, got * (1.0 - left)], axis=0)
    got = jnp.concatenate([got.astype(BF16), jnp.zeros((512 - 16 * ROWS, 256), BF16)], axis=0)
    edges[...] = dot(turn_x[...], got).astype(BF16).reshape(16, 32, 256)
    a0 = bands[0:256, 0:32]
    a12 = bands[256:768, 0:32]
    for i, slot in enumerate((6, 7, 8)):
        edge0[i] = rounded(dot(a0, edges[slot]))
    for i in range(4):
        both = jnp.concatenate([edges[4 * i, :, 0:128], edges[4 * i + 2, :, 0:128]], axis=1)
        out = rounded(dot(a12, both))
        edge12[2 * i], edge12[2 * i + 1] = out[:, 0:128], out[:, 128:256]

    def filtered(level, q, plane):
        for c16 in range(2):
            start = level * ORIENT + c16 * 16
            s2 = [w2[k, start : start + 16] for k in range(TAPS)]
            for o in range(8):
                row = (level - 1) * 256 + o * ORIENT + c16 * 16
                here = slice(row, row + 16)
                total = sum(s2[k] * plane(q + level * (k - 2), here) for k in range(TAPS))
                second12[q, here, :] = total.astype(BF16)

    def own_plane(e, here):
        return first12[e, here, :]

    def any_plane(e, here):
        if 0 <= e < 16:
            return first12[e, here, :]
        return edge12[e + 4 if e < 0 else e - 12, here, :]

    for level in (1, 2):
        reach = 2 * level

        def inner(q, _, level=level):
            filtered(level, q, own_plane)
            return 0

        lax.fori_loop(reach, 16 - reach, inner, 0)
        for i in range(reach):
            filtered(level, i, any_plane)
            filtered(level, 15 - i, any_plane)


def attributes_kernel(
    two_sided, live_smem, live_ref, bands, w2, w3, moves1, moves2, select, gather, first0, edge0,
    second12, dh_ref, attr_ref, gram_ref, halo2,
):
    depth_first = side_flags()[1]
    stored = 48 if two_sided else 40

    n = iota((1, 256), 1)
    kept = n // stored
    sample = 2 * kept - jnp.where(kept == 4, 1, 0) + jnp.where(depth_first == 1, 0, 120)
    sample = jnp.where(kept < KEPT, sample, -1)
    spread = ones_where(iota((128, 256), 0) == sample)
    rows = 32 * stored
    got = dh_ref[...].reshape(ROWS * stored, 128)
    got = jnp.concatenate([got, jnp.zeros((rows - ROWS * stored, 128), BF16)], axis=0)
    wide = dot(got, spread)
    wide = jnp.where(iota((rows, 256), 0) % stored == n % stored, wide, 0.0).astype(BF16)
    lanes = dot(gather[...], wide).astype(BF16)
    for level in range(3):
        cols = dot(lanes, select[level]).astype(BF16)
        part = rounded(dot(bands[level * 256 : level * 256 + 256, 0:32], cols))
        total = jnp.zeros((256, 128), F32)
        for k in range(TAPS):
            total = total + part[:, k * 128 : k * 128 + 128] * tall(w2, level, k)
        total = rounded(total)
        if level == 0:
            w3_0, w3_1, w3_4 = [tall(w3, 0, k) for k in (0, 1, 4)]
            before_first = total * w3_0 + pltpu.roll(total, 1, 1) * w3_1
            total = jnp.where(iota((256, 128), 1) % 8 == 7, before_first, total * w3_4)
        halo2[level] = total


    def one_q(q, plane):
        align = (128 - 8 * q) % 128
        live_q = [live_smem[2 * o, 2 * q].astype(F32) for o in range(8)]
        lane = iota((16, 128), 1)

        def put(o, start, total):
            at = start % ORIENT
            attr_ref[2 * o + q // 8, start // ORIENT, q % 8, at : at + 16, :] = (total * live_q[o]).astype(BF16)

        for level in (1, 2):
            halo = pltpu.roll(halo2[level], align, 1).astype(BF16)
            value = second12[q, (level - 1) * 256 : level * 256, :]
            moved = dot(jnp.concatenate([value, halo], axis=1), (moves1 if level == 1 else moves2)[...])
            for c16 in range(2):
                start = level * ORIENT + c16 * 16
                s3 = [w3[k, start : start + 16] for k in range(TAPS)]
                for o in range(8):
                    rows = slice(o * ORIENT + c16 * 16, o * ORIENT + c16 * 16 + 16)
                    total = s3[2] * value[rows].astype(F32)
                    for i, k in enumerate((0, 1, 3, 4)):
                        total = total + s3[k] * moved[rows, i * 128 : i * 128 + 128]
                    put(o, start, total)
        for c16 in range(2):
            s2 = [w2[k, c16 * 16 : c16 * 16 + 16] for k in range(TAPS)]
            s3 = [w3[k, c16 * 16 : c16 * 16 + 16] for k in range(TAPS)]
            for o in range(8):
                rows = slice(o * ORIENT + c16 * 16, o * ORIENT + c16 * 16 + 16)
                both = []
                for ts in (slice(0, 128), slice(128, 256)):
                    total = sum(s2[k] * plane(2 * q + k - 2, rows, ts) for k in range(TAPS))
                    both.append(rounded(total))
                even, odd = both
                halo = pltpu.roll(halo2[0, rows], align, 1)
                back = jnp.where(lane == 127, halo, s3[0] * even + s3[1] * odd)
                ahead = jnp.where(lane == 0, halo, s3[4] * even)
                moved = pltpu.roll(back, 1, 1) + pltpu.roll(ahead, 127, 1)
                put(o, c16 * 16, s3[2] * even + s3[3] * odd + moved)

    def add_gram(q, total):
        for o in range(0, 8, 2):
            both = jnp.concatenate(
                [
                    jnp.concatenate([attr_ref[2 * i + q // 8, level, q % 8] for level in range(3)], axis=0)
                    for i in (o, o + 1)
                ],
                axis=1,
            )
            total = total + lax.dot_general(
                both, both, (((1,), (1,)), ((), ())), preferred_element_type=F32
            )
        return total

    def own_plane(j, rows, ts):
        return first0[j, rows, ts]

    def any_plane(j, rows, ts):
        if 0 <= j < 32:
            return first0[j, rows, ts]
        return edge0[j + 2 if j < 0 else 2, rows, ts]

    def next_q(q, total):
        total = add_gram(q - 1, total)
        one_q(q, own_plane)
        return total

    one_q(0, any_plane)
    gram = lax.fori_loop(1, 15, next_q, jnp.zeros((CHAN, CHAN), F32))
    gram = add_gram(14, gram)
    one_q(15, any_plane)
    gram = add_gram(15, gram)
    alive = live_ref[...]
    chosen = (iota(alive.shape, 0) % 2 == 0) & (iota(alive.shape, 1) % 2 == 0)
    count = jnp.sum(jnp.where(chosen, alive.astype(F32), 0.0)) * 128.0
    gram_ref[...] = jnp.full((CHAN, 128), count, F32)
    gram_ref[:, 0:CHAN] = gram


def whiten_kernel(mine_ref, other_ref, attr_ref, out_hbm, factor_ref, inverse, kron, out_ref, sems):
    total = mine_ref[...] + other_ref[...]
    lane = iota((8, 128), 1)
    sub = iota((8, 128), 0)
    count = jnp.broadcast_to(total[0:1, CHAN : CHAN + 1], (8, 128))
    blocks = []
    for g in range(CHAN // 8):
        blocks.append(jnp.where(lane < CHAN, total[8 * g : 8 * g + 8] / count, 0.0))

    n = iota((CHAN, 768), 1)
    spread = ones_where(iota((CHAN, 768), 0) == n // 256 * ORIENT + n % ORIENT)
    tall = ones_where(iota((256, ORIENT), 0) // 8 == iota((256, ORIENT), 1))

    def spread_inverse(level):
        depth = 256 * (level + 1)
        low = inverse[level * ORIENT : (level + 1) * ORIENT, 0:CHAN].astype(BF16)
        full = dot(tall, dot(low, spread[:, 0:depth]).astype(BF16))
        keep = iota((256, depth), 0) % 8 == iota((256, depth), 1) // ORIENT % 8
        kron[level, :, 0:depth] = jnp.where(keep, full, 0.0).astype(BF16)

    def sent(level):
        cs = slice(level * ORIENT, (level + 1) * ORIENT)
        return pltpu.make_async_copy(out_ref.at[cs], out_hbm.at[cs], sems.at[level])

    def whiten_pair(level, pair):
        depth = 256 * (level + 1)
        halves = []
        for half in range(2):
            rows = [
                attr_ref[2 * (2 * pair + i) + half, 0 : level + 1].reshape(depth, 128) for i in range(2)
            ]
            halves.append(dot(kron[level, :, 0:depth], jnp.concatenate(rows, axis=1)))
        for i in range(2):
            both = [half[:, i * 128 : i * 128 + 128].reshape(ORIENT, 8, 128) for half in halves]
            out_ref[level * ORIENT : (level + 1) * ORIENT, 2 * pair + i] = jnp.concatenate(
                both, axis=1
            ).astype(BF16)
        if pair == 3:
            sent(level).start()

    row_lane = iota((1, 128), 1)

    def finish(j, row, inv_row, pivot):
        scale = lax.rsqrt(pivot)
        factor_ref[j : j + 1, :] = (jnp.where(row_lane >= j, row, 0.0) * scale)[:, 0:CHAN]
        inverse[j : j + 1, :] = jnp.where(row_lane <= j, inv_row, 0.0) * scale

    def spread_lane(block, j):
        return jnp.broadcast_to(block[:, j : j + 1], (8, 128))

    def spread_row(block, i):
        return jnp.broadcast_to(block[i : i + 1, :], (8, 128))

    for j in range(0, CHAN, 4):
        g, s = j // 8, j % 8
        top = blocks[g]
        cols = [spread_lane(top, j + i) for i in range(4)]
        rows = [spread_row(top, s + i) for i in range(4)]
        d = [[spread_row(cols[min(m, i)], s + max(m, i)) for i in range(4)] for m in range(4)]
        p_inv = 1.0 / (d[0][0] * d[1][1] - d[0][1] * d[0][1])
        adj = [[d[1][1], -d[0][1]], [-d[0][1], d[0][0]]]
        h = [
            [(d[2 + m][0] * adj[0][i] + d[2 + m][1] * adj[1][i]) * p_inv for i in range(2)]
            for m in range(2)
        ]
        t = [
            [d[2 + m][2 + i] - (h[m][0] * d[0][2 + i] + h[m][1] * d[1][2 + i]) for i in range(2)]
            for m in range(2)
        ]
        t01 = t[1][0]
        t_inv = 1.0 / (t[0][0] * t[1][1] - t01 * t01)
        unit = []
        for i in range(4):
            value = rows[i]
            for m in range(4):
                value = jnp.where(lane == j + m, 1.0 if m == i else 0.0, value)
            unit.append(value)
        below = [unit[2 + m] - (h[m][0] * unit[0] + h[m][1] * unit[1]) for m in range(2)]
        up2 = (t[1][1] * below[0] - t01 * below[1]) * t_inv
        up3 = (t[0][0] * below[1] - t01 * below[0]) * t_inv
        inner = [unit[0] * d[1][1] - unit[1] * d[0][1], unit[1] * d[0][0] - unit[0] * d[0][1]]
        up0 = inner[0] * p_inv - (h[0][0] * up2 + h[1][0] * up3)
        up1 = inner[1] * p_inv - (h[0][1] * up2 + h[1][1] * up3)
        ups = (up0, up1, up2, up3)
        ratio0 = d[0][1] / d[0][0]
        ratio1 = t01 / t[0][0]
        mix0 = rows[2] - (h[0][0] * rows[0] + h[0][1] * rows[1])
        mix1 = rows[3] - (h[1][0] * rows[0] + h[1][1] * rows[1])
        solved = [rows[0], rows[1] - ratio0 * rows[0], mix0, mix1 - ratio1 * mix0]
        inv_solved = [unit[0], unit[1] - ratio0 * unit[0], below[0], below[1] - ratio1 * below[0]]
        pivots = [d[0][0], d[1][1] - d[0][1] * ratio0, t[0][0], t[1][1] - t01 * ratio1]
        for i in range(4):
            finish(j + i, solved[i][0:1], inv_solved[i][0:1], pivots[i][0:1])
        if j % ORIENT == ORIENT - 4:
            spread_inverse(j // ORIENT)
        if j >= ORIENT and j % 8 == 4:
            whiten_pair(j // ORIENT - 1, j % ORIENT // 8)
        if j == CHAN - 4:
            break
        inside = (lane >= j) & (lane < j + 4)
        for k in range(g, CHAN // 8):
            if k > g:
                cols = [spread_lane(blocks[k], j + i) for i in range(4)]
            else:
                if s == 4:
                    continue
                cols = [jnp.where(sub > s + 3, col, 0.0) for col in cols]
            change = (cols[0] * ups[0] + cols[1] * ups[1]) + (cols[2] * ups[2] + cols[3] * ups[3])
            blocks[k] = jnp.where(inside, 0.0, blocks[k]) - change

    for pair in range(4):
        whiten_pair(2, pair)
    for level in range(3):
        sent(level).wait()


def local(seismic, trace_live, filter_taps):
    il_len, xl_len, t_len = seismic.shape
    assert (il_len, xl_len, t_len) == (16, 32, 256) and lax.axis_size("depth") == 2
    taps = filter_taps.astype(F32)
    x_index = lax.axis_index("xline")
    d_index = lax.axis_index("depth")
    two_sided = lax.axis_size("xline") > 2
    vmem = pl.BlockSpec(memory_space=pltpu.VMEM)
    smem = pl.BlockSpec(memory_space=pltpu.SMEM)

    live, near, far = pl.pallas_call(
        live_kernel,
        out_shape=(
            jax.ShapeDtypeStruct((il_len * xl_len, t_len), BF16),
            jax.ShapeDtypeStruct((SENT * xl_len, t_len), BF16),
            jax.ShapeDtypeStruct((SENT * xl_len, t_len), BF16),
        ),
        in_specs=[vmem] * 2,
        out_specs=(vmem,) * 3,
        compiler_params=pltpu.CompilerParams(vmem_limit_bytes=LIVE_VMEM),
        name="live",
    )(trace_live.astype(F32), seismic)
    il_size = lax.axis_size("inline")
    near_pairs = [(i, i ^ 1) for i in range(il_size) if i ^ 1 < il_size]
    far_pairs = [(i, i - 1 if i % 2 == 0 else i + 1) for i in range(1, il_size)]
    far_pairs = [(i, j) for i, j in far_pairs if j < il_size]
    near = lax.ppermute(near, "inline", near_pairs)
    far = lax.ppermute(far, "inline", far_pairs)
    parts = [v.reshape(-1, xl_len, t_len) for v in (live, near, far)]
    stored = 48 if two_sided else 40
    bands, w2, w3, pick, turn, own_phases = pl.pallas_call(
        prepare_kernel,
        out_shape=(
            jax.ShapeDtypeStruct((3 * 256, 128), BF16),
            jax.ShapeDtypeStruct((TAPS, CHAN, 128), F32),
            jax.ShapeDtypeStruct((TAPS, CHAN, 128), F32),
            jax.ShapeDtypeStruct((256, 256), BF16),
            jax.ShapeDtypeStruct((512, 512), BF16),
            jax.ShapeDtypeStruct((512, 256), BF16),
        ),
        in_specs=[vmem] * 2,
        out_specs=(vmem,) * 6,
        compiler_params=pltpu.CompilerParams(vmem_limit_bytes=PREPARE_VMEM),
        cost_estimate=pl.CostEstimate(flops=10**9, bytes_accessed=4 * 10**6, transcendentals=0),
        name="prepare",
    )(taps, live)

    def stack(js):
        return jnp.concatenate([v[:, js] for v in parts], axis=0)

    low, high = slice(0, REACH), slice(xl_len - REACH, xl_len)
    if two_sided:
        xh = [shifted(stack(high), "xline", 1), shifted(stack(low), "xline", -1)]
    else:
        xh = [flipped(jnp.where(x_index == 0, stack(high), stack(low)), [("xline", 1)])]
    first0, first12, edge, turn_x, moves1, moves2, select, gather = pl.pallas_call(
        functools.partial(inline_kernel, stored),
        out_shape=(
            jax.ShapeDtypeStruct((xl_len, 256, 256), F32),
            jax.ShapeDtypeStruct((xl_len // 2, 512, 128), F32),
            jax.ShapeDtypeStruct((ROWS * xl_len, 128), BF16),
            jax.ShapeDtypeStruct((512, 512), BF16),
            jax.ShapeDtypeStruct((256, 512), BF16),
            jax.ShapeDtypeStruct((256, 512), BF16),
            jax.ShapeDtypeStruct((3, 256, TAPS * 128), BF16),
            jax.ShapeDtypeStruct((32, 32 * stored), BF16),
        ),
        in_specs=[vmem] * 7,
        out_specs=(vmem,) * 8,
        scratch_shapes=[pltpu.VMEM((32, 32, 256), BF16)],
        compiler_params=pltpu.CompilerParams(vmem_limit_bytes=INLINE_VMEM),
        cost_estimate=pl.CostEstimate(flops=4 * 10**9, bytes_accessed=16 * 10**6, transcendentals=0),
        name="inline",
    )(bands, pick, turn, live, own_phases, near, far)

    def side(x):
        return jnp.where(d_index == 0, x[:, :, t_len - 128 :], x[:, :, :128])

    dh = jnp.concatenate([edge.reshape(ROWS, xl_len, 128)] + [side(x) for x in xh], axis=1)
    dh = flipped(dh, [("depth", 1)])
    xrows = jnp.concatenate([x.reshape(REACH * ROWS, t_len) for x in xh], axis=0)
    edge0, second12 = pl.pallas_call(
        functools.partial(crossline_kernel, two_sided),
        out_shape=(
            jax.ShapeDtypeStruct((3, 256, 256), F32),
            jax.ShapeDtypeStruct((16, 512, 128), BF16),
        ),
        in_specs=[vmem] * 6,
        out_specs=(vmem,) * 2,
        scratch_shapes=[
            pltpu.VMEM((16, 32, 256), BF16),
            pltpu.VMEM((8, 512, 128), F32),
        ],
        compiler_params=pltpu.CompilerParams(vmem_limit_bytes=CROSS_VMEM),
        cost_estimate=pl.CostEstimate(flops=3 * 10**9, bytes_accessed=9 * 10**6, transcendentals=0),
        name="crossline",
    )(bands, w2, pick, turn_x, first12, xrows)
    attr, gram = pl.pallas_call(
        functools.partial(attributes_kernel, two_sided),
        out_shape=(
            jax.ShapeDtypeStruct((16, 3, 8, ORIENT, 128), BF16),
            jax.ShapeDtypeStruct((CHAN, 128), F32),
        ),
        in_specs=[smem] + [vmem] * 12,
        out_specs=(vmem, vmem),
        scratch_shapes=[pltpu.VMEM((3, 256, 128), F32)],
        compiler_params=pltpu.CompilerParams(vmem_limit_bytes=ATTR_VMEM),
        name="attributes",
    )(
        trace_live, trace_live, bands, w2, w3, moves1, moves2, select, gather, first0, edge0,
        second12, dh,
    )

    mine, other = summed(gram)
    out, factor = pl.pallas_call(
        whiten_kernel,
        out_shape=(
            jax.ShapeDtypeStruct((CHAN, 8, 16, 128), BF16),
            jax.ShapeDtypeStruct((CHAN, CHAN), F32),
        ),
        in_specs=[vmem] * 3,
        out_specs=(pl.BlockSpec(memory_space=pl.ANY), vmem),
        scratch_shapes=[
            pltpu.VMEM((CHAN, 128), F32),
            pltpu.VMEM((3, 256, 768), BF16),
            pltpu.VMEM((CHAN, 8, 16, 128), BF16),
            pltpu.SemaphoreType.DMA((3,)),
        ],
        compiler_params=pltpu.CompilerParams(vmem_limit_bytes=WHITEN_VMEM),
        name="whiten",
    )(mine, other, attr)
    return out, factor


def solution(mesh):
    placed = (P(("survey", "inline"), "xline", "depth"), P(("survey", "inline"), "xline"), P())
    return jax.shard_map(
        local,
        mesh=mesh,
        in_specs=placed,
        out_specs=(P(None, ("survey", "inline"), "xline", "depth"), P("survey", None)),
        check_vma=False,
    )
```

```python
import functools
import math

import jax
import jax.numpy as jnp
from jax import lax
from jax.experimental import pallas as pl
from jax.experimental.pallas import tpu as pltpu
from jax.sharding import PartitionSpec as P

ORIENT = 32
TAPS = 5
CHAN = 96
REACH = 8
LAST_ROWS = (8, 10, 12, 14, 15)
FIRST_ROWS = (0, 2, 4, 6, 7)
SENT = 5
ROWS = 16 + 2 * SENT
KEPT = 5
F32 = jnp.float32
BF16 = jnp.bfloat16
LIVE_VMEM = 4 * 1024 * 1024
PREPARE_VMEM = 8 * 1024 * 1024
INLINE_VMEM = 22 * 1024 * 1024
CROSS_VMEM = 16 * 1024 * 1024
ATTR_VMEM = 22 * 1024 * 1024
WHITEN_VMEM = 14 * 1024 * 1024


def iota(shape, dim):
    return lax.broadcasted_iota(jnp.int32, shape, dim)


def rounded(value):
    return value.astype(BF16).astype(F32)


def ones_where(mask):
    return jnp.where(mask, 1.0, 0.0).astype(BF16)


def dot(a, b):
    return jnp.dot(a, b, preferred_element_type=F32)


def shifted(value, axis, step):
    size = lax.axis_size(axis)
    return lax.ppermute(value, axis, [(i, i + step) for i in range(size) if 0 <= i + step < size])


def flipped(value, flips):
    axes = tuple(axis for axis, _ in flips)
    sizes = [lax.axis_size(axis) for axis in axes]
    pairs = []
    for source in range(math.prod(sizes)):
        target, rest, stride = 0, source, 1
        for size, (_, bit) in reversed(list(zip(sizes, flips))):
            target += ((rest % size) ^ bit) * stride
            rest, stride = rest // size, stride * size
        pairs.append((source, target))
    return lax.ppermute(value, axes, pairs)


def bits_of(axis):
    size = lax.axis_size(axis)
    assert size & (size - 1) == 0
    return [(axis, 2 ** i) for i in range(size.bit_length() - 1)]


def summed(value):
    x_bits, il_bits = bits_of("xline"), bits_of("inline")
    for bit in bits_of("depth") + x_bits[1:] + il_bits[2:]:
        value = value + flipped(value, [bit])
    one, two = il_bits[0], x_bits[0]
    a, b, c = flipped(value, [one]), flipped(value, [two]), flipped(value, [one, two])
    value = (value + a) + (b + c)
    return value, flipped(value, [il_bits[1]])


def halo_select(level, stored, x_left, depth_first):
    dilation = 2 ** level
    rows, cols = 256, TAPS * 128
    lane = iota((1, cols), 1)
    k = lane // 128
    within = lane % 128
    place = (within + 4) % 8 - 4
    q = ((within + 4) // 8) % 16
    j = 2 * q + dilation * (k - 2)
    slot = jnp.where(j < 0, 40 + j, j)
    if stored == 48:
        slot = jnp.where(j >= 32, j + 8, slot)
    else:
        slot = jnp.where((j < 0) & (x_left == 0), -999999, slot)
        slot = jnp.where((j >= 32) & (x_left == 1), -999999, slot)
    kept = jnp.where(place >= 0, place, place + 4)
    if level == 0:
        kept = jnp.where(place == -2, 4, kept)
    source = kept * stored + slot
    source = jnp.where((place >= 0) & (depth_first == 0), -1, source)
    source = jnp.where((place < 0) & (depth_first == 1), -1, source)
    return ones_where(iota((rows, cols), 0) == source)


def shift_matrix(shifts):
    lane = iota((1, 128 * len(shifts)), 1)
    source = lane % 128
    for i, shift in enumerate(shifts):
        source = jnp.where(lane // 128 == i, source + shift, source)
    past = (source + 128) % 128 + 128
    source = jnp.where(source < 0, past, jnp.where(source >= 128, past, source))
    return ones_where(iota((256, 128 * len(shifts)), 0) == source)


def side_flags():
    x_left = jnp.where(lax.axis_index("xline") == 1, 1, 0)
    depth_first = jnp.where(lax.axis_index("depth") == 0, 1, 0)
    return x_left, depth_first, lax.axis_index("inline") % 2


def live_kernel(trace_ref, seismic_ref, live_ref, near_ref, far_ref):
    n_il, n_xl, _ = seismic_ref.shape
    eye = iota((n_xl, n_xl), 0) == iota((n_xl, n_xl), 1)
    for p in range(n_il):
        row = jnp.broadcast_to(trace_ref[p : p + 1, :], (n_xl, n_xl))
        kept = dot(jnp.where(eye, row, 0.0).astype(BF16), seismic_ref[p])
        live_ref[p * n_xl : (p + 1) * n_xl, :] = kept.astype(BF16)
    odd = side_flags()[2]

    def put(ref, rows):
        for i, p in enumerate(rows):
            ref[i * n_xl : (i + 1) * n_xl] = live_ref[p * n_xl : (p + 1) * n_xl]

    @pl.when(odd == 1)
    def _():
        put(near_ref, FIRST_ROWS)
        put(far_ref, LAST_ROWS)

    @pl.when(odd == 0)
    def _():
        put(near_ref, LAST_ROWS)
        put(far_ref, FIRST_ROWS)


def banded(level, taps_ref, bands, il_odd):
    lane = iota((ORIENT, 128), 1)
    cs = slice(level * ORIENT, (level + 1) * ORIENT)
    cols = [jnp.broadcast_to(taps_ref[0, cs, k : k + 1], (ORIENT, 128)) for k in range(TAPS)]
    for o in range(8):
        total = jnp.zeros((ORIENT, 128), F32)
        for k in range(TAPS):
            p = 2 * o + 2 ** level * (k - 2)
            if p < 0:
                place = 16 + SENT + LAST_ROWS.index(p + 16) - SENT * il_odd
            elif p >= 16:
                place = 16 + FIRST_ROWS.index(p - 16) + SENT * il_odd
            else:
                place = p
            total = jnp.where(lane == place, cols[k], total)
        bands[pl.ds(level * 256 + o * ORIENT, ORIENT), :] = total.astype(BF16)


def phase_pick():
    n = iota((256, 256), 1)
    return ones_where(iota((256, 256), 0) == jnp.where(n < 128, 2 * n, 2 * n - 255))


def prepare_kernel(
    taps_ref, own_ref, bands, w2, w3, pick, turn, own_out
):
    il_odd = side_flags()[2]
    for k in range(TAPS):
        w2[k] = jnp.broadcast_to(taps_ref[1, :, k : k + 1], (CHAN, 128))
        w3[k] = jnp.broadcast_to(taps_ref[2, :, k : k + 1], (CHAN, 128))
    for level in range(3):
        banded(level, taps_ref, bands, il_odd)
    pick[...] = phase_pick()
    own_out[...] = dot(own_ref[...], pick[...]).astype(BF16)
    r = iota((512, 512), 0)
    c = iota((512, 512), 1)
    turn[...] = ones_where(c == r % 32 * 16 + r // 32)


def inline_kernel(
    stored, bands, pick, turn, own_ref, own_phases, near_ref, far_ref, first0, first12, edge_ref,
    turn_x, moves1, moves2, select, gather, planes,
):
    x_left, depth_first, _ = side_flags()
    r = iota((512, 512), 0)
    c = iota((512, 512), 1)
    source = r // 256 * (8 * ROWS) + r % 32 * 8 + r // 32 % 8
    turn_x[...] = ones_where(jnp.where(r % 32 < ROWS, source, -1) == c)
    moves1[...] = shift_matrix((-2, -1, 1, 2))
    moves2[...] = shift_matrix((-4, -2, 2, 4))
    rows = 32 * stored
    gather[...] = ones_where(iota((32, rows), 1) // stored == iota((32, rows), 0))
    for level in range(3):
        select[level] = halo_select(level, stored, x_left, depth_first)

    def put_edge(ts):
        for at, ref in ((0, own_ref), (512, near_ref), (512 + near_ref.shape[0], far_ref)):
            edge_ref[at : at + ref.shape[0], :] = ref[:, ts]

    pl.when(depth_first == 1)(lambda: put_edge(slice(128, 256)))
    pl.when(depth_first == 0)(lambda: put_edge(slice(0, 128)))

    own = own_phases[...].reshape(16, 32, 256)
    near = dot(near_ref[...], pick[...]).astype(BF16).reshape(SENT, 32, 256)
    far = dot(far_ref[...], pick[...]).astype(BF16).reshape(SENT, 32, 256)
    none = jnp.zeros((32 - ROWS, 16, 256), BF16)
    for half in range(2):
        js = slice(half * 16, half * 16 + 16)
        block = jnp.concatenate([own[:, js], near[:, js], far[:, js], none], axis=0).reshape(512, 256)
        planes[half * 16 : half * 16 + 16] = dot(turn[...], block).astype(BF16).reshape(16, 32, 256)

    a0 = bands[0:256, 0:32]
    a12 = bands[256:768, 0:32]
    def level0_first(j, _):
        first0[j] = rounded(dot(a0, planes[j]))
        return 0

    lax.fori_loop(0, 32, level0_first, 0, unroll=16)

    def even_first(pair, _):
        both = jnp.concatenate([planes[4 * pair, :, 0:128], planes[4 * pair + 2, :, 0:128]], axis=1)
        out = rounded(dot(a12, both))
        first12[2 * pair] = out[:, 0:128]
        first12[2 * pair + 1] = out[:, 128:256]
        return 0

    lax.fori_loop(0, 8, even_first, 0, unroll=8)


def tall(ref, level, k):
    return jnp.concatenate([ref[k, level * ORIENT : (level + 1) * ORIENT]] * 8, axis=0)


def crossline_kernel(
    two_sided, bands, w2, pick, turn_x, first12, xh_ref, edge0, second12, edges, edge12
):
    x_left = side_flags()[0]

    got = dot(xh_ref[...], pick[...])
    if not two_sided:
        left = jnp.where(x_left == 1, 1.0, 0.0)
        got = jnp.concatenate([got * left, got * (1.0 - left)], axis=0)
    got = jnp.concatenate([got.astype(BF16), jnp.zeros((512 - 16 * ROWS, 256), BF16)], axis=0)
    edges[...] = dot(turn_x[...], got).astype(BF16).reshape(16, 32, 256)
    a0 = bands[0:256, 0:32]
    a12 = bands[256:768, 0:32]
    for i, slot in enumerate((6, 7, 8)):
        edge0[i] = rounded(dot(a0, edges[slot]))
    for i in range(4):
        both = jnp.concatenate([edges[4 * i, :, 0:128], edges[4 * i + 2, :, 0:128]], axis=1)
        out = rounded(dot(a12, both))
        edge12[2 * i], edge12[2 * i + 1] = out[:, 0:128], out[:, 128:256]

    def filtered(level, q, plane):
        for c16 in range(2):
            start = level * ORIENT + c16 * 16
            s2 = [w2[k, start : start + 16] for k in range(TAPS)]
            for o in range(8):
                row = (level - 1) * 256 + o * ORIENT + c16 * 16
                here = slice(row, row + 16)
                total = sum(s2[k] * plane(q + level * (k - 2), here) for k in range(TAPS))
                second12[q, here, :] = total.astype(BF16)

    def own_plane(e, here):
        return first12[e, here, :]

    def any_plane(e, here):
        if 0 <= e < 16:
            return first12[e, here, :]
        return edge12[e + 4 if e < 0 else e - 12, here, :]

    for level in (1, 2):
        reach = 2 * level

        def inner(q, _, level=level):
            filtered(level, q, own_plane)
            return 0

        lax.fori_loop(reach, 16 - reach, inner, 0, unroll=4)
        for i in range(reach):
            filtered(level, i, any_plane)
            filtered(level, 15 - i, any_plane)


def attributes_kernel(
    two_sided, live_smem, live_ref, bands, w2, w3, moves1, moves2, select, gather, first0, edge0,
    second12, dh_ref, attr_ref, gram_ref, halo2,
):
    depth_first = side_flags()[1]
    stored = 48 if two_sided else 40

    n = iota((1, 256), 1)
    kept = n // stored
    sample = 2 * kept - jnp.where(kept == 4, 1, 0) + jnp.where(depth_first == 1, 0, 120)
    sample = jnp.where(kept < KEPT, sample, -1)
    spread = ones_where(iota((128, 256), 0) == sample)
    rows = 32 * stored
    got = dh_ref[...].reshape(ROWS * stored, 128)
    got = jnp.concatenate([got, jnp.zeros((rows - ROWS * stored, 128), BF16)], axis=0)
    wide = dot(got, spread)
    wide = jnp.where(iota((rows, 256), 0) % stored == n % stored, wide, 0.0).astype(BF16)
    lanes = dot(gather[...], wide).astype(BF16)
    for level in range(3):
        cols = dot(lanes, select[level]).astype(BF16)
        part = rounded(dot(bands[level * 256 : level * 256 + 256, 0:32], cols))
        total = jnp.zeros((256, 128), F32)
        for k in range(TAPS):
            total = total + part[:, k * 128 : k * 128 + 128] * tall(w2, level, k)
        total = rounded(total)
        if level == 0:
            w3_0, w3_1, w3_4 = [tall(w3, 0, k) for k in (0, 1, 4)]
            before_first = total * w3_0 + pltpu.roll(total, 1, 1) * w3_1
            total = jnp.where(iota((256, 128), 1) % 8 == 7, before_first, total * w3_4)
        halo2[level] = total


    def one_q(q, plane):
        align = (128 - 8 * q) % 128
        live_q = [live_smem[2 * o, 2 * q].astype(F32) for o in range(8)]
        lane = iota((16, 128), 1)

        def put(o, start, total):
            at = start % ORIENT
            attr_ref[2 * o + q // 8, start // ORIENT, q % 8, at : at + 16, :] = (total * live_q[o]).astype(BF16)

        for level in (1, 2):
            halo = pltpu.roll(halo2[level], align, 1).astype(BF16)
            value = second12[q, (level - 1) * 256 : level * 256, :]
            moved = dot(jnp.concatenate([value, halo], axis=1), (moves1 if level == 1 else moves2)[...])
            for c16 in range(2):
                start = level * ORIENT + c16 * 16
                s3 = [w3[k, start : start + 16] for k in range(TAPS)]
                for o in range(8):
                    rows = slice(o * ORIENT + c16 * 16, o * ORIENT + c16 * 16 + 16)
                    total = s3[2] * value[rows].astype(F32)
                    for i, k in enumerate((0, 1, 3, 4)):
                        total = total + s3[k] * moved[rows, i * 128 : i * 128 + 128]
                    put(o, start, total)
        for c16 in range(2):
            s2 = [w2[k, c16 * 16 : c16 * 16 + 16] for k in range(TAPS)]
            s3 = [w3[k, c16 * 16 : c16 * 16 + 16] for k in range(TAPS)]
            for o in range(8):
                rows = slice(o * ORIENT + c16 * 16, o * ORIENT + c16 * 16 + 16)
                both = []
                for ts in (slice(0, 128), slice(128, 256)):
                    total = sum(s2[k] * plane(2 * q + k - 2, rows, ts) for k in range(TAPS))
                    both.append(rounded(total))
                even, odd = both
                halo = pltpu.roll(halo2[0, rows], align, 1)
                back = jnp.where(lane == 127, halo, s3[0] * even + s3[1] * odd)
                ahead = jnp.where(lane == 0, halo, s3[4] * even)
                moved = pltpu.roll(back, 1, 1) + pltpu.roll(ahead, 127, 1)
                put(o, c16 * 16, s3[2] * even + s3[3] * odd + moved)

    def add_gram(q, total):
        for o in range(0, 8, 2):
            both = jnp.concatenate(
                [
                    jnp.concatenate([attr_ref[2 * i + q // 8, level, q % 8] for level in range(3)], axis=0)
                    for i in (o, o + 1)
                ],
                axis=1,
            )
            total = total + lax.dot_general(
                both, both, (((1,), (1,)), ((), ())), preferred_element_type=F32
            )
        return total

    def own_plane(j, rows, ts):
        return first0[j, rows, ts]

    def any_plane(j, rows, ts):
        if 0 <= j < 32:
            return first0[j, rows, ts]
        return edge0[j + 2 if j < 0 else 2, rows, ts]

    def next_q(q, total):
        total = add_gram(q - 1, total)
        one_q(q, own_plane)
        return total

    one_q(0, any_plane)
    gram = lax.fori_loop(1, 15, next_q, jnp.zeros((CHAN, CHAN), F32))
    gram = add_gram(14, gram)
    one_q(15, any_plane)
    gram = add_gram(15, gram)
    alive = live_ref[...]
    chosen = (iota(alive.shape, 0) % 2 == 0) & (iota(alive.shape, 1) % 2 == 0)
    count = jnp.sum(jnp.where(chosen, alive.astype(F32), 0.0)) * 128.0
    gram_ref[...] = jnp.full((CHAN, 128), count, F32)
    gram_ref[:, 0:CHAN] = gram


def whiten_kernel(mine_ref, other_ref, attr_ref, out_hbm, factor_ref, inverse, kron, out_ref, sems):
    total = mine_ref[...] + other_ref[...]
    lane = iota((8, 128), 1)
    sub = iota((8, 128), 0)
    count = jnp.broadcast_to(total[0:1, CHAN : CHAN + 1], (8, 128))
    blocks = []
    for g in range(CHAN // 8):
        blocks.append(jnp.where(lane < CHAN, total[8 * g : 8 * g + 8] / count, 0.0))

    n = iota((CHAN, 768), 1)
    spread = ones_where(iota((CHAN, 768), 0) == n // 256 * ORIENT + n % ORIENT)
    tall = ones_where(iota((256, ORIENT), 0) // 8 == iota((256, ORIENT), 1))

    def spread_inverse(level):
        depth = 256 * (level + 1)
        low = inverse[level * ORIENT : (level + 1) * ORIENT, 0:CHAN].astype(BF16)
        full = dot(tall, dot(low, spread[:, 0:depth]).astype(BF16))
        keep = iota((256, depth), 0) % 8 == iota((256, depth), 1) // ORIENT % 8
        kron[level, :, 0:depth] = jnp.where(keep, full, 0.0).astype(BF16)

    def sent(level):
        cs = slice(level * ORIENT, (level + 1) * ORIENT)
        return pltpu.make_async_copy(out_ref.at[cs], out_hbm.at[cs], sems.at[level])

    def whiten_pair(level, pair):
        depth = 256 * (level + 1)
        halves = []
        for half in range(2):
            rows = [
                attr_ref[2 * (2 * pair + i) + half, 0 : level + 1].reshape(depth, 128) for i in range(2)
            ]
            halves.append(dot(kron[level, :, 0:depth], jnp.concatenate(rows, axis=1)))
        for i in range(2):
            both = [half[:, i * 128 : i * 128 + 128].reshape(ORIENT, 8, 128) for half in halves]
            out_ref[level * ORIENT : (level + 1) * ORIENT, 2 * pair + i] = jnp.concatenate(
                both, axis=1
            ).astype(BF16)
        if pair == 3:
            sent(level).start()

    row_lane = iota((1, 128), 1)

    def finish(j, row, inv_row, pivot):
        scale = lax.rsqrt(pivot)
        factor_ref[j : j + 1, :] = (jnp.where(row_lane >= j, row, 0.0) * scale)[:, 0:CHAN]
        inverse[j : j + 1, :] = jnp.where(row_lane <= j, inv_row, 0.0) * scale

    def spread_lane(block, j):
        return jnp.broadcast_to(block[:, j : j + 1], (8, 128))

    def spread_row(block, i):
        return jnp.broadcast_to(block[i : i + 1, :], (8, 128))

    for j in range(0, CHAN, 4):
        g, s = j // 8, j % 8
        top = blocks[g]
        cols = [spread_lane(top, j + i) for i in range(4)]
        rows = [spread_row(top, s + i) for i in range(4)]
        d = [[spread_row(cols[min(m, i)], s + max(m, i)) for i in range(4)] for m in range(4)]
        p_inv = 1.0 / (d[0][0] * d[1][1] - d[0][1] * d[0][1])
        adj = [[d[1][1], -d[0][1]], [-d[0][1], d[0][0]]]
        h = [
            [(d[2 + m][0] * adj[0][i] + d[2 + m][1] * adj[1][i]) * p_inv for i in range(2)]
            for m in range(2)
        ]
        t = [
            [d[2 + m][2 + i] - (h[m][0] * d[0][2 + i] + h[m][1] * d[1][2 + i]) for i in range(2)]
            for m in range(2)
        ]
        t01 = t[1][0]
        t_inv = 1.0 / (t[0][0] * t[1][1] - t01 * t01)
        unit = []
        for i in range(4):
            value = rows[i]
            for m in range(4):
                value = jnp.where(lane == j + m, 1.0 if m == i else 0.0, value)
            unit.append(value)
        below = [unit[2 + m] - (h[m][0] * unit[0] + h[m][1] * unit[1]) for m in range(2)]
        up2 = (t[1][1] * below[0] - t01 * below[1]) * t_inv
        up3 = (t[0][0] * below[1] - t01 * below[0]) * t_inv
        inner = [unit[0] * d[1][1] - unit[1] * d[0][1], unit[1] * d[0][0] - unit[0] * d[0][1]]
        up0 = inner[0] * p_inv - (h[0][0] * up2 + h[1][0] * up3)
        up1 = inner[1] * p_inv - (h[0][1] * up2 + h[1][1] * up3)
        ups = (up0, up1, up2, up3)
        ratio0 = d[0][1] / d[0][0]
        ratio1 = t01 / t[0][0]
        mix0 = rows[2] - (h[0][0] * rows[0] + h[0][1] * rows[1])
        mix1 = rows[3] - (h[1][0] * rows[0] + h[1][1] * rows[1])
        solved = [rows[0], rows[1] - ratio0 * rows[0], mix0, mix1 - ratio1 * mix0]
        inv_solved = [unit[0], unit[1] - ratio0 * unit[0], below[0], below[1] - ratio1 * below[0]]
        pivots = [d[0][0], d[1][1] - d[0][1] * ratio0, t[0][0], t[1][1] - t01 * ratio1]
        for i in range(4):
            finish(j + i, solved[i][0:1], inv_solved[i][0:1], pivots[i][0:1])
        if j % ORIENT == ORIENT - 4:
            spread_inverse(j // ORIENT)
        if j >= ORIENT and j % 8 == 4:
            whiten_pair(j // ORIENT - 1, j % ORIENT // 8)
        if j == CHAN - 4:
            break
        inside = (lane >= j) & (lane < j + 4)
        for k in range(g, CHAN // 8):
            if k > g:
                cols = [spread_lane(blocks[k], j + i) for i in range(4)]
            else:
                if s == 4:
                    continue
                cols = [jnp.where(sub > s + 3, col, 0.0) for col in cols]
            change = (cols[0] * ups[0] + cols[1] * ups[1]) + (cols[2] * ups[2] + cols[3] * ups[3])
            blocks[k] = jnp.where(inside, 0.0, blocks[k]) - change

    for pair in range(4):
        whiten_pair(2, pair)
    for level in range(3):
        sent(level).wait()


def local(seismic, trace_live, filter_taps):
    il_len, xl_len, t_len = seismic.shape
    assert (il_len, xl_len, t_len) == (16, 32, 256) and lax.axis_size("depth") == 2
    taps = filter_taps.astype(F32)
    x_index = lax.axis_index("xline")
    d_index = lax.axis_index("depth")
    two_sided = lax.axis_size("xline") > 2
    vmem = pl.BlockSpec(memory_space=pltpu.VMEM)
    smem = pl.BlockSpec(memory_space=pltpu.SMEM)

    live, near, far = pl.pallas_call(
        live_kernel,
        out_shape=(
            jax.ShapeDtypeStruct((il_len * xl_len, t_len), BF16),
            jax.ShapeDtypeStruct((SENT * xl_len, t_len), BF16),
            jax.ShapeDtypeStruct((SENT * xl_len, t_len), BF16),
        ),
        in_specs=[vmem] * 2,
        out_specs=(vmem,) * 3,
        compiler_params=pltpu.CompilerParams(vmem_limit_bytes=LIVE_VMEM),
        name="live",
    )(trace_live.astype(F32), seismic)
    il_size = lax.axis_size("inline")
    near_pairs = [(i, i ^ 1) for i in range(il_size) if i ^ 1 < il_size]
    far_pairs = [(i, i - 1 if i % 2 == 0 else i + 1) for i in range(1, il_size)]
    far_pairs = [(i, j) for i, j in far_pairs if j < il_size]
    near = lax.ppermute(near, "inline", near_pairs)
    far = lax.ppermute(far, "inline", far_pairs)
    parts = [v.reshape(-1, xl_len, t_len) for v in (live, near, far)]
    stored = 48 if two_sided else 40
    bands, w2, w3, pick, turn, own_phases = pl.pallas_call(
        prepare_kernel,
        out_shape=(
            jax.ShapeDtypeStruct((3 * 256, 128), BF16),
            jax.ShapeDtypeStruct((TAPS, CHAN, 128), F32),
            jax.ShapeDtypeStruct((TAPS, CHAN, 128), F32),
            jax.ShapeDtypeStruct((256, 256), BF16),
            jax.ShapeDtypeStruct((512, 512), BF16),
            jax.ShapeDtypeStruct((512, 256), BF16),
        ),
        in_specs=[vmem] * 2,
        out_specs=(vmem,) * 6,
        compiler_params=pltpu.CompilerParams(vmem_limit_bytes=PREPARE_VMEM),
        cost_estimate=pl.CostEstimate(flops=10**9, bytes_accessed=4 * 10**6, transcendentals=0),
        name="prepare",
    )(taps, live)

    def stack(js):
        return jnp.concatenate([v[:, js] for v in parts], axis=0)

    low, high = slice(0, REACH), slice(xl_len - REACH, xl_len)
    if two_sided:
        xh = [shifted(stack(high), "xline", 1), shifted(stack(low), "xline", -1)]
    else:
        xh = [flipped(jnp.where(x_index == 0, stack(high), stack(low)), [("xline", 1)])]
    first0, first12, edge, turn_x, moves1, moves2, select, gather = pl.pallas_call(
        functools.partial(inline_kernel, stored),
        out_shape=(
            jax.ShapeDtypeStruct((xl_len, 256, 256), F32),
            jax.ShapeDtypeStruct((xl_len // 2, 512, 128), F32),
            jax.ShapeDtypeStruct((ROWS * xl_len, 128), BF16),
            jax.ShapeDtypeStruct((512, 512), BF16),
            jax.ShapeDtypeStruct((256, 512), BF16),
            jax.ShapeDtypeStruct((256, 512), BF16),
            jax.ShapeDtypeStruct((3, 256, TAPS * 128), BF16),
            jax.ShapeDtypeStruct((32, 32 * stored), BF16),
        ),
        in_specs=[vmem] * 7,
        out_specs=(vmem,) * 8,
        scratch_shapes=[pltpu.VMEM((32, 32, 256), BF16)],
        compiler_params=pltpu.CompilerParams(vmem_limit_bytes=INLINE_VMEM),
        cost_estimate=pl.CostEstimate(flops=4 * 10**9, bytes_accessed=16 * 10**6, transcendentals=0),
        name="inline",
    )(bands, pick, turn, live, own_phases, near, far)

    def side(x):
        return jnp.where(d_index == 0, x[:, :, t_len - 128 :], x[:, :, :128])

    dh = jnp.concatenate([edge.reshape(ROWS, xl_len, 128)] + [side(x) for x in xh], axis=1)
    dh = flipped(dh, [("depth", 1)])
    xrows = jnp.concatenate([x.reshape(REACH * ROWS, t_len) for x in xh], axis=0)
    edge0, second12 = pl.pallas_call(
        functools.partial(crossline_kernel, two_sided),
        out_shape=(
            jax.ShapeDtypeStruct((3, 256, 256), F32),
            jax.ShapeDtypeStruct((16, 512, 128), BF16),
        ),
        in_specs=[vmem] * 6,
        out_specs=(vmem,) * 2,
        scratch_shapes=[
            pltpu.VMEM((16, 32, 256), BF16),
            pltpu.VMEM((8, 512, 128), F32),
        ],
        compiler_params=pltpu.CompilerParams(vmem_limit_bytes=CROSS_VMEM),
        cost_estimate=pl.CostEstimate(flops=3 * 10**9, bytes_accessed=9 * 10**6, transcendentals=0),
        name="crossline",
    )(bands, w2, pick, turn_x, first12, xrows)
    attr, gram = pl.pallas_call(
        functools.partial(attributes_kernel, two_sided),
        out_shape=(
            jax.ShapeDtypeStruct((16, 3, 8, ORIENT, 128), BF16),
            jax.ShapeDtypeStruct((CHAN, 128), F32),
        ),
        in_specs=[smem] + [vmem] * 12,
        out_specs=(vmem, vmem),
        scratch_shapes=[pltpu.VMEM((3, 256, 128), F32)],
        compiler_params=pltpu.CompilerParams(vmem_limit_bytes=ATTR_VMEM),
        name="attributes",
    )(
        trace_live, trace_live, bands, w2, w3, moves1, moves2, select, gather, first0, edge0,
        second12, dh,
    )

    mine, other = summed(gram)
    out, factor = pl.pallas_call(
        whiten_kernel,
        out_shape=(
            jax.ShapeDtypeStruct((CHAN, 8, 16, 128), BF16),
            jax.ShapeDtypeStruct((CHAN, CHAN), F32),
        ),
        in_specs=[vmem] * 3,
        out_specs=(pl.BlockSpec(memory_space=pl.ANY), vmem),
        scratch_shapes=[
            pltpu.VMEM((CHAN, 128), F32),
            pltpu.VMEM((3, 256, 768), BF16),
            pltpu.VMEM((CHAN, 8, 16, 128), BF16),
            pltpu.SemaphoreType.DMA((3,)),
        ],
        compiler_params=pltpu.CompilerParams(vmem_limit_bytes=WHITEN_VMEM),
        name="whiten",
    )(mine, other, attr)
    return out, factor


def solution(mesh):
    placed = (P(("survey", "inline"), "xline", "depth"), P(("survey", "inline"), "xline"), P())
    return jax.shard_map(
        local,
        mesh=mesh,
        in_specs=placed,
        out_specs=(P(None, ("survey", "inline"), "xline", "depth"), P("survey", None)),
        check_vma=False,
    )
```
